256 devices in a mesh: ctx: 64 (over x, z, core), head: 4 (over y).
Axes of the slice: x: 4, y: 4, z: 8, core: 2. Of those that a mesh axis runs over, the one named last changes fastest.
Arguments:
- queries: bfloat16 [12288, 1024], P(('ctx', 'head')), may hold values from -1.5 to 1.5, as said below
- key_inputs: bfloat16 [12288, 1024], P(('ctx', 'head')), may hold values from -1.5 to 1.5, as said below
- value_inputs: bfloat16 [12288, 1024], P(('ctx', 'head')), may hold values from -6 to 6
- out_grad: bfloat16 [12288, 1024], P(('ctx', 'head')), may hold values from -6 to 6
- attn_output: bfloat16 [12288, 1024], P(('ctx', 'head')), may hold values from -6 to 6
- gate_logits: bfloat16 [12288, 8], P(('ctx', 'head')), may hold values from 0 to 16
- lse: float32 [12288, 8], P(('ctx', 'head')), as said below
Outputs:
- query_grad: bfloat16 [12288, 1024], P(('ctx', 'head'))
- key_grad: bfloat16 [12288, 1024], P(('ctx', 'head'))
- value_grad: bfloat16 [12288, 1024], P(('ctx', 'head'))
- gate_grad: bfloat16 [12288, 8], P(('ctx', 'head'))
The draws below stay inside these ranges and needn't reach their ends.
Inputs may be any that keep to these rules, and one draw needn't show every extreme that they name: `queries`: queries of every token. `key_inputs`: keys of every token. `lse`: the forward pass's log-sum-exp of each query's scores.
All inputs are finite; a program needn't handle non-finite values.
Results may differ from the reference program's by a relative error of at most 0.0052.
Values may be sent and summed in bfloat16 or wider, within the bound.
A program may use at most 128 MiB of HBM per device.

```python
import math
import jax
import jax.numpy as jnp
from jax import lax

HEAD_GROUP = 8
DH = 128
SEQUENCE_TOKENS = 12288


def key_table(key):
    shared_key = jax.random.fold_in(key, 21)
    return jax.random.uniform(shared_key, (SEQUENCE_TOKENS, HEAD_GROUP * DH), minval=-1.5, maxval=1.5)


def draw_key_inputs(key, part):
    return key_table(key).astype(jnp.float32).astype(jnp.bfloat16)


def query_table(key):
    key = jax.random.fold_in(key, 5)
    own = jax.random.uniform(key, (SEQUENCE_TOKENS, HEAD_GROUP * DH), minval=-1.5, maxval=1.5)
    mixed = own
    return jnp.clip(mixed, -1.5, 1.5).astype(jnp.float32).astype(jnp.bfloat16)


def draw_queries(key, part):
    return query_table(key)


def gate_table(key, fast_share):
    key = jax.random.fold_in(key, 11)
    rapid_random_key, baseline_random_key, jitter_random_key, spike_random_key, retain_random_key, gradual_random_key = jax.random.split(key, 6)
    bell_noise = jnp.clip(0.5 * jax.random.normal(jitter_random_key, (SEQUENCE_TOKENS, HEAD_GROUP)), -1.0, 1.0)
    random_jitter = bell_noise
    fast = jax.random.bernoulli(rapid_random_key, fast_share, (HEAD_GROUP,))
    fast_level = jax.random.uniform(baseline_random_key, (HEAD_GROUP,), minval=jnp.log(30.0), maxval=jnp.log(50.0))
    slow_level = jnp.log(SEQUENCE_TOKENS / (0.3 * jnp.log(10.0))) + jax.random.uniform(gradual_random_key, (HEAD_GROUP,), minval=0.0, maxval=1.6)
    baseline_offset = jnp.where(fast, fast_level, slow_level)
    spike_noise = jax.random.bernoulli(spike_random_key, 2.0 / SEQUENCE_TOKENS, (SEQUENCE_TOKENS, HEAD_GROUP))
    spike_amplitude = jax.random.uniform(retain_random_key, (SEQUENCE_TOKENS, HEAD_GROUP), minval=0.0, maxval=1.4)
    gate_scores_raw = jnp.where(spike_noise, spike_amplitude, baseline_offset[None, :] + random_jitter)
    return gate_scores_raw.astype(jnp.float32).astype(jnp.bfloat16)


def draw_gate_logits(key, part):
    return gate_table(key, 0.5)


def draw_lse(key, part):
    gate_scores_raw = gate_table(key, 0.5)
    key = jax.random.fold_in(key, 13)
    keep = jnp.exp(jax.nn.log_sigmoid(gate_scores_raw.astype(jnp.float32)))

    def step(total, keep_row):
        total = keep_row * total + 1.0
        return (total, total)
    final, totals = lax.scan(step, jnp.zeros((HEAD_GROUP,), jnp.float32), keep)
    jitter = jax.random.uniform(key, (SEQUENCE_TOKENS, HEAD_GROUP), minval=-0.2, maxval=0.2)
    return (jnp.log(totals) + 0.28 + jitter).astype(jnp.float32)


def block_scale(key, dims, cuts, low, top_value):
    loudness, own = 1.0, jax.random.fold_in(key, 6)
    for axis_at, blocks in cuts:
        draws = jnp.exp(jax.random.uniform(jax.random.fold_in(own, axis_at), (blocks,), jnp.float32, low / len(cuts), top_value / len(cuts)))
        loudness = loudness * jnp.repeat(draws, dims[axis_at] // blocks).reshape([-1 if axis == axis_at else 1 for axis in range(len(dims))])
    return loudness


def bell_draw(own_key, extent, scale, most, cuts=(), kind=jnp.bfloat16):
    loudness = block_scale(own_key, extent, cuts, -0.22, 0.18) if cuts else 1.0
    drawn = jax.random.normal(own_key, extent, jnp.float32) * scale * loudness
    return jnp.minimum(jnp.maximum(drawn, -most), most).astype(kind)


def setup_inputs(seed: int = 0) -> dict:
    key_of = jax.random.split(jax.random.key(seed), 8)
    queries = draw_queries(jax.random.fold_in(key_of[7], 71), 0)
    key_inputs = draw_key_inputs(jax.random.fold_in(key_of[7], 71), 0)
    value_inputs = bell_draw(key_of[2], (SEQUENCE_TOKENS, HEAD_GROUP * DH), 1.0, 6.0, ((0, 256),))
    out_grad = bell_draw(key_of[3], (SEQUENCE_TOKENS, HEAD_GROUP * DH), 1.0, 6.0, ((0, 256),))
    attn_output = bell_draw(key_of[4], (SEQUENCE_TOKENS, HEAD_GROUP * DH), 1.0, 6.0, ((0, 256),))
    gate_logits = draw_gate_logits(jax.random.fold_in(key_of[7], 71), 0)
    lse = draw_lse(jax.random.fold_in(key_of[7], 71), 0)
    return dict(queries=queries, key_inputs=key_inputs, value_inputs=value_inputs, out_grad=out_grad, attn_output=attn_output, gate_logits=gate_logits, lse=lse)


def head_backward(items):
    query_head, key_head, value_head, grad_head, output_head, curve_head, lse_head = items
    score_scale = DH ** -0.5
    block_len = math.gcd(SEQUENCE_TOKENS, 1024)
    block_count = SEQUENCE_TOKENS // block_len
    key_pos = jnp.arange(SEQUENCE_TOKENS, dtype=jnp.int32)

    def one_block(carry_in, block_index):
        key_acc, value_acc, column_acc = carry_in
        first_row = block_index * block_len
        query_blk = lax.dynamic_slice_in_dim(query_head, first_row, block_len, 0)
        grad_blk = lax.dynamic_slice_in_dim(grad_head, first_row, block_len, 0)
        output_blk = lax.dynamic_slice_in_dim(output_head, first_row, block_len, 0)
        curve_blk = lax.dynamic_slice_in_dim(curve_head, first_row, block_len, 0)
        lse_blk = lax.dynamic_slice_in_dim(lse_head, first_row, block_len, 0)
        query_pos = first_row + jnp.arange(block_len, dtype=jnp.int32)
        causal = key_pos[None, :] <= query_pos[:, None]
        scores = score_scale * jnp.dot(query_blk, key_head.T, preferred_element_type=jnp.float32) + curve_blk[:, None] - curve_head[None, :]
        probs = jnp.where(causal, jnp.exp(scores - lse_blk[:, None]), 0.0)
        row_delta = jnp.sum(grad_blk.astype(jnp.float32) * output_blk.astype(jnp.float32), axis=1)
        grad_probs = jnp.dot(grad_blk, value_head.T, preferred_element_type=jnp.float32)
        score_grad = probs * (grad_probs - row_delta[:, None])
        score_half = score_grad.astype(jnp.bfloat16)
        probs_half = probs.astype(jnp.bfloat16)
        query_part = score_scale * jnp.dot(score_half, key_head, preferred_element_type=jnp.float32)
        key_acc = key_acc + jnp.dot(score_half.T, query_blk, preferred_element_type=jnp.float32)
        value_acc = value_acc + jnp.dot(probs_half.T, grad_blk, preferred_element_type=jnp.float32)
        column_acc = column_acc + jnp.sum(score_grad, axis=0)
        return (key_acc, value_acc, column_acc), (query_part, jnp.sum(score_grad, axis=1))

    zero_rows = jnp.zeros((SEQUENCE_TOKENS, DH), jnp.float32)
    start = (zero_rows, zero_rows, jnp.zeros((SEQUENCE_TOKENS,), jnp.float32))
    (key_acc, value_acc, column_acc), (query_parts, row_parts) = lax.scan(one_block, start, jnp.arange(block_count, dtype=jnp.int32))
    query_grad = query_parts.reshape(SEQUENCE_TOKENS, DH)
    curve_grad = row_parts.reshape(SEQUENCE_TOKENS) - column_acc
    return query_grad, score_scale * key_acc, value_acc, curve_grad


def reference(queries, key_inputs, value_inputs, out_grad, attn_output, gate_logits, lse):
    def by_head(array):
        return array.reshape(SEQUENCE_TOKENS, HEAD_GROUP, DH).transpose(1, 0, 2)

    gate_float = gate_logits.astype(jnp.float32)
    log_gates = jax.nn.log_sigmoid(gate_float)
    curve = jnp.cumsum(log_gates, axis=0)
    query_grad, key_grad, value_grad, curve_grad = lax.map(head_backward, (by_head(queries), by_head(key_inputs), by_head(value_inputs), by_head(out_grad), by_head(attn_output), curve.T, lse.T))
    gate_sum = jnp.flip(jnp.cumsum(jnp.flip(curve_grad, 1), axis=1), 1)
    gate_grad = (gate_sum.T * jax.nn.sigmoid(-gate_float)).astype(jnp.bfloat16)

    def merged(array):
        return array.transpose(1, 0, 2).reshape(SEQUENCE_TOKENS, HEAD_GROUP * DH).astype(jnp.bfloat16)

    return merged(query_grad), merged(key_grad), merged(value_grad), gate_grad
```

```python
import functools
import math

import jax
import jax.numpy as jnp
from jax import lax
from jax.experimental import pallas as pl
from jax.experimental.pallas import tpu as pltpu
from jax.sharding import PartitionSpec as P

CORES = 2
LOG2E = math.log2(math.e)
F32 = jnp.float32
BF16 = jnp.bfloat16
NT = (((1,), (1,)), ((), ()))
NN = (((1,), (0,)), ((), ()))


def dot(a, b, dims):
    return lax.dot_general(a, b, dims, preferred_element_type=F32)


def lane_scan(value, reverse):
    width = value.shape[1]
    lane = lax.broadcasted_iota(jnp.int32, value.shape, 1)
    shift = 1
    while shift < width:
        if reverse:
            moved = pltpu.roll(value, width - shift, 1)
            value = value + jnp.where(lane < width - shift, moved, 0.0)
        else:
            moved = pltpu.roll(value, shift, 1)
            value = value + jnp.where(lane >= shift, moved, 0.0)
        shift *= 2
    return value


def body(
    X, Z, Y, R, D,
    q_in, k_in, v_in, g_in, o_in, gate_in, lse_in,
    dq_out, dk_out, dv_out, dgate_out,
    g_loc, o_loc, st_out,
    qst_in, kst_in, q_all, g_all, qst_all, k_all, v_all, kst_all,
    kt_all, kcol, tot_x, tot_z, pq, pk,
    dqt, row_sum, dq_own, dk_acc, dv_acc, cs_acc,
    dq_snd, dq_rcv, rs_snd, rs_rcv, dk_snd, dv_snd, dk_rcv, dv_rcv, cs_snd, cs_rcv,
    tot2_x, tot2_z, dq_fin, dk_fin, dv_fin, gs_snd, gs_rcv,
    loc_sem, p1_r, p1_s, z_r, z_s, x_r, x_s, t_r, t_s, t2_r, t2_s,
    dq_r, dq_s, rs_r, rs_s, dk_r, dk_s, f_r, f_s,
):
    H = Y * CORES
    B = H * R
    half = Z // 2
    scale = D ** -0.5
    ctx = lax.axis_index("ctx")
    y = lax.axis_index("head")
    c = ctx % CORES
    z = (ctx // CORES) % Z
    x = ctx // (CORES * Z)
    xr = X - 1 - x
    xq = jnp.where(z < half, x, xr)
    head = y * CORES + c
    part = c * Y + y

    def dev(x_, z_, c_, y_):
        return ((x_ * Z + z_) * CORES + c_, y_)

    def remote(src, dst, ssem, rsem, to):
        return pltpu.make_async_remote_copy(
            src_ref=src, dst_ref=dst, send_sem=ssem, recv_sem=rsem,
            device_id=to, device_id_type=pl.DeviceIdType.MESH,
        )

    def drain(ref, sem):
        pltpu.make_async_copy(ref, ref, sem).wait()

    loc = [
        pltpu.make_async_copy(g_in, g_loc, loc_sem.at[0]),
        pltpu.make_async_copy(o_in, o_loc, loc_sem.at[1]),
    ]
    for copy in loc:
        copy.start()

    barrier = pltpu.get_barrier_semaphore()
    group = [(dc, dy) for dy in range(Y) for dc in range(CORES)]
    partners = 0

    def greet(to):
        pl.semaphore_signal(barrier, inc=1, device_id=to, device_id_type=pl.DeviceIdType.MESH)

    for dc, dy in group:
        cc, yy = (c + dc) % CORES, (y + dy) % Y
        if (dc, dy) != (0, 0):
            greet(dev(x, z, cc, yy))
            partners += 1
        greet(dev(xr, z, cc, yy))
        partners += 1
    for d in range(1, Z):
        zz = (z + d) % Z
        greet(dev(x, zz, c, y))
        greet(dev(xr, zz, c, y))
        partners += 2
    for d in range(1, X):
        xx = (x + d) % X

        @pl.when(xx != xr)
        def _():
            greet(dev(xx, z, c, y))
    partners += X - 2
    pl.semaphore_wait(barrier, partners)

    row0 = pl.multiple_of(part * R, R)

    def to_home(src, dst, idx, to, here):
        if here is True:
            pltpu.make_async_copy(src, dst, p1_r.at[idx]).start()
        elif here is False:
            remote(src, dst, p1_s.at[idx], p1_r.at[idx], to).start()
        else:
            @pl.when(here)
            def _():
                pltpu.make_async_copy(src, dst, p1_r.at[idx]).start()

            @pl.when(jnp.logical_not(here))
            def _():
                remote(src, dst, p1_s.at[idx], p1_r.at[idx], to).start()

    def columns(h_):
        return pl.ds(pl.multiple_of(h_ * D, D), D)

    for dc, dy in group:
        cc, yy = (c + dc) % CORES, (y + dy) % Y
        hh = yy * CORES + cc
        mine = (dc, dy) == (0, 0)
        q_here = (z < half) if mine else False
        for idx, src, dst in ((0, q_in, q_all), (1, g_in, g_all)):
            to_home(src.at[:, columns(hh)], dst.at[z, pl.ds(row0, R), :], idx, dev(xq, z, cc, yy), q_here)
        for idx, src, dst in ((2, k_in, k_all), (3, v_in, v_all)):
            to_home(src.at[:, columns(hh)], dst.at[x, pl.ds(row0, R), :], idx, dev(x, z, cc, yy), mine)

    for copy in loc:
        copy.wait()
    st_out[...] = jnp.zeros_like(st_out)
    log_gate = jax.nn.log_sigmoid(gate_in[...].astype(F32)).T
    lse_t = lse_in[...].T
    for h in range(H):
        product = g_loc[:, h * D:(h + 1) * D].astype(F32) * o_loc[:, h * D:(h + 1) * D].astype(F32)
        st_out[h, 0:1, 0:R] = jnp.sum(product.T, axis=0, keepdims=True)
        st_out[h, 1:2, 0:R] = lse_t[h:h + 1, :]
        st_out[h, 2:3, 0:R] = log_gate[h:h + 1, :]
    for dc, dy in group:
        cc, yy = (c + dc) % CORES, (y + dy) % Y
        hh = yy * CORES + cc
        mine = (dc, dy) == (0, 0)
        to_home(st_out.at[hh], kst_in.at[part], 5, dev(x, z, cc, yy), mine)
        to_home(st_out.at[hh], qst_in.at[part], 4, dev(xq, z, cc, yy), (z < half) if mine else False)

    right, left = dev(x, (z + 1) % Z, c, y), dev(x, (z + Z - 1) % Z, c, y)
    ring = (q_all, qst_all, g_all)

    def hop(direction, slot, s):
        to = right if direction == 0 else left
        for arr, ref in enumerate(ring):
            last = (direction == 0) == (arr < 2)
            limit = half if last else half - 1

            @pl.when(s < limit)
            def _(arr=arr, ref=ref):
                remote(ref.at[slot], ref.at[slot], z_s.at[direction, arr, s], z_r.at[direction, arr, s], to).start()

    def hop_wait(direction, slot, s, arrs):
        for arr in arrs:
            drain(ring[arr].at[slot], z_r.at[direction, arr, s])

    def wide(tile):
        return jnp.concatenate([tile, jnp.zeros((8, B - 128), F32)], axis=1) if B > 128 else tile[:, :B]

    def assemble(ref):
        total = wide(ref[0])
        for s in range(1, H):
            total = total + pltpu.roll(wide(ref[s]), s * R, 1)
        return total

    drain(kst_in, p1_r.at[5])
    k_stats = assemble(kst_in)
    k_curve = lane_scan(k_stats, False)
    kst_all[x] = k_curve
    tot_x[x] = jnp.broadcast_to(k_curve[2:3, B - 1:B], (8, 128))
    for d in range(1, X):
        xx = (x + d) % X
        remote(tot_x.at[x], tot_x.at[x], t_s.at[0, xx], t_r.at[0, x], dev(xx, z, c, y)).start()

    drain(qst_in, p1_r.at[4])
    q_stats = assemble(qst_in)
    q_curve = lane_scan(q_stats, False)
    qst_all[z, 0:1, :] = (q_curve[2:3] - q_stats[1:2]) * LOG2E
    qst_all[z, 1:2, :] = q_stats[0:1]
    qst_all[z, 2:8, :] = jnp.zeros((6, B), F32)
    drain(q_all.at[z], p1_r.at[0])
    drain(g_all.at[z], p1_r.at[1])
    hop(0, z, 0)
    hop(1, z, 0)

    drain(k_all.at[x], p1_r.at[2])
    drain(v_all.at[x], p1_r.at[3])
    for d in range(1, X):
        xx = (x + d) % X
        to = dev(xx, z, c, y)
        for arr, ref in enumerate((k_all, v_all, kst_all)):
            remote(ref.at[x], ref.at[x], x_s.at[arr, xx], x_r.at[arr, x], to).start()

    def share_x(tot, recv):
        for d in range(1, X):
            xx = (x + d) % X
            drain(tot.at[xx], recv.at[0, xx])

    def share_z(tot, all_z, send, recv):
        all_z[z] = tot[...]
        for d in range(1, Z):
            zz = (z + d) % Z
            remote(all_z.at[z], all_z.at[z], send.at[1, zz], recv.at[1, z], dev(x, zz, c, y)).start()

    def share_end(all_z, recv):
        for d in range(1, Z):
            zz = (z + d) % Z
            drain(all_z.at[zz], recv.at[1, zz])

    share_x(tot_x, t_r)
    share_z(tot_x, tot_z, t_s, t_r)
    dk_acc[...] = jnp.zeros_like(dk_acc)
    dv_acc[...] = jnp.zeros_like(dv_acc)
    cs_acc[...] = jnp.zeros_like(cs_acc)
    for d in range(X):
        xx = (x + d) % X
        if d:
            for arr, ref in enumerate((k_all, v_all, kst_all)):
                drain(ref.at[xx], x_r.at[arr, xx])
        kt_all[xx] = k_all[xx].astype(F32).T.astype(BF16)
        column = kst_all[xx].T[:, 2:3] * LOG2E
        kcol[xx] = jnp.broadcast_to(column, (B, 128))
    share_end(tot_z, t_r)

    block_at = lax.broadcasted_iota(jnp.int32, (Z, X, 8, 128), 1) * Z + lax.broadcasted_iota(
        jnp.int32, (Z, X, 8, 128), 0
    )

    def sum_where(all_z, chosen):
        return jnp.sum(jnp.where(chosen, all_z[...], 0.0), axis=(0, 1))

    def slot_x(slot):
        return jnp.where(slot < half, x, xr)

    def fill_pq(slot, carry):
        pq[slot] = sum_where(tot_z, block_at < slot_x(slot) * Z + slot) * LOG2E
        return carry

    def fill_pk(kb, carry):
        pk[kb] = sum_where(tot_z, block_at < kb * Z + z) * LOG2E
        return carry

    lax.fori_loop(0, Z, fill_pq, 0)
    lax.fori_loop(0, X, fill_pk, 0)

    def lanes(value, width):
        return value[:, :width] if width <= 128 else jnp.concatenate([value] * (width // 128), axis=1)

    def pair(slot, kb, masked):
        k_blk, v_blk = k_all[kb], v_all[kb]
        q_blk, g_blk = q_all[slot], g_all[slot]
        away = pq[slot, 0:1, :] - pk[kb, 0:1, :]
        row = qst_all[slot, 0:1, :] + lanes(away, B)
        delta = qst_all[slot, 1:2, :]
        s = dot(k_blk, q_blk, NT)
        prob = jnp.exp2(s * (scale * LOG2E) + row - lanes(kcol[kb], B))
        if masked:
            key_at = lax.broadcasted_iota(jnp.int32, (B, B), 0)
            query_at = lax.broadcasted_iota(jnp.int32, (B, B), 1)
            prob = jnp.where(key_at <= query_at, prob, 0.0)
        grad = prob * (dot(v_blk, g_blk, NT) - delta)
        prob_half, grad_half = prob.astype(BF16), grad.astype(BF16)
        dv_acc[kb] += dot(prob_half, g_blk, NN)
        dk_acc[kb] += dot(grad_half, q_blk, NN)
        dqt[...] += dot(kt_all[kb], grad_half, NN)
        row_sum[0:1, :] += jnp.sum(grad, axis=0, keepdims=True)
        if B > 128:
            folded = grad[:, 0:128]
            for at in range(128, B, 128):
                folded = folded + grad[:, at:at + 128]
            cs_acc[kb] += folded
        else:
            cs_acc[kb, :, 0:B] += grad

    def dq_copy(slot):
        return remote(dq_snd.at[slot], dq_rcv.at[z], dq_s.at[slot], dq_r.at[z], dev(x, slot, c, y))

    def rs_copy(slot):
        return remote(rs_snd.at[slot], rs_rcv.at[z], rs_s.at[slot], rs_r.at[z], dev(slot_x(slot), slot, c, y))

    def one_slot(t, carry):
        s = (t + 1) // 2
        odd = t % 2 == 1
        slot = (jnp.where(odd, z - s, z + s) + Z) % Z

        @pl.when(jnp.logical_and(odd, s < half))
        def _():
            hop_wait(0, slot, s - 1, (0, 1, 2))
            hop(0, slot, s)
            other = (z + s) % Z
            hop_wait(1, other, s - 1, (0, 1, 2))
            hop(1, other, s)

        @pl.when(t == Z - 1)
        def _():
            hop_wait(0, slot, s - 1, (0, 1))
            hop_wait(1, slot, s - 1, (2,))

        at_x = slot_x(slot)
        dqt[...] = jnp.zeros_like(dqt)
        row_sum[...] = jnp.zeros_like(row_sum)
        full = at_x + jnp.where(z < slot, 1, 0)

        def one_pair(kb, inner):
            pair(slot, kb, False)
            return inner

        lax.fori_loop(0, full, one_pair, 0)

        @pl.when(slot == z)
        def _():
            pair(slot, at_x, True)

        rs_snd[slot] = row_sum[...]
        dq_now = dqt[...].T * scale

        @pl.when(slot == z)
        def _():
            dq_own[...] = dq_now

        @pl.when(slot != z)
        def _():
            dq_snd[slot] = dq_now.astype(BF16)
            dq_copy(slot).start()

        here = jnp.logical_and(slot == z, at_x == x)

        @pl.when(here)
        def _():
            pltpu.make_async_copy(rs_snd.at[slot], rs_rcv.at[z], rs_r.at[z]).start()

        @pl.when(jnp.logical_not(here))
        def _():
            rs_copy(slot).start()

        return carry

    lax.fori_loop(0, Z, one_slot, 0)

    def cs_lanes(kb):
        return jnp.broadcast_to(jnp.sum(cs_acc[kb].T, axis=0, keepdims=True), (8, B))

    for d in range(1, X):
        xx = (x + d) % X
        to = dev(xx, z, c, y)
        dk_snd[xx] = (dk_acc[xx] * scale).astype(BF16)
        dv_snd[xx] = dv_acc[xx].astype(BF16)
        cs_snd[xx] = cs_lanes(xx)
        for arr, (snd, rcv) in enumerate(((dk_snd, dk_rcv), (dv_snd, dv_rcv), (cs_snd, cs_rcv))):
            remote(snd.at[xx], rcv.at[x], dk_s.at[arr, xx], dk_r.at[arr, x], to).start()

    def give_back(value_ref, out_ref, idx, at_x, always_here):
        for dc, dy in group:
            cc, yy = (c + dc) % CORES, (y + dy) % Y
            src = value_ref.at[pl.ds(pl.multiple_of((cc * Y + yy) * R, R), R), :]
            dst = out_ref.at[:, columns(head)]
            to = dev(at_x, z, cc, yy)
            mine = (dc, dy) == (0, 0)
            if mine and always_here:
                pltpu.make_async_copy(src, dst, f_r.at[idx]).start()
            elif mine:
                @pl.when(at_x == x)
                def _(src=src, dst=dst):
                    pltpu.make_async_copy(src, dst, f_r.at[idx]).start()

                @pl.when(at_x != x)
                def _(src=src, dst=dst, to=to):
                    remote(src, dst, f_s.at[idx], f_r.at[idx], to).start()
            else:
                remote(src, dst, f_s.at[idx], f_r.at[idx], to).start()

    dq_sum = dq_own[...]
    for d in range(1, Z):
        zz = (z + d) % Z
        drain(dq_rcv.at[zz], dq_r.at[zz])
        dq_sum = dq_sum + dq_rcv[zz].astype(F32)
    dq_fin[...] = dq_sum.astype(BF16)
    give_back(dq_fin, dq_out, 0, xq, False)

    rows = jnp.zeros((8, B), F32)
    for d in range(Z):
        zz = (z + d) % Z
        drain(rs_rcv.at[zz], rs_r.at[zz])
        rows = rows + rs_rcv[zz]
    columns_sum = cs_lanes(x)
    dk_sum = dk_acc[x] * scale
    dv_sum = dv_acc[x]
    for d in range(1, X):
        xx = (x + d) % X
        drain(cs_rcv.at[xx], dk_r.at[2, xx])
        columns_sum = columns_sum + cs_rcv[xx]
    curve_grad = jnp.broadcast_to(rows[0:1], (8, B)) - columns_sum
    later = lane_scan(curve_grad, True)
    tot2_x[x] = jnp.broadcast_to(later[:, 0:1], (8, 128))
    for d in range(1, X):
        xx = (x + d) % X
        remote(tot2_x.at[x], tot2_x.at[x], t2_s.at[0, xx], t2_r.at[0, x], dev(xx, z, c, y)).start()
    for d in range(1, X):
        xx = (x + d) % X
        drain(dk_rcv.at[xx], dk_r.at[0, xx])
        dk_sum = dk_sum + dk_rcv[xx].astype(F32)
        drain(dv_rcv.at[xx], dk_r.at[1, xx])
        dv_sum = dv_sum + dv_rcv[xx].astype(F32)
    share_x(tot2_x, t2_r)
    share_z(tot2_x, tot2_z, t2_s, t2_r)
    dk_fin[...] = dk_sum.astype(BF16)
    give_back(dk_fin, dk_out, 1, x, True)
    dv_fin[...] = dv_sum.astype(BF16)
    give_back(dv_fin, dv_out, 2, x, True)
    share_end(tot2_z, t2_r)
    after = sum_where(tot2_z, block_at > x * Z + z)
    gate_sum = later + lanes(after, B)
    for s in range(H):
        moved = pltpu.roll(gate_sum, (B - s * R) % B, 1) if s else gate_sum
        gs_snd[s] = moved[:, 0:128] if B >= 128 else jnp.concatenate([moved, jnp.zeros((8, 128 - B), F32)], axis=1)
    for dc, dy in group:
        cc, yy = (c + dc) % CORES, (y + dy) % Y
        src, dst = gs_snd.at[cc * Y + yy], gs_rcv.at[head]
        if (dc, dy) == (0, 0):
            pltpu.make_async_copy(src, dst, f_r.at[3]).start()
        else:
            remote(src, dst, f_s.at[3], f_r.at[3], dev(x, z, cc, yy)).start()
    drain(gs_rcv, f_r.at[3])
    sub = lax.broadcasted_iota(jnp.int32, (8, 128), 0)
    by_head = jnp.zeros((8, 128), F32)
    for h in range(H):
        by_head = by_head + jnp.where(sub == h, gs_rcv[h], 0.0)
    gate_t = by_head.T[0:R, 0:H]
    dgate_out[...] = (gate_t * jax.nn.sigmoid(-gate_in[...].astype(F32))).astype(BF16)

    drain(dq_out, f_r.at[0])
    drain(dk_out, f_r.at[1])
    drain(dv_out, f_r.at[2])
    for d in range(1, X):
        xx = (x + d) % X
        for arr, ref in enumerate((k_all, v_all, kst_all)):
            drain(ref.at[x], x_s.at[arr, xx])
        for arr, ref in enumerate((dk_snd, dv_snd, cs_snd)):
            drain(ref.at[xx], dk_s.at[arr, xx])
        drain(tot_x.at[x], t_s.at[0, xx])
        drain(tot2_x.at[x], t2_s.at[0, xx])
    for d in range(1, Z):
        zz = (z + d) % Z
        drain(tot_z.at[z], t_s.at[1, zz])
        drain(tot2_z.at[z], t2_s.at[1, zz])
        drain(dq_snd.at[zz], dq_s.at[zz])
        drain(rs_snd.at[zz], rs_s.at[zz])

    @pl.when(xq != x)
    def _():
        drain(rs_snd.at[z], rs_s.at[z])

    for s in range(half):
        for direction in range(2):
            for arr, ref in enumerate(ring):
                last = (direction == 0) == (arr < 2)
                if s < (half if last else half - 1):
                    slot = (z - s + Z) % Z if direction == 0 else (z + s) % Z
                    drain(ref.at[slot], z_s.at[direction, arr, s])
    few, full = pl.ds(0, B - R), pl.ds(0, B)
    drain(k_all.at[x, few, :], p1_s.at[2])
    drain(v_all.at[x, few, :], p1_s.at[3])
    drain(kst_in.at[pl.ds(0, H - 1)], p1_s.at[5])
    drain(dk_fin.at[few, :], f_s.at[1])
    drain(dv_fin.at[few, :], f_s.at[2])
    drain(gs_snd.at[pl.ds(0, H - 1)], f_s.at[3])

    @pl.when(z < half)
    def _():
        drain(q_all.at[z, few, :], p1_s.at[0])
        drain(g_all.at[z, few, :], p1_s.at[1])
        drain(qst_in.at[pl.ds(0, H - 1)], p1_s.at[4])
        drain(dq_fin.at[few, :], f_s.at[0])

    @pl.when(z >= half)
    def _():
        drain(q_all.at[z, full, :], p1_s.at[0])
        drain(g_all.at[z, full, :], p1_s.at[1])
        drain(qst_in, p1_s.at[4])
        drain(dq_fin.at[full, :], f_s.at[0])


def plane(contexts):
    chips = contexts // CORES
    along_x = 1
    while 2 * along_x * 2 * along_x * 2 <= chips * 2 and along_x * 2 * 2 <= chips:
        along_x *= 2
    return along_x, chips // along_x


def per_device(X, Z, Y, *args):
    R, columns = args[0].shape
    H = Y * CORES
    D = columns // H
    B = H * R
    half = Z // 2
    vm = pltpu.VMEM
    dma = pltpu.SemaphoreType.DMA
    any_spec = pl.BlockSpec(memory_space=pl.ANY)
    vm_spec = pl.BlockSpec(memory_space=pltpu.VMEM)
    scratch = [
        vm((R, columns), BF16), vm((R, columns), BF16), vm((H, 8, 128), F32),
        vm((H, 8, 128), F32), vm((H, 8, 128), F32),
        vm((Z, B, D), BF16), vm((Z, B, D), BF16), vm((Z, 8, B), F32),
        vm((X, B, D), BF16), vm((X, B, D), BF16), vm((X, 8, B), F32),
        vm((X, D, B), BF16), vm((X, B, 128), F32),
        vm((X, 8, 128), F32), vm((Z, X, 8, 128), F32), vm((Z, 8, 128), F32), vm((X, 8, 128), F32),
        vm((D, B), F32), vm((8, B), F32), vm((B, D), F32),
        vm((X, B, D), F32), vm((X, B, D), F32), vm((X, B, 128), F32),
        vm((Z, B, D), BF16), vm((Z, B, D), BF16), vm((Z, 8, B), F32), vm((Z, 8, B), F32),
        vm((X, B, D), BF16), vm((X, B, D), BF16), vm((X, B, D), BF16), vm((X, B, D), BF16),
        vm((X, 8, B), F32), vm((X, 8, B), F32),
        vm((X, 8, 128), F32), vm((Z, X, 8, 128), F32),
        vm((B, D), BF16), vm((B, D), BF16), vm((B, D), BF16),
        vm((H, 8, 128), F32), vm((H, 8, 128), F32),
        dma((2,)), dma((6,)), dma((6,)), dma((2, 3, half)), dma((2, 3, half)),
        dma((3, X)), dma((3, X)), dma((2, Z)), dma((2, Z)), dma((2, Z)), dma((2, Z)),
        dma((Z,)), dma((Z,)), dma((Z,)), dma((Z,)), dma((3, X)), dma((3, X)), dma((4,)), dma((4,)),
    ]
    big = jax.ShapeDtypeStruct((R, columns), BF16)
    return pl.pallas_call(
        functools.partial(body, X, Z, Y, R, D),
        out_shape=(big, big, big, jax.ShapeDtypeStruct((R, H), BF16)),
        in_specs=[any_spec] * 5 + [vm_spec] * 2,
        out_specs=(any_spec, any_spec, any_spec, vm_spec),
        scratch_shapes=scratch,
        compiler_params=pltpu.CompilerParams(
            collective_id=0, has_side_effects=True, vmem_limit_bytes=48 * 1024 * 1024
        ),
    )(*args)


def solution(mesh):
    X, Z = plane(mesh.shape["ctx"])
    Y = mesh.shape["head"]
    rows = P(("ctx", "head"), None)
    return jax.shard_map(
        functools.partial(per_device, X, Z, Y),
        mesh=mesh,
        in_specs=(rows,) * 7,
        out_specs=(rows,) * 4,
        check_vma=False,
    )
```

```python
import functools
import math

import jax
import jax.numpy as jnp
from jax import lax
from jax.experimental import pallas as pl
from jax.experimental.pallas import tpu as pltpu
from jax.sharding import PartitionSpec as P

CORES = 2
WIDTH = 128
LOG2E = math.log2(math.e)
F32 = jnp.float32
BF16 = jnp.bfloat16
NT = (((1,), (1,)), ((), ()))
NN = (((1,), (0,)), ((), ()))


def dot(a, b, dims):
    return lax.dot_general(a, b, dims, preferred_element_type=F32)


def iota(shape, axis):
    return lax.broadcasted_iota(jnp.int32, shape, axis)


def section_of(index, size, count):
    return sum(((index >= k * size).astype(jnp.int32) for k in range(1, count)), jnp.zeros_like(index))


def section_scan(value, size, count, reverse):
    lane = iota(value.shape, 1)
    inner = lane - size * section_of(lane, size, count)
    width, shift = value.shape[1], 1
    while shift < size:
        if reverse:
            value = value + jnp.where(inner < size - shift, pltpu.roll(value, width - shift, 1), 0.0)
        else:
            value = value + jnp.where(inner >= shift, pltpu.roll(value, shift, 1), 0.0)
        shift *= 2
    return value


def row_scan(value, reverse):
    row, rows = iota(value.shape, 0), value.shape[0]

    def moved(arr, shift):
        if reverse:
            return jnp.where(row < rows - shift, pltpu.roll(arr, rows - shift, 0), 0.0)
        return jnp.where(row >= shift, pltpu.roll(arr, shift, 0), 0.0)

    value, shift = moved(value, 1), 1
    while shift < rows:
        value = value + moved(value, shift)
        shift *= 2
    return value


def lanes(value, width):
    return value[:, :width] if width <= 128 else jnp.concatenate([value] * (width // 128), axis=1)


def body(
    X, Z, Y, R, KC,
    q_in, k_in, v_in, g_in, o_in, gate_in, lse_in,
    dq_out, dk_out, dv_out, dgate_out,
    g_loc, o_loc, gate_pad, st_out, qst_in, kst_in,
    q_all, g_all, qst_all, k_all, v_all, kst_all, kcol, kpos, tot_all, p_all,
    kt_all, q_row, dqt, dqt_own, row_acc, dk_acc, dv_acc, cs_acc,
    sib_snd, sib_rcv, dq_snd, dq_rcv, rs_snd, rs_rcv, dk_snd, dv_snd, dk_rcv, dv_rcv, cs_snd, cs_rcv,
    after_all, dq_fin, dk_fin, dv_fin, gs_snd, gs_rcv,
    loc_sem, p1_r, p1_s, x_r, x_s, y_r, y_s, sib_r, sib_s, qs_r, qs_s, ks_r, ks_s,
    t_r, t_s, dsib_r, dsib_s, dq_r, dq_s, rs_r, rs_s, dk_r, dk_s, cs_r, cs_s, f_r, f_s,
):
    D, H = WIDTH, Z
    half, CY = Z // 2, CORES * Y
    HB, B = half * R, Z * R
    scale = D ** -0.5
    ctx = lax.axis_index("ctx")
    y = lax.axis_index("head")
    c = ctx % CORES
    z = (ctx // CORES) % Z
    x = ctx // (CORES * Z)
    xr = X - 1 - x
    xk = jnp.where(z < half, x, xr)
    cy = c * Y + y
    mesh_id = pl.DeviceIdType.MESH

    def dev(x_, z_, c_, y_):
        return ((x_ * Z + z_) * CORES + c_, y_)

    def remote(src, dst, ssem, rsem, to):
        return pltpu.make_async_remote_copy(
            src_ref=src, dst_ref=dst, send_sem=ssem, recv_sem=rsem, device_id=to, device_id_type=mesh_id
        )

    def drain(ref, sem):
        pltpu.make_async_copy(ref, ref, sem).wait()

    def send(src, dst, ssem, rsem, to, here):
        if here is False:
            remote(src, dst, ssem, rsem, to).start()
        elif here is True:
            pltpu.make_async_copy(src, dst, rsem).start()
        else:
            @pl.when(here)
            def _():
                pltpu.make_async_copy(src, dst, rsem).start()

            @pl.when(jnp.logical_not(here))
            def _():
                remote(src, dst, ssem, rsem, to).start()

    loc = [
        pltpu.make_async_copy(g_in, g_loc, loc_sem.at[0]),
        pltpu.make_async_copy(o_in, o_loc, loc_sem.at[1]),
    ]
    for copy in loc:
        copy.start()

    barrier = pltpu.get_barrier_semaphore()
    plane = [(dx, dc, dy) for dx in range(X) for dc in range(CORES) for dy in range(Y)][1:]

    def greet(to):
        pl.semaphore_signal(barrier, inc=1, device_id=to, device_id_type=mesh_id)

    for d in range(1, Z):
        zz = (z + d) % Z
        greet(dev(x, zz, c, y))
        greet(dev(xr, zz, c, y))
    for dx, dc, dy in plane:
        greet(dev((x + dx) % X, z, (c + dc) % CORES, (y + dy) % Y))
    pl.semaphore_wait(barrier, 2 * (Z - 1) + len(plane))

    def columns(h_):
        return pl.ds(pl.multiple_of(h_ * D, D), D)

    z_half = z // half

    def z_rows(block):
        return pl.ds(pl.multiple_of(block * HB + (z % half) * R, R), R)

    def block_rows(block):
        return pl.ds(pl.multiple_of(block * HB, HB), HB)

    for idx, src, dst in ((0, q_in, q_all), (1, g_in, g_all), (2, k_in, k_all), (3, v_in, v_all)):
        for d in range(Z):
            zz = (z + d) % Z
            if idx < 2:
                at, to, here = dst.at[2 * x + z_half, z_rows(c), :], dev(x, zz, c, y), d == 0
            else:
                at, to = dst.at[z_half, z_rows(y), :], dev(xk, zz, c, y)
                here = (xk == x) if d == 0 else False
            send(src.at[:, columns(zz)], at, p1_s.at[idx], p1_r.at[idx], to, here)

    for copy in loc:
        copy.wait()
    st_out[...] = jnp.zeros_like(st_out)
    gate_pad[...] = jnp.zeros_like(gate_pad)
    gate_float = gate_in[...].astype(F32)
    gate_pad[0:H, 0:R] = jax.nn.log_sigmoid(gate_float)
    curve = section_scan(gate_pad[...], R, 1, False)
    lse_rows = lse_in[...]
    for h in range(H):
        cut = slice(h * D, (h + 1) * D)
        product = g_loc[:, cut].astype(F32) * o_loc[:, cut].astype(F32)
        st_out[h, 0:1, 0:R] = jnp.sum(product.T, axis=0, keepdims=True)
        st_out[h, 1:2, 0:R] = lse_rows[h:h + 1, :]
        st_out[h, 2:3, 0:R] = curve[h:h + 1, 0:R]
    for d in range(Z):
        zz = (z + d) % Z
        send(st_out.at[zz], qst_in.at[z], p1_s.at[4], p1_r.at[4], dev(x, zz, c, y), d == 0)
        send(
            st_out.at[zz], kst_in.at[z], p1_s.at[5], p1_r.at[5], dev(xk, zz, c, y),
            (xk == x) if d == 0 else False,
        )

    def q_block(ref, x_, c_):
        return ref.at[pl.ds(2 * x_, 2), block_rows(c_), :]

    def k_block(ref, y_):
        return ref.at[:, block_rows(y_), :]

    sibling = dev(x, z, 1 - c, y)
    queries = [functools.partial(q_block, ref, c_=c) for ref in (q_all, g_all)]
    keys = [functools.partial(k_block, ref) for ref in (k_all, v_all)]

    def x_dev(x_):
        return dev(x_, z, c, y)

    def y_dev(y_):
        return dev(x, z, c, y_)

    def ring_start(blocks, arr, at, n, place, snd, rcv):
        if n > 1:
            block = blocks[arr](at)
            remote(block, block, snd.at[arr, 0], rcv.at[arr, 0], place((at + 1) % n)).start()
        if n > 2:
            remote(block, block, snd.at[arr, 1], rcv.at[arr, 1], place((at + n - 1) % n)).start()

    def ring_onward(blocks, arr, at, n, place, snd, rcv):
        if n > 2:
            came, to = ((at + n - 1) % n, (at + 1) % n) if arr == 0 else ((at + 1) % n, (at + n - 1) % n)
            drain(blocks[arr](came), rcv.at[arr, arr])
            remote(blocks[arr](came), blocks[arr](came), snd.at[arr, 2], rcv.at[arr, 2], place(to)).start()
        elif n > 1:
            drain(blocks[arr]((at + 1) % n), rcv.at[arr, 0])

    def ring_other(blocks, arr, at, n, rcv):
        if n > 2:
            drain(blocks[arr]((at + 1) % n if arr == 0 else (at + n - 1) % n), rcv.at[arr, 1 - arr])

    def ring_last(blocks, arr, at, n, rcv):
        if n > 2:
            drain(blocks[arr]((at + 2) % n), rcv.at[arr, 2])

    def ring_sent(blocks, arr, at, n, snd):
        block = blocks[arr](at)
        for k in range(0 if n == 1 else 1 if n == 2 else 3):
            drain(block, snd.at[arr, k])

    def to_sibling(arr, x_):
        block = queries[arr](x_)
        remote(block, block, sib_s.at[arr, x_], sib_r.at[arr, x_], sibling).start()

    for arr in range(2):
        drain(queries[arr](x), p1_r.at[arr])
        ring_start(queries, arr, x, X, x_dev, x_s, x_r)
        to_sibling(arr, x)

    def wide(tile):
        return jnp.concatenate([tile, jnp.zeros((8, B - 128), F32)], axis=1) if B > 128 else tile[:, :B]

    def assemble(ref):
        total = wide(ref[0])
        for s in range(1, Z):
            total = total + pltpu.roll(wide(ref[s]), s * R, 1)
        return total

    row_at = iota((8, 128), 0)
    drain(qst_in, p1_r.at[4])
    totals = jnp.zeros((8, 128), F32)
    for s in range(Z):
        totals = jnp.where(row_at == s, jnp.broadcast_to(qst_in[s, 2:3, R - 1:R], (8, 128)), totals)
    tot_all[x * CY + cy] = totals

    def spread(ref, slot, semr, sems):
        for dx, dc, dy in plane:
            to = dev((x + dx) % X, z, (c + dc) % CORES, (y + dy) % Y)
            remote(ref.at[slot], ref.at[slot], sems, semr, to).start()

    spread(tot_all, x * CY + cy, t_r.at[0], t_s.at[0])
    q_stats = assemble(qst_in)
    xc = x * CORES + c
    qst_all[xc, 0:1, :] = q_stats[2:3] - q_stats[1:2]
    qst_all[xc, 1:2, :] = q_stats[0:1]
    qst_all[xc, 2:8, :] = jnp.zeros((6, B), F32)
    q_team = [(dx, dc) for dx in range(X) for dc in range(CORES)][1:]
    for dx, dc in q_team:
        x_, c_ = (x + dx) % X, (c + dc) % CORES
        mine = qst_all.at[xc]
        remote(mine, mine, qs_s.at[0], qs_r.at[0], dev(x_, z, c_, y)).start()

    drain(kst_in, p1_r.at[5])
    kst_all[y] = assemble(kst_in)
    for dy in range(1, Y):
        mine = kst_all.at[y]
        remote(mine, mine, ks_s.at[0], ks_r.at[0], y_dev((y + dy) % Y)).start()
    for arr in range(2):
        drain(keys[arr](y), p1_r.at[2 + arr])
        ring_start(keys, arr, y, Y, y_dev, y_s, y_r)

    dk_acc[...] = jnp.zeros_like(dk_acc)
    dv_acc[...] = jnp.zeros_like(dv_acc)
    cs_acc[...] = jnp.zeros_like(cs_acc)
    dqt[...] = jnp.zeros_like(dqt)
    row_acc[...] = jnp.zeros_like(row_acc)
    k_at = iota((Y * HB, 128), 0)
    k_y = section_of(k_at, HB, Y)
    k_rest = k_at - HB * k_y
    k_z = section_of(k_rest, R, half)
    kpos[...] = k_z * (CY * R) + c * (Y * R) + k_y * R + (k_rest - R * k_z)
    q_at = iota((8, B), 1)
    q_c = section_of(q_at, HB, CORES)
    q_rest = q_at - HB * q_c
    q_z = section_of(q_rest, R, half)
    qpos = q_z * (CY * R) + q_c * (Y * R) + y * R + (q_rest - R * q_z)

    for arr in range(2):
        ring_onward(queries, arr, x, X, x_dev, x_s, x_r)
        if X > 1:
            to_sibling(arr, (x + X - 1) % X if arr == 0 or X == 2 else (x + 1) % X)
    for arr in range(2):
        ring_onward(keys, arr, y, Y, y_dev, y_s, y_r)
    if X > 2:
        for arr in range(2):
            ring_other(queries, arr, x, X, x_r)
            to_sibling(arr, (x + 1) % X if arr == 0 else (x + X - 1) % X)

    few = X * CY - 1
    drain(tot_all.at[pl.ds(0, few)], t_r.at[0])
    before = jnp.zeros((8, 128), F32)
    for x_ in range(X):
        level = jnp.zeros((8, 128), F32)
        for k in range(CY):
            level = level + tot_all[x_ * CY + k]
        run = before + row_scan(level, False)
        for k in range(CY):
            p_all[x_ * CY + k] = run
            run = run + tot_all[x_ * CY + k]
        before = before + jnp.sum(level, axis=0, keepdims=True)

    piece_row, piece_lane = iota((8, B), 0), iota((8, B), 1)
    in_piece = piece_row == section_of(piece_lane, R, Z)

    def along_lanes(tile):
        return jnp.sum(jnp.where(in_piece, lanes(tile, B), 0.0), axis=0, keepdims=True)

    low = iota((8, B), 1) < HB

    def halves(first, second):
        return (
            jnp.where(low, first, pltpu.roll(second, HB, 1)),
            jnp.where(low, pltpu.roll(first, HB, 1), second),
        )

    drain(qst_all.at[pl.ds(0, len(q_team))], qs_r.at[0])
    for x_ in range(X):
        rows = []
        for c_ in range(CORES):
            bias = along_lanes(p_all[x_ * CY + c_ * Y + y])
            stat = qst_all[x_ * CORES + c_]
            rows.append(jnp.where(iota((8, B), 0) == 0, (stat + bias) * LOG2E, stat))
        lo, hi = halves(*rows)
        q_row[2 * x_] = lo
        q_row[2 * x_ + 1] = hi

    if Y > 1:
        drain(kst_all.at[pl.ds(0, Y - 1)], ks_r.at[0])
    for y_ in range(Y):
        tile = jnp.where(row_at < half, p_all[x * CY + c * Y + y_], p_all[xr * CY + c * Y + y_])
        column = ((kst_all[y_] + along_lanes(tile)) * LOG2E).T[:, 2:3]
        spread_column = jnp.broadcast_to(column, (B, 128))
        kcol[0, y_ * HB:(y_ + 1) * HB, :] = spread_column[0:HB]
        kcol[1, y_ * HB:(y_ + 1) * HB, :] = spread_column[HB:B]

    for arr in range(2):
        ring_other(keys, arr, y, Y, y_r)
    for arr in range(2):
        ring_last(keys, arr, y, Y, y_r)
    if X > 2:
        for arr in range(2):
            ring_last(queries, arr, x, X, x_r)
            to_sibling(arr, (x + 2) % X)
    for arr in range(2):
        for x_ in range(X):
            drain(q_block(q_all, x_, 1 - c), sib_r.at[arr, x_])

    def pair(u, kh, masked):
        q_blk, g_blk, stat = q_all[u], g_all[u], q_row[u]
        row, delta = stat[0:1], stat[1:2]

        def chunk(k, carry):
            at = pl.ds(pl.multiple_of(k * KC, KC), KC)
            k_blk, v_blk = k_all[kh, at, :], v_all[kh, at, :]
            s = dot(k_blk, q_blk, NT)
            prob = jnp.exp2(s * (scale * LOG2E) + row - lanes(kcol[kh, at, :], B))
            if masked:
                prob = jnp.where(lanes(kpos[at, :], B) <= qpos[0:1], prob, 0.0)
            grad = prob * (dot(v_blk, g_blk, NT) - delta)
            prob_half, grad_half = prob.astype(BF16), grad.astype(BF16)
            dv_acc[kh, at, :] += dot(prob_half, g_blk, NN)
            dk_acc[kh, at, :] += dot(grad_half, q_blk, NN)
            dqt[u] += dot(kt_all[kh, k], grad_half, NN)
            row_acc[u, 0:1, :] += jnp.sum(grad, axis=0, keepdims=True)
            if B > 128:
                folded = grad[:, 0:128]
                for lane in range(128, B, 128):
                    folded = folded + grad[:, lane:lane + 128]
                cs_acc[kh, at, :] += folded
            else:
                cs_acc[kh, at, 0:B] += grad
            return carry

        lax.fori_loop(0, Y * HB // KC, chunk, 0)

    for kh in range(2):
        for k in range(Y * HB // KC):
            kt_all[kh, k] = k_all[kh, k * KC:(k + 1) * KC, :].astype(F32).T.astype(BF16)
    for kh in range(2):
        first = 2 * x if kh == 0 else 2 * xr + 1
        pair(first, kh, True)

        def one(u, carry, kh=kh):
            pair(u, kh, False)
            return carry

        lax.fori_loop(first + 1, 2 * X, one, 0)

    for x_ in range(X):
        lo, hi = halves(row_acc[2 * x_], row_acc[2 * x_ + 1])
        for c_, tile in ((0, lo), (1, hi)):
            rs_snd[x_ * CORES + c_] = tile

    def team(dx, dc):
        return (x + dx) % X, (c + dc) % CORES

    for dx, dc in [(0, 0)] + q_team:
        x_, c_ = team(dx, dc)
        send(
            rs_snd.at[x_ * CORES + c_], rs_rcv.at[xc], rs_s.at[0], rs_r.at[0], dev(x_, z, c_, y), (dx, dc) == (0, 0)
        )
    for y_ in range(Y):
        rows = pl.ds(y_ * HB, HB)
        column = jnp.concatenate([cs_acc[0, rows, :], cs_acc[1, rows, :]], axis=0)
        cs_snd[y_] = jnp.broadcast_to(jnp.sum(column.T, axis=0, keepdims=True), (8, B))
    for dy in range(Y):
        y_ = (y + dy) % Y
        send(cs_snd.at[y_], cs_rcv.at[0, y], cs_s.at[0], cs_r.at[0], y_dev(y_), dy == 0)
        send(cs_snd.at[y_], cs_rcv.at[1, y], cs_s.at[1], cs_r.at[1], dev(xr, z, c, y_), False)

    for dx in range(X):
        x_ = (x + dx) % X
        for hf in range(2):
            dqt_unit = dqt[2 * x_ + hf].T * scale
            lower, upper = dqt_unit[0:HB], dqt_unit[HB:B]
            mine = jnp.where(c == 0, lower, upper)
            theirs = jnp.where(c == 0, upper, lower)
            sib_snd[x_, hf] = theirs.astype(BF16)
            dqt_own[x_, hf] = mine
        remote(sib_snd.at[x_], sib_rcv.at[x_], dsib_s.at[x_], dsib_r.at[x_], sibling).start()

    for dy in range(1, Y):
        y_ = (y + dy) % Y
        rows = block_rows(y_)
        for kh in range(2):
            dk_snd[y_, kh] = (dk_acc[kh, rows, :] * scale).astype(BF16)
            dv_snd[y_, kh] = dv_acc[kh, rows, :].astype(BF16)
        remote(dk_snd.at[y_], dk_rcv.at[y], dk_s.at[0, y_], dk_r.at[0, y], y_dev(y_)).start()
        remote(dv_snd.at[y_], dv_rcv.at[y], dk_s.at[1, y_], dk_r.at[1, y], y_dev(y_)).start()

    for dx in range(1, X):
        x_ = (x + dx) % X
        drain(sib_rcv.at[x_], dsib_r.at[x_])
        dq_snd[x_] = (dqt_own[x_] + sib_rcv[x_].astype(F32)).astype(BF16)
        remote(dq_snd.at[x_], dq_rcv.at[x], dq_s.at[x_], dq_r.at[x], x_dev(x_)).start()

    drain(rs_rcv, rs_r.at[0])
    drain(cs_rcv.at[0], cs_r.at[0])
    drain(cs_rcv.at[1], cs_r.at[1])
    rows_sum = jnp.zeros((8, B), F32)
    for x_ in range(X):
        for c_ in range(CORES):
            rows_sum = rows_sum + rs_rcv[x_ * CORES + c_]
    columns_sum = jnp.zeros((8, B), F32)
    for y_ in range(Y):
        columns_sum = columns_sum + jnp.where(low, cs_rcv[0, y_], cs_rcv[1, y_])
    later = section_scan(jnp.broadcast_to(rows_sum[0:1], (8, B)) - columns_sum, R, Z, True)
    totals = jnp.zeros((8, 128), F32)
    for s in range(Z):
        totals = jnp.where(row_at == s, jnp.broadcast_to(later[0:1, s * R:s * R + 1], (8, 128)), totals)
    after_all[x * CY + cy] = totals
    spread(after_all, x * CY + cy, t_r.at[1], t_s.at[1])

    def give_back(fin, out, idx, keyed):
        for d in range(Z):
            zz = (z + d) % Z
            src = fin.at[zz // half, pl.ds(pl.multiple_of((zz % half) * R, R), R), :]
            dst = out.at[:, columns(z)]
            at_x = jnp.where(zz < half, x, xr) if keyed else x
            here = False if d else ((at_x == x) if keyed else True)
            send(src, dst, f_s.at[idx], f_r.at[idx], dev(at_x, zz, c, y), here)

    for rcv, acc, fin, out, idx, factor in (
        (dk_rcv, dk_acc, dk_fin, dk_out, 1, scale), (dv_rcv, dv_acc, dv_fin, dv_out, 2, 1.0)
    ):
        own = block_rows(y)
        sums = [acc[kh, own, :] * factor for kh in range(2)]
        for dy in range(1, Y):
            y_ = (y + dy) % Y
            drain(rcv.at[y_], dk_r.at[idx - 1, y_])
            sums = [sums[kh] + rcv[y_, kh].astype(F32) for kh in range(2)]
        for kh in range(2):
            fin[kh] = sums[kh].astype(BF16)
        give_back(fin, out, idx, True)

    drain(sib_rcv.at[x], dsib_r.at[x])
    dq_sum = dqt_own[x] + sib_rcv[x].astype(F32)
    for dx in range(1, X):
        x_ = (x + dx) % X
        drain(dq_rcv.at[x_], dq_r.at[x_])
        dq_sum = dq_sum + dq_rcv[x_].astype(F32)
    dq_fin[...] = dq_sum.astype(BF16)
    give_back(dq_fin, dq_out, 0, False)

    drain(after_all.at[pl.ds(0, few)], t_r.at[1])
    after = jnp.zeros((8, 128), F32)
    for x_ in range(X):
        level = jnp.zeros((8, 128), F32)
        for k in range(CY):
            tile = after_all[x_ * CY + k]
            level = level + tile
            after = after + jnp.where(jnp.logical_and(x_ == x, k > cy), tile, 0.0)
        after = after + jnp.where(x_ == x, row_scan(level, True), 0.0)
        after = after + jnp.where(x_ > x, jnp.sum(level, axis=0, keepdims=True), 0.0)
    gate_sum = later + along_lanes(after)
    for s in range(Z):
        moved = pltpu.roll(gate_sum, (B - s * R) % B, 1) if s else gate_sum
        gs_snd[s] = moved[:, 0:128] if B >= 128 else jnp.concatenate([moved, jnp.zeros((8, 128 - B), F32)], axis=1)
    for d in range(Z):
        zz = (z + d) % Z
        send(gs_snd.at[zz], gs_rcv.at[z], f_s.at[3], f_r.at[3], dev(x, zz, c, y), d == 0)
    drain(gs_rcv, f_r.at[3])
    by_head = jnp.zeros((8, 128), F32)
    for h in range(H):
        by_head = by_head + jnp.where(row_at == h, gs_rcv[h], 0.0)
    dgate_out[...] = (by_head[0:H, 0:R] * jax.nn.sigmoid(-gate_float)).astype(BF16)

    for arr in range(2):
        ring_sent(queries, arr, x, X, x_s)
        ring_sent(keys, arr, y, Y, y_s)
        for x_ in range(X):
            drain(queries[arr](x_), sib_s.at[arr, x_])
        for dy in range(1, Y):
            y_ = (y + dy) % Y
            drain(dk_snd.at[y_], dk_s.at[arr, y_])
    drain(qst_all.at[pl.ds(0, len(q_team))], qs_s.at[0])
    drain(rs_snd.at[pl.ds(0, len(q_team))], rs_s.at[0])
    if Y > 1:
        drain(kst_all.at[pl.ds(0, Y - 1)], ks_s.at[0])
        drain(cs_snd.at[pl.ds(0, Y - 1)], cs_s.at[0])
    drain(cs_snd, cs_s.at[1])
    drain(tot_all.at[pl.ds(0, few)], t_s.at[0])
    drain(after_all.at[pl.ds(0, few)], t_s.at[1])
    for dx in range(X):
        x_ = (x + dx) % X
        drain(sib_snd.at[x_], dsib_s.at[x_])
        if dx:
            drain(dq_snd.at[x_], dq_s.at[x_])

    for idx in range(4):
        less, more = q_in.at[:, pl.ds(0, (Z - 1) * D)], q_in
        if idx < 2:
            drain(less, p1_s.at[idx])
        else:
            @pl.when(xk == x)
            def _(idx=idx, less=less):
                drain(less, p1_s.at[idx])

            @pl.when(xk != x)
            def _(idx=idx, more=more):
                drain(more, p1_s.at[idx])
    drain(qst_in.at[pl.ds(0, Z - 1)], p1_s.at[4])
    drain(gs_snd.at[pl.ds(0, Z - 1)], f_s.at[3])

    @pl.when(xk == x)
    def _():
        drain(kst_in.at[pl.ds(0, Z - 1)], p1_s.at[5])
        drain(q_in.at[:, pl.ds(0, (Z - 1) * D)], f_s.at[1])
        drain(q_in.at[:, pl.ds(0, (Z - 1) * D)], f_s.at[2])

    @pl.when(xk != x)
    def _():
        drain(kst_in, p1_s.at[5])
        drain(q_in, f_s.at[1])
        drain(q_in, f_s.at[2])

    drain(q_in.at[:, pl.ds(0, (Z - 1) * D)], f_s.at[0])
    drain(dq_out, f_r.at[0])
    drain(dk_out, f_r.at[1])
    drain(dv_out, f_r.at[2])


def per_device(X, Y, *args):
    R, columns = args[0].shape
    D, Z, C = WIDTH, columns // WIDTH, CORES
    HB, B, H = Z // 2 * R, Z * R, Z
    KC = min(256, Y * HB)
    vm = pltpu.VMEM
    dma = pltpu.SemaphoreType.DMA
    any_spec = pl.BlockSpec(memory_space=pl.ANY)
    vm_spec = pl.BlockSpec(memory_space=pltpu.VMEM)
    queries, keys = (2 * X, C * HB, D), (2, Y * HB, D)
    block, tile = (2, HB, D), (8, 128)
    scratch = [
        vm((R, columns), BF16), vm((R, columns), BF16), vm(tile, F32),
        vm((H,) + tile, F32), vm((Z,) + tile, F32), vm((Z,) + tile, F32),
        vm(queries, BF16), vm(queries, BF16), vm((X * C, 8, B), F32),
        vm(keys, BF16), vm(keys, BF16), vm((Y, 8, B), F32),
        vm((2, Y * HB, 128), F32), vm((Y * HB, 128), jnp.int32),
        vm((X * C * Y,) + tile, F32), vm((X * C * Y,) + tile, F32),
        vm((2, Y * HB // KC, D, KC), BF16), vm((2 * X, 8, B), F32),
        vm((2 * X, D, B), F32), vm((X,) + block, F32), vm((2 * X, 8, B), F32),
        vm(keys, F32), vm(keys, F32), vm((2, Y * HB, 128), F32),
        vm((X,) + block, BF16), vm((X,) + block, BF16), vm((X,) + block, BF16), vm((X,) + block, BF16),
        vm((X * C, 8, B), F32), vm((X * C, 8, B), F32),
        vm((Y,) + block, BF16), vm((Y,) + block, BF16), vm((Y,) + block, BF16), vm((Y,) + block, BF16),
        vm((Y, 8, B), F32), vm((2, Y, 8, B), F32),
        vm((X * C * Y,) + tile, F32), vm(block, BF16), vm(block, BF16), vm(block, BF16),
        vm((Z,) + tile, F32), vm((H,) + tile, F32),
        dma((2,)), dma((6,)), dma((6,)), dma((2, 3)), dma((2, 3)), dma((2, 3)), dma((2, 3)),
        dma((2, X)), dma((2, X)), dma((1,)), dma((1,)), dma((1,)), dma((1,)),
        dma((2,)), dma((2,)), dma((X,)), dma((X,)), dma((X,)), dma((X,)), dma((1,)), dma((1,)),
        dma((2, Y)), dma((2, Y)), dma((2,)), dma((2,)), dma((4,)), dma((4,)),
    ]
    big = jax.ShapeDtypeStruct((R, columns), BF16)
    dq, dk, dv, dgate = pl.pallas_call(
        functools.partial(body, X, Z, Y, R, KC),
        out_shape=(big, big, big, jax.ShapeDtypeStruct((H, R), BF16)),
        in_specs=[any_spec] * 5 + [vm_spec] * 2,
        out_specs=(any_spec, any_spec, any_spec, vm_spec),
        scratch_shapes=scratch,
        compiler_params=pltpu.CompilerParams(
            collective_id=0, has_side_effects=True, vmem_limit_bytes=63 * 1024 * 1024
        ),
    )(*args[:5], args[5].T, args[6].T)
    return dq, dk, dv, dgate.T


def solution(mesh):
    rows = P(("ctx", "head"), None)

    def whole(*args):
        X = mesh.shape["ctx"] // (CORES * (args[0].shape[1] // WIDTH))
        return jax.shard_map(
            functools.partial(per_device, X, mesh.shape["head"]),
            mesh=mesh,
            in_specs=(rows,) * 7,
            out_specs=(rows,) * 4,
            check_vma=False,
        )(*args)

    return whole
```

```python
import functools
import math

import jax
import jax.numpy as jnp
from jax import lax
from jax.experimental import pallas as pl
from jax.experimental.pallas import tpu as pltpu
from jax.sharding import PartitionSpec as P

CORES = 2
WIDTH = 128
LOG2E = math.log2(math.e)
F32 = jnp.float32
BF16 = jnp.bfloat16
NT = (((1,), (1,)), ((), ()))
NN = (((1,), (0,)), ((), ()))


def dot(a, b, dims):
    return lax.dot_general(a, b, dims, preferred_element_type=F32)


def iota(shape, axis):
    return lax.broadcasted_iota(jnp.int32, shape, axis)


def section_of(index, size, count):
    return sum(((index >= k * size).astype(jnp.int32) for k in range(1, count)), jnp.zeros_like(index))


def section_scan(value, size, count, reverse):
    lane = iota(value.shape, 1)
    inner = lane - size * section_of(lane, size, count)
    width, shift = value.shape[1], 1
    while shift < size:
        if reverse:
            value = value + jnp.where(inner < size - shift, pltpu.roll(value, width - shift, 1), 0.0)
        else:
            value = value + jnp.where(inner >= shift, pltpu.roll(value, shift, 1), 0.0)
        shift *= 2
    return value


def row_scan(value, reverse):
    row, rows = iota(value.shape, 0), value.shape[0]

    def moved(arr, shift):
        if reverse:
            return jnp.where(row < rows - shift, pltpu.roll(arr, rows - shift, 0), 0.0)
        return jnp.where(row >= shift, pltpu.roll(arr, shift, 0), 0.0)

    value, shift = moved(value, 1), 1
    while shift < rows:
        value = value + moved(value, shift)
        shift *= 2
    return value


def lanes(value, width):
    return value[:, :width] if width <= 128 else jnp.concatenate([value] * (width // 128), axis=1)


def body(
    X, Z, Y, R,
    q_in, k_in, v_in, g_in, o_in, gate_in, lse_in,
    dq_out, dk_out, dv_out, dgate_out,
    g_loc, o_loc, gate_pad, st_out, qst_in, kst_in,
    q_all, g_all, qst_all, k_all, v_all, kst_all, kcol, kpos, tot_all, p_all,
    kt_own, kt_next, kt_far, q_row, dqt, dqt_own, row_acc, dk_acc, dv_acc, cs_acc,
    sib_snd, sib_rcv, dq_snd, dq_rcv, rs_snd, rs_rcv, dk_snd, dv_snd, dk_rcv, dv_rcv, cs_snd, cs_rcv,
    after_all, dq_fin, dk_fin, dv_fin, gs_snd, gs_rcv,
    loc_sem, p1_r, p1_s, x_r, x_s, y_r, y_s, sib_r, sib_s, qs_r, qs_s, ks_r, ks_s,
    t_r, t_s, dsib_r, dsib_s, dq_r, dq_s, rs_r, rs_s, dk_r, dk_s, cs_r, cs_s, f_r, f_s,
):
    D, H = WIDTH, Z
    half, CY = Z // 2, CORES * Y
    HB, B = half * R, Z * R
    scale = D ** -0.5
    ctx = lax.axis_index("ctx")
    y = lax.axis_index("head")
    c = ctx % CORES
    z = (ctx // CORES) % Z
    x = ctx // (CORES * Z)
    xr = X - 1 - x
    xk = jnp.where(z < half, x, xr)
    cy = c * Y + y
    mesh_id = pl.DeviceIdType.MESH

    def dev(x_, z_, c_, y_):
        return ((x_ * Z + z_) * CORES + c_, y_)

    def remote(src, dst, ssem, rsem, to):
        return pltpu.make_async_remote_copy(
            src_ref=src, dst_ref=dst, send_sem=ssem, recv_sem=rsem, device_id=to, device_id_type=mesh_id
        )

    def drain(ref, sem):
        pltpu.make_async_copy(ref, ref, sem).wait()

    def send(src, dst, ssem, rsem, to, here):
        if here is False:
            remote(src, dst, ssem, rsem, to).start()
        elif here is True:
            pltpu.make_async_copy(src, dst, rsem).start()
        else:
            @pl.when(here)
            def _():
                pltpu.make_async_copy(src, dst, rsem).start()

            @pl.when(jnp.logical_not(here))
            def _():
                remote(src, dst, ssem, rsem, to).start()

    loc = [
        pltpu.make_async_copy(g_in, g_loc, loc_sem.at[0]),
        pltpu.make_async_copy(o_in, o_loc, loc_sem.at[1]),
    ]
    for copy in loc:
        copy.start()

    barrier = pltpu.get_barrier_semaphore()
    plane = [(dx, dc, dy) for dx in range(X) for dc in range(CORES) for dy in range(Y)][1:]

    def greet(to):
        pl.semaphore_signal(barrier, inc=1, device_id=to, device_id_type=mesh_id)

    for d in range(1, Z):
        zz = (z + d) % Z
        greet(dev(x, zz, c, y))
        greet(dev(xr, zz, c, y))
    for dx, dc, dy in plane:
        greet(dev((x + dx) % X, z, (c + dc) % CORES, (y + dy) % Y))
    for copy in loc:
        copy.wait()
    st_out[...] = jnp.zeros_like(st_out)
    gate_pad[...] = jnp.zeros_like(gate_pad)
    gate_float = gate_in[...].astype(F32)
    gate_pad[0:H, 0:R] = jax.nn.log_sigmoid(gate_float)
    curve = section_scan(gate_pad[...], R, 1, False)
    lse_rows = lse_in[...]
    for h in range(H):
        cut = slice(h * D, (h + 1) * D)
        product = g_loc[:, cut].astype(F32) * o_loc[:, cut].astype(F32)
        st_out[h, 0:1, 0:R] = jnp.sum(product.T, axis=0, keepdims=True)
        st_out[h, 1:2, 0:R] = lse_rows[h:h + 1, :]
        st_out[h, 2:3, 0:R] = curve[h:h + 1, 0:R]
    pl.semaphore_wait(barrier, 2 * (Z - 1) + len(plane))

    z_order = sorted(range(Z), key=lambda d: -min(d, Z - d))

    def columns(h_):
        return pl.ds(pl.multiple_of(h_ * D, D), D)

    z_half = z // half

    def z_rows(block):
        return pl.ds(pl.multiple_of(block * HB + (z % half) * R, R), R)

    def block_rows(block):
        return pl.ds(pl.multiple_of(block * HB, HB), HB)

    for d in z_order:
        zz = (z + d) % Z
        send(st_out.at[zz], qst_in.at[z], p1_s.at[4], p1_r.at[4], dev(x, zz, c, y), d == 0)
        send(
            st_out.at[zz], kst_in.at[z], p1_s.at[5], p1_r.at[5], dev(xk, zz, c, y),
            (xk == x) if d == 0 else False,
        )

    for idx, src, dst in ((0, q_in, q_all), (1, g_in, g_all), (2, k_in, k_all), (3, v_in, v_all)):
        for d in z_order:
            zz = (z + d) % Z
            if idx < 2:
                at, to, here = dst.at[x, z_half, z_rows(c), :], dev(x, zz, c, y), d == 0
            else:
                at, to = dst.at[z_half, z_rows(0), :], dev(xk, zz, c, y)
                here = (xk == x) if d == 0 else False
            send(src.at[:, columns(zz)], at, p1_s.at[idx], p1_r.at[idx], to, here)

    def q_block(ref, x_, c_):
        return ref.at[x_, :, block_rows(c_), :]

    def k_block(ref, slot):
        return ref.at[:, block_rows(slot), :]

    sibling = dev(x, z, 1 - c, y)
    queries = [functools.partial(q_block, ref, c_=c) for ref in (q_all, g_all)]
    keys = [functools.partial(k_block, ref) for ref in (k_all, v_all)]

    def x_dev(d):
        return dev((x + d) % X, z, c, y)

    def y_dev(d):
        return dev(x, z, c, (y + d) % Y)

    order = [0, 1, Y - 1, 2][:Y] if Y > 2 else [0, 1][:Y]

    def q_id(d, e):
        return (x + d) % X

    def k_id(d, e):
        return order.index((d - e) % Y)

    def ring_copy(blocks, arr, name, d, e, place, section, snd, rcv):
        src, dst = blocks[arr](name(d, 0)), blocks[arr](name(d, e))
        return remote(src, dst, snd.at[arr, section], rcv.at[arr, section], place(e))

    def ring_start(blocks, arr, name, n, place, snd, rcv):
        if n > 1:
            ring_copy(blocks, arr, name, 0, 1, place, 0, snd, rcv).start()
        if n > 2:
            ring_copy(blocks, arr, name, 0, -1, place, 1, snd, rcv).start()

    def ring_onward(blocks, arr, name, n, place, snd, rcv):
        came = -1 if arr == 0 else 1
        if n > 1:
            drain(blocks[arr](name(came, 0)), rcv.at[arr, arr if n > 2 else 0])
        if n > 2:
            ring_copy(blocks, arr, name, came, -came, place, 2, snd, rcv).start()

    def ring_other(blocks, arr, name, n, rcv):
        if n > 2:
            drain(blocks[arr](name(1 if arr == 0 else -1, 0)), rcv.at[arr, 1 - arr])

    def ring_last(blocks, arr, name, n, rcv):
        if n > 2:
            drain(blocks[arr](name(2, 0)), rcv.at[arr, 2])

    def ring_sent(blocks, arr, name, n, snd):
        block = blocks[arr](name(0, 0))
        for k in range(0 if n == 1 else 1 if n == 2 else 3):
            drain(block, snd.at[arr, k])

    def to_sibling(arr, x_):
        block = queries[arr](x_)
        remote(block, block, sib_s.at[arr, x_], sib_r.at[arr, x_], sibling).start()

    def wide(tile):
        return jnp.concatenate([tile, jnp.zeros((8, B - 128), F32)], axis=1) if B > 128 else tile[:, :B]

    def assemble(ref):
        total = wide(ref[0])
        for s in range(1, Z):
            total = total + pltpu.roll(wide(ref[s]), s * R, 1)
        return total

    row_at = iota((8, 128), 0)
    drain(qst_in, p1_r.at[4])
    totals = jnp.zeros((8, 128), F32)
    for s in range(Z):
        totals = jnp.where(row_at == s, jnp.broadcast_to(qst_in[s, 2:3, R - 1:R], (8, 128)), totals)
    tot_all[x * CY + cy] = totals

    def spread(ref, slot, semr, sems):
        for dx, dc, dy in plane:
            to = dev((x + dx) % X, z, (c + dc) % CORES, (y + dy) % Y)
            remote(ref.at[slot], ref.at[slot], sems, semr, to).start()

    spread(tot_all, x * CY + cy, t_r.at[0], t_s.at[0])
    q_stats = assemble(qst_in)
    xc = x * CORES + c
    qst_all[xc, 0:1, :] = q_stats[2:3] - q_stats[1:2]
    qst_all[xc, 1:2, :] = q_stats[0:1]
    qst_all[xc, 2:8, :] = jnp.zeros((6, B), F32)
    q_team = [(dx, dc) for dx in range(X) for dc in range(CORES)][1:]
    for dx, dc in q_team:
        x_, c_ = (x + dx) % X, (c + dc) % CORES
        mine = qst_all.at[xc]
        remote(mine, mine, qs_s.at[0], qs_r.at[0], dev(x_, z, c_, y)).start()

    drain(kst_in, p1_r.at[5])
    kst_all[y] = assemble(kst_in)
    for dy in range(1, Y):
        mine = kst_all.at[y]
        remote(mine, mine, ks_s.at[0], ks_r.at[0], y_dev(dy)).start()
    for arr in range(2):
        drain(queries[arr](x), p1_r.at[arr])
        ring_start(queries, arr, q_id, X, x_dev, x_s, x_r)
        to_sibling(arr, x)

    dk_acc[...] = jnp.zeros_like(dk_acc)
    dv_acc[...] = jnp.zeros_like(dv_acc)
    cs_acc[...] = jnp.zeros_like(cs_acc)
    dqt[...] = jnp.zeros_like(dqt)
    row_acc[...] = jnp.zeros_like(row_acc)
    k_at = iota((HB, 128), 0)
    k_z = section_of(k_at, R, half)
    for slot, dy in enumerate(order):
        k_y = (y + dy) % Y
        kpos[slot * HB:(slot + 1) * HB, :] = k_z * (CY * R) + c * (Y * R) + k_y * R + (k_at - R * k_z)
    q_at = iota((8, 2 * B), 1)
    q_half = (q_at >= B).astype(jnp.int32)
    q_rest = q_at - B * q_half
    q_c = section_of(q_rest, HB, CORES)
    q_rest = q_rest - HB * q_c
    q_z = section_of(q_rest, R, half)
    qpos = (q_half * half + q_z) * (CY * R) + q_c * (Y * R) + y * R + (q_rest - R * q_z)

    few = X * CY - 1
    drain(tot_all.at[pl.ds(0, few)], t_r.at[0])
    before = jnp.zeros((8, 128), F32)
    for x_ in range(X):
        level = jnp.zeros((8, 128), F32)
        for k in range(CY):
            level = level + tot_all[x_ * CY + k]
        run = before + row_scan(level, False)
        for k in range(CY):
            p_all[x_ * CY + k] = run
            run = run + tot_all[x_ * CY + k]
        before = before + jnp.sum(level, axis=0, keepdims=True)

    piece_row, piece_lane = iota((8, B), 0), iota((8, B), 1)
    in_piece = piece_row == section_of(piece_lane, R, Z)

    def along_lanes(tile):
        return jnp.sum(jnp.where(in_piece, lanes(tile, B), 0.0), axis=0, keepdims=True)

    low = iota((8, B), 1) < HB

    def halves(first, second):
        return (
            jnp.where(low, first, pltpu.roll(second, HB, 1)),
            jnp.where(low, pltpu.roll(first, HB, 1), second),
        )

    drain(qst_all.at[pl.ds(0, len(q_team))], qs_r.at[0])
    for x_ in range(X):
        rows = []
        for c_ in range(CORES):
            bias = along_lanes(p_all[x_ * CY + c_ * Y + y])
            stat = qst_all[x_ * CORES + c_]
            rows.append(jnp.where(iota((8, B), 0) == 0, (stat + bias) * LOG2E, stat))
        q_row[x_] = jnp.concatenate(halves(*rows), axis=1)

    if Y > 1:
        drain(kst_all.at[pl.ds(0, Y - 1)], ks_r.at[0])
    for slot, dy in enumerate(order):
        y_ = (y + dy) % Y
        tile = jnp.where(row_at < half, p_all[x * CY + c * Y + y_], p_all[xr * CY + c * Y + y_])
        column = ((kst_all[y_] + along_lanes(tile)) * LOG2E).T[:, 2:3]
        spread_column = jnp.broadcast_to(column, (B, 128))
        kcol[0, slot * HB:(slot + 1) * HB, :] = spread_column[0:HB]
        kcol[1, slot * HB:(slot + 1) * HB, :] = spread_column[HB:B]

    def pair(x_, kh, rows, turned, masked):
        q_blk, g_blk = q_all[x_].reshape(2 * B, D), g_all[x_].reshape(2 * B, D)
        stat = q_row[x_]
        row, delta = stat[0:1], stat[1:2]
        k_blk, v_blk = k_all[kh, rows, :], v_all[kh, rows, :]
        s = dot(k_blk, q_blk, NT)
        prob = jnp.exp2(s * (scale * LOG2E) + row - lanes(kcol[kh, rows, :], 2 * B))
        if masked:
            at = kpos[rows, :] + kh * (half * CY * R)
            prob = jnp.where(lanes(at, 2 * B) <= qpos[0:1], prob, 0.0)
        grad = prob * (dot(v_blk, g_blk, NT) - delta)
        prob_half, grad_half = prob.astype(BF16), grad.astype(BF16)
        dv_acc[kh, rows, :] += dot(prob_half, g_blk, NN)
        dk_acc[kh, rows, :] += dot(grad_half, q_blk, NN)
        dqt[x_] += dot(turned[kh], grad_half, NN)
        row_acc[x_, 0:1, :] += jnp.sum(grad, axis=0, keepdims=True)
        if B > 64:
            folded = grad[:, 0:128]
            for lane in range(128, 2 * B, 128):
                folded = folded + grad[:, lane:lane + 128]
            cs_acc[kh, rows, :] += folded
        else:
            cs_acc[kh, rows, 0:2 * B] += grad

    def key_turn(turned, rows):
        for kh in range(2):
            turned[kh] = k_all[kh, rows, :].astype(F32).T.astype(BF16)

    kt_all = (kt_own, kt_next, kt_far) if Y > 2 else (kt_own, kt_far)

    def sib_wait(x_):
        for arr in range(2):
            drain(q_block((q_all, g_all)[arr], x_, 1 - c), sib_r.at[arr, x_])

    def curve_send(slot):
        rows, dy = pl.ds(slot * HB, HB), order[slot]
        column = jnp.concatenate([cs_acc[0, rows, :], cs_acc[1, rows, :]], axis=0)
        cs_snd[slot] = jnp.broadcast_to(jnp.sum(column.T, axis=0, keepdims=True), (8, B))
        send(cs_snd.at[slot], cs_rcv.at[0, y], cs_s.at[0], cs_r.at[0], y_dev(dy), dy == 0)
        send(cs_snd.at[slot], cs_rcv.at[1, y], cs_s.at[1], cs_r.at[1], dev(xr, z, c, (y + dy) % Y), False)

    key_sums = ((dk_acc, dk_snd, dk_rcv, scale), (dv_acc, dv_snd, dv_rcv, 1.0))

    def key_send(slot):
        side = order.index(-order[slot] % Y) - 1
        for arr, (acc, snd, rcv, factor) in enumerate(key_sums):
            for kh in range(2):
                snd[slot, kh] = (acc[kh, slot * HB:(slot + 1) * HB, :] * factor).astype(BF16)
            remote(
                snd.at[slot], rcv.at[side], dk_s.at[arr, slot], dk_r.at[arr, side], y_dev(order[slot])
            ).start()

    def query_steps(i):
        if i == 1:
            for arr in range(2):
                ring_onward(queries, arr, q_id, X, x_dev, x_s, x_r)
                to_sibling(arr, (x + X - 1) % X if arr == 0 else (x + 1) % X)
            if X > 2:
                for arr in range(2):
                    ring_other(queries, arr, q_id, X, x_r)
                    to_sibling(arr, (x + 1) % X if arr == 0 else (x + X - 1) % X)
        if i == X - 1:
            for arr in range(2):
                ring_onward(keys, arr, k_id, Y, y_dev, y_s, y_r)
        if i == 3:
            for arr in range(2):
                ring_last(queries, arr, q_id, X, x_r)
                to_sibling(arr, (x + 2) % X)
        if i:
            sib_wait((x + x_order[i]) % X)

    def rows_done(x_):
        tiles = halves(row_acc[x_, :, 0:B], row_acc[x_, :, B:2 * B])
        for c_ in range(CORES):
            rs_snd[x_ * CORES + c_] = tiles[c_]
            src, dst = rs_snd.at[x_ * CORES + c_], rs_rcv.at[xc]
            here = jnp.logical_and(x_ == x, c_ == c)
            send(src, dst, rs_s.at[0], rs_r.at[0], dev(x_, z, c_, y), here)
        dq_part = dqt[x_].T * scale
        for hf in range(2):
            lower, upper = dq_part[hf * B:hf * B + HB], dq_part[hf * B + HB:hf * B + B]
            dqt_own[x_, hf] = jnp.where(c == 0, lower, upper)
            sib_snd[x_, hf] = jnp.where(c == 0, upper, lower).astype(BF16)
        remote(sib_snd.at[x_], sib_rcv.at[x_], dsib_s.at[x_], dsib_r.at[x_], sibling).start()

    def rows_home(x_):
        drain(sib_rcv.at[x_], dsib_r.at[x_])
        dq_snd[x_] = (dqt_own[x_] + sib_rcv[x_].astype(F32)).astype(BF16)
        remote(dq_snd.at[x_], dq_rcv.at[x], dq_s.at[x_], dq_r.at[x], dev(x_, z, c, y)).start()

    x_order = [0, 1, X - 1, 2][:X] if X > 2 else [0, 1][:X]
    bands = {1: [(0, 1)], 2: [(0, 1), (1, 1)], 4: [(0, 1), (1, 2), (3, 1)]}[Y]

    def pick(values, at):
        return sum(jnp.where(at == k, v, 0) for k, v in enumerate(values))

    for arr in range(2):
        drain(keys[arr](0), p1_r.at[2 + arr])
        ring_start(keys, arr, k_id, Y, y_dev, y_s, y_r)
    sib_wait(x)

    def band(first_slot, slots, turned, last, before_step):
        rows = pl.ds(first_slot * HB, slots * HB)
        key_turn(turned, rows)

        def step(i, carry):
            for k in range(1, X):
                if before_step:
                    pl.when(i == k)(functools.partial(before_step, k))
            x_ = (x + pick(x_order, X - 1 - i if last else i)) % X

            def key_half(kh, inner):
                first = jnp.where(kh == 0, x, xr)

                @pl.when(x_ > first)
                def _():
                    pair(x_, kh, rows, turned, False)

                @pl.when(x_ == first)
                def _():
                    pair(x_, kh, rows, turned, True)

                return inner

            lax.fori_loop(0, 2, key_half, 0)
            if last:
                rows_done(x_)

                @pl.when(i > 0)
                def _():
                    rows_home((x + pick(x_order, X - i)) % X)

            return carry

        lax.fori_loop(0, X, step, 0)

    for b, (first_slot, slots) in enumerate(bands):
        if b == 1:
            for arr in range(2):
                ring_other(keys, arr, k_id, Y, y_r)
        if b == 2:
            for arr in range(2):
                ring_last(keys, arr, k_id, Y, y_r)
        band(first_slot, slots, kt_all[b], b == len(bands) - 1, None if b else query_steps)
        for slot in range(first_slot, first_slot + slots):
            curve_send(slot)
        if b:
            for slot in range(first_slot, first_slot + slots):
                key_send(slot)

    def give_back(fin, out, idx, keyed):
        for d in z_order:
            zz = (z + d) % Z
            src = fin.at[zz // half, pl.ds(pl.multiple_of((zz % half) * R, R), R), :]
            dst = out.at[:, columns(z)]
            at_x = jnp.where(zz < half, x, xr) if keyed else x
            here = False if d else ((at_x == x) if keyed else True)
            send(src, dst, f_s.at[idx], f_r.at[idx], dev(at_x, zz, c, y), here)

    drain(sib_rcv.at[x], dsib_r.at[x])
    dq_sum = dqt_own[x] + sib_rcv[x].astype(F32)
    for dx in range(1, X):
        x_ = (x + dx) % X
        drain(dq_rcv.at[x_], dq_r.at[x_])
        dq_sum = dq_sum + dq_rcv[x_].astype(F32)
    dq_fin[...] = dq_sum.astype(BF16)
    give_back(dq_fin, dq_out, 0, False)

    drain(rs_rcv, rs_r.at[0])
    drain(cs_rcv.at[0], cs_r.at[0])
    drain(cs_rcv.at[1], cs_r.at[1])
    rows_sum = jnp.zeros((8, B), F32)
    for x_ in range(X):
        for c_ in range(CORES):
            rows_sum = rows_sum + rs_rcv[x_ * CORES + c_]
    columns_sum = jnp.zeros((8, B), F32)
    for y_ in range(Y):
        columns_sum = columns_sum + jnp.where(low, cs_rcv[0, y_], cs_rcv[1, y_])
    later = section_scan(jnp.broadcast_to(rows_sum[0:1], (8, B)) - columns_sum, R, Z, True)
    totals = jnp.zeros((8, 128), F32)
    for s in range(Z):
        totals = jnp.where(row_at == s, jnp.broadcast_to(later[0:1, s * R:s * R + 1], (8, 128)), totals)
    after_all[x * CY + cy] = totals
    spread(after_all, x * CY + cy, t_r.at[1], t_s.at[1])

    for rcv, acc, fin, out, idx, factor in (
        (dk_rcv, dk_acc, dk_fin, dk_out, 1, scale), (dv_rcv, dv_acc, dv_fin, dv_out, 2, 1.0)
    ):
        sums = [acc[kh, 0:HB, :] * factor for kh in range(2)]
        for side in range(Y - 1):
            drain(rcv.at[side], dk_r.at[idx - 1, side])
            sums = [sums[kh] + rcv[side, kh].astype(F32) for kh in range(2)]
        for kh in range(2):
            fin[kh] = sums[kh].astype(BF16)
        give_back(fin, out, idx, True)

    drain(after_all.at[pl.ds(0, few)], t_r.at[1])
    after = jnp.zeros((8, 128), F32)
    for x_ in range(X):
        level = jnp.zeros((8, 128), F32)
        for k in range(CY):
            tile = after_all[x_ * CY + k]
            level = level + tile
            after = after + jnp.where(jnp.logical_and(x_ == x, k > cy), tile, 0.0)
        after = after + jnp.where(x_ == x, row_scan(level, True), 0.0)
        after = after + jnp.where(x_ > x, jnp.sum(level, axis=0, keepdims=True), 0.0)
    gate_sum = later + along_lanes(after)
    for s in range(Z):
        moved = pltpu.roll(gate_sum, (B - s * R) % B, 1) if s else gate_sum
        gs_snd[s] = moved[:, 0:128] if B >= 128 else jnp.concatenate([moved, jnp.zeros((8, 128 - B), F32)], axis=1)
    for d in z_order:
        zz = (z + d) % Z
        send(gs_snd.at[zz], gs_rcv.at[z], f_s.at[3], f_r.at[3], dev(x, zz, c, y), d == 0)
    drain(gs_rcv, f_r.at[3])
    by_head = jnp.zeros((8, 128), F32)
    for h in range(H):
        by_head = by_head + jnp.where(row_at == h, gs_rcv[h], 0.0)
    dgate_out[...] = (by_head[0:H, 0:R] * jax.nn.sigmoid(-gate_float)).astype(BF16)

    for arr in range(2):
        ring_sent(queries, arr, q_id, X, x_s)
        ring_sent(keys, arr, k_id, Y, y_s)
        for x_ in range(X):
            drain(queries[arr](x_), sib_s.at[arr, x_])
        for slot in range(1, Y):
            drain(dk_snd.at[slot], dk_s.at[arr, slot])
    drain(qst_all.at[pl.ds(0, len(q_team))], qs_s.at[0])
    drain(rs_snd.at[pl.ds(0, len(q_team))], rs_s.at[0])
    if Y > 1:
        drain(kst_all.at[pl.ds(0, Y - 1)], ks_s.at[0])
        drain(cs_snd.at[pl.ds(0, Y - 1)], cs_s.at[0])
    drain(cs_snd, cs_s.at[1])
    drain(tot_all.at[pl.ds(0, few)], t_s.at[0])
    drain(after_all.at[pl.ds(0, few)], t_s.at[1])
    for dx in range(X):
        x_ = (x + dx) % X
        drain(sib_snd.at[x_], dsib_s.at[x_])
        if dx:
            drain(dq_snd.at[x_], dq_s.at[x_])

    for idx in range(4):
        less, more = q_in.at[:, pl.ds(0, (Z - 1) * D)], q_in
        if idx < 2:
            drain(less, p1_s.at[idx])
        else:
            @pl.when(xk == x)
            def _(idx=idx, less=less):
                drain(less, p1_s.at[idx])

            @pl.when(xk != x)
            def _(idx=idx, more=more):
                drain(more, p1_s.at[idx])
    drain(qst_in.at[pl.ds(0, Z - 1)], p1_s.at[4])
    drain(gs_snd.at[pl.ds(0, Z - 1)], f_s.at[3])

    @pl.when(xk == x)
    def _():
        drain(kst_in.at[pl.ds(0, Z - 1)], p1_s.at[5])
        drain(q_in.at[:, pl.ds(0, (Z - 1) * D)], f_s.at[1])
        drain(q_in.at[:, pl.ds(0, (Z - 1) * D)], f_s.at[2])

    @pl.when(xk != x)
    def _():
        drain(kst_in, p1_s.at[5])
        drain(q_in, f_s.at[1])
        drain(q_in, f_s.at[2])

    drain(q_in.at[:, pl.ds(0, (Z - 1) * D)], f_s.at[0])
    drain(dq_out, f_r.at[0])
    drain(dk_out, f_r.at[1])
    drain(dv_out, f_r.at[2])


def per_device(X, Y, *args):
    R, columns = args[0].shape
    D, Z, C = WIDTH, columns // WIDTH, CORES
    HB, B, H = Z // 2 * R, Z * R, Z
    vm = pltpu.VMEM
    dma = pltpu.SemaphoreType.DMA
    any_spec = pl.BlockSpec(memory_space=pl.ANY)
    vm_spec = pl.BlockSpec(memory_space=pltpu.VMEM)
    queries, keys = (X, 2, C * HB, D), (2, Y * HB, D)
    block, tile = (2, HB, D), (8, 128)
    scratch = [
        vm((R, columns), BF16), vm((R, columns), BF16), vm(tile, F32),
        vm((H,) + tile, F32), vm((Z,) + tile, F32), vm((Z,) + tile, F32),
        vm(queries, BF16), vm(queries, BF16), vm((X * C, 8, B), F32),
        vm(keys, BF16), vm(keys, BF16), vm((Y, 8, B), F32),
        vm((2, Y * HB, 128), F32), vm((Y * HB, 128), jnp.int32),
        vm((X * C * Y,) + tile, F32), vm((X * C * Y,) + tile, F32),
        vm((2, D, HB), BF16), vm((2, D, 2 * HB), BF16), vm((2, D, HB), BF16), vm((X, 8, 2 * B), F32),
        vm((X, D, 2 * B), F32), vm((X,) + block, F32), vm((X, 8, 2 * B), F32),
        vm(keys, F32), vm(keys, F32), vm((2, Y * HB, 128), F32),
        vm((X,) + block, BF16), vm((X,) + block, BF16), vm((X,) + block, BF16), vm((X,) + block, BF16),
        vm((X * C, 8, B), F32), vm((X * C, 8, B), F32),
        vm((Y,) + block, BF16), vm((Y,) + block, BF16), vm((Y,) + block, BF16), vm((Y,) + block, BF16),
        vm((Y, 8, B), F32), vm((2, Y, 8, B), F32),
        vm((X * C * Y,) + tile, F32), vm(block, BF16), vm(block, BF16), vm(block, BF16),
        vm((Z,) + tile, F32), vm((H,) + tile, F32),
        dma((2,)), dma((6,)), dma((6,)), dma((2, 3)), dma((2, 3)), dma((2, 3)), dma((2, 3)),
        dma((2, X)), dma((2, X)), dma((1,)), dma((1,)), dma((1,)), dma((1,)),
        dma((2,)), dma((2,)), dma((X,)), dma((X,)), dma((X,)), dma((X,)), dma((1,)), dma((1,)),
        dma((2, Y)), dma((2, Y)), dma((2,)), dma((2,)), dma((4,)), dma((4,)),
    ]
    big = jax.ShapeDtypeStruct((R, columns), BF16)
    dq, dk, dv, dgate = pl.pallas_call(
        functools.partial(body, X, Z, Y, R),
        out_shape=(big, big, big, jax.ShapeDtypeStruct((H, R), BF16)),
        in_specs=[any_spec] * 5 + [vm_spec] * 2,
        out_specs=(any_spec, any_spec, any_spec, vm_spec),
        scratch_shapes=scratch,
        compiler_params=pltpu.CompilerParams(
            collective_id=0, has_side_effects=True, vmem_limit_bytes=63 * 1024 * 1024
        ),
    )(*args[:5], args[5].T, args[6].T)
    return dq, dk, dv, dgate.T


def solution(mesh):
    rows = P(("ctx", "head"), None)

    def whole(*args):
        X = mesh.shape["ctx"] // (CORES * (args[0].shape[1] // WIDTH))
        return jax.shard_map(
            functools.partial(per_device, X, mesh.shape["head"]),
            mesh=mesh,
            in_specs=(rows,) * 7,
            out_specs=(rows,) * 4,
            check_vma=False,
        )(*args)

    return whole
```

```python
import functools
import math

import jax
import jax.numpy as jnp
from jax import lax
from jax.experimental import pallas as pl
from jax.experimental.pallas import tpu as pltpu
from jax.sharding import PartitionSpec as P

CORES = 2
WIDTH = 128
LOG2E = math.log2(math.e)
F32 = jnp.float32
BF16 = jnp.bfloat16
NT = (((1,), (1,)), ((), ()))
NN = (((1,), (0,)), ((), ()))


def dot(a, b, dims):
    return lax.dot_general(a, b, dims, preferred_element_type=F32)


def iota(shape, axis):
    return lax.broadcasted_iota(jnp.int32, shape, axis)


def section_of(index, size, count):
    return sum(((index >= k * size).astype(jnp.int32) for k in range(1, count)), jnp.zeros_like(index))


def section_scan(value, size, count, reverse):
    lane = iota(value.shape, 1)
    inner = lane - size * section_of(lane, size, count)
    width, shift = value.shape[1], 1
    while shift < size:
        if reverse:
            value = value + jnp.where(inner < size - shift, pltpu.roll(value, width - shift, 1), 0.0)
        else:
            value = value + jnp.where(inner >= shift, pltpu.roll(value, shift, 1), 0.0)
        shift *= 2
    return value


def row_scan(value, reverse):
    row, rows = iota(value.shape, 0), value.shape[0]

    def moved(arr, shift):
        if reverse:
            return jnp.where(row < rows - shift, pltpu.roll(arr, rows - shift, 0), 0.0)
        return jnp.where(row >= shift, pltpu.roll(arr, shift, 0), 0.0)

    value, shift = moved(value, 1), 1
    while shift < rows:
        value = value + moved(value, shift)
        shift *= 2
    return value


def lanes(value, width):
    return value[:, :width] if width <= 128 else jnp.concatenate([value] * (width // 128), axis=1)


def body(
    X, Z, Y, R,
    q_in, k_in, v_in, g_in, o_in, gate_in, lse_in,
    dq_out, dk_out, dv_out, dgate_out,
    g_loc, o_loc, gate_pad, st_q, st_k, qst_in, kst_in,
    q_all, g_all, qst_all, k_all, v_all, kst_all, kcol, kpos, tot_all, p_all,
    kt_own, kt_next, kt_far, q_row, dqt, dqt_own, row_acc, dk_acc, dv_acc, cs_acc,
    sib_snd, sib_rcv, dq_snd, dq_rcv, rs_snd, rs_rcv, dk_snd, dv_snd, dk_rcv, dv_rcv, cs_snd, cs_rcv,
    after_own, after_all, dq_fin, dk_fin, dv_fin, gs_snd, gs_rcv,
    loc_sem, p1_r, p1_s, x_r, x_s, y_r, y_s, sib_r, sib_s, qs_r, qs_s, ks_r, ks_s,
    t_r, t_s, dsib_r, dsib_s, dq_r, dq_s, rs_r, rs_s, dk_r, dk_s, cs_r, cs_s, f_r, f_s,
):
    D, H = WIDTH, Z
    half, CY = Z // 2, CORES * Y
    HB, B = half * R, Z * R
    scale = D ** -0.5
    ctx = lax.axis_index("ctx")
    y = lax.axis_index("head")
    c = ctx % CORES
    z = (ctx // CORES) % Z
    x = ctx // (CORES * Z)
    xr = X - 1 - x
    xk = jnp.where(z < half, x, xr)
    cy = c * Y + y
    mesh_id = pl.DeviceIdType.MESH

    def dev(x_, z_, c_, y_):
        return ((x_ * Z + z_) * CORES + c_, y_)

    def remote(src, dst, ssem, rsem, to):
        return pltpu.make_async_remote_copy(
            src_ref=src, dst_ref=dst, send_sem=ssem, recv_sem=rsem, device_id=to, device_id_type=mesh_id
        )

    def drain(ref, sem):
        pltpu.make_async_copy(ref, ref, sem).wait()

    def send(src, dst, ssem, rsem, to, here):
        if here is False:
            remote(src, dst, ssem, rsem, to).start()
        elif here is True:
            pltpu.make_async_copy(src, dst, rsem).start()
        else:
            @pl.when(here)
            def _():
                pltpu.make_async_copy(src, dst, rsem).start()

            @pl.when(jnp.logical_not(here))
            def _():
                remote(src, dst, ssem, rsem, to).start()

    loc = [
        pltpu.make_async_copy(g_in, g_loc, loc_sem.at[0]),
        pltpu.make_async_copy(o_in, o_loc, loc_sem.at[1]),
    ]
    for copy in loc:
        copy.start()

    barrier = pltpu.get_barrier_semaphore()
    plane = [(dx, dc, dy) for dx in range(X) for dc in range(CORES) for dy in range(Y)][1:]

    def greet(to):
        pl.semaphore_signal(barrier, inc=1, device_id=to, device_id_type=mesh_id)

    for d in range(1, Z):
        zz = (z + d) % Z
        greet(dev(x, zz, c, y))
        greet(dev(xr, zz, c, y))
    for dx, dc, dy in plane:
        greet(dev((x + dx) % X, z, (c + dc) % CORES, (y + dy) % Y))
    for copy in loc:
        copy.wait()
    st_q[...] = jnp.zeros_like(st_q)
    st_k[...] = jnp.zeros_like(st_k)
    gate_pad[...] = jnp.zeros_like(gate_pad)
    gate_float = gate_in[...].astype(F32)
    gate_pad[0:H, 0:R] = jax.nn.log_sigmoid(gate_float)
    curve = section_scan(gate_pad[...], R, 1, False)
    lse_rows = lse_in[...]
    for h in range(H):
        cut = slice(h * D, (h + 1) * D)
        product = g_loc[:, cut].astype(F32) * o_loc[:, cut].astype(F32)
        st_q[h, 0:1, 0:R] = curve[h:h + 1, 0:R] - lse_rows[h:h + 1, :]
        st_q[h, 0:1, 127:128] = curve[h:h + 1, R - 1:R]
        st_q[h, 1:2, 0:R] = jnp.sum(product.T, axis=0, keepdims=True)
        st_k[h, 0:1, 0:R] = curve[h:h + 1, 0:R]
    pl.semaphore_wait(barrier, 2 * (Z - 1) + len(plane))

    z_order = sorted(range(Z), key=lambda d: -min(d, Z - d))

    def columns(h_):
        return pl.ds(pl.multiple_of(h_ * D, D), D)

    z_half = z // half

    def z_rows(block):
        return pl.ds(pl.multiple_of(block * HB + (z % half) * R, R), R)

    def block_rows(block):
        return pl.ds(pl.multiple_of(block * HB, HB), HB)

    for d in z_order:
        zz = (z + d) % Z
        send(st_q.at[zz], qst_in.at[z], p1_s.at[4], p1_r.at[4], dev(x, zz, c, y), d == 0)
        send(
            st_k.at[zz], kst_in.at[z], p1_s.at[5], p1_r.at[5], dev(xk, zz, c, y),
            (xk == x) if d == 0 else False,
        )

    for idx, src, dst in ((0, q_in, q_all), (1, g_in, g_all), (2, k_in, k_all), (3, v_in, v_all)):
        for d in z_order:
            zz = (z + d) % Z
            if idx < 2:
                at, to, here = dst.at[x, z_half, z_rows(c), :], dev(x, zz, c, y), d == 0
            else:
                at, to = dst.at[z_half, z_rows(0), :], dev(xk, zz, c, y)
                here = (xk == x) if d == 0 else False
            send(src.at[:, columns(zz)], at, p1_s.at[idx], p1_r.at[idx], to, here)

    def q_block(ref, x_, c_):
        return ref.at[x_, :, block_rows(c_), :]

    def k_block(ref, slot):
        return ref.at[:, block_rows(slot), :]

    sibling = dev(x, z, 1 - c, y)
    queries = [functools.partial(q_block, ref, c_=c) for ref in (q_all, g_all)]
    keys = [functools.partial(k_block, ref) for ref in (k_all, v_all)]

    def x_dev(d):
        return dev((x + d) % X, z, c, y)

    def y_dev(d):
        return dev(x, z, c, (y + d) % Y)

    order = [0, 1, Y - 1, 2][:Y] if Y > 2 else [0, 1][:Y]

    def q_id(d, e):
        return (x + d) % X

    def k_id(d, e):
        return order.index((d - e) % Y)

    def ring_copy(blocks, arr, name, d, e, place, section, snd, rcv):
        src, dst = blocks[arr](name(d, 0)), blocks[arr](name(d, e))
        return remote(src, dst, snd.at[arr, section], rcv.at[arr, section], place(e))

    def ring_start(blocks, arr, name, n, place, snd, rcv):
        if n > 1:
            ring_copy(blocks, arr, name, 0, 1, place, 0, snd, rcv).start()
        if n > 2:
            ring_copy(blocks, arr, name, 0, -1, place, 1, snd, rcv).start()

    def ring_onward(blocks, arr, name, n, place, snd, rcv):
        came = -1 if arr == 0 else 1
        if n > 1:
            drain(blocks[arr](name(came, 0)), rcv.at[arr, arr if n > 2 else 0])
        if n > 2:
            ring_copy(blocks, arr, name, came, -came, place, 2, snd, rcv).start()

    def ring_other(blocks, arr, name, n, rcv):
        if n > 2:
            drain(blocks[arr](name(1 if arr == 0 else -1, 0)), rcv.at[arr, 1 - arr])

    def ring_last(blocks, arr, name, n, rcv):
        if n > 2:
            drain(blocks[arr](name(2, 0)), rcv.at[arr, 2])

    def ring_sent(blocks, arr, name, n, snd):
        block = blocks[arr](name(0, 0))
        for k in range(0 if n == 1 else 1 if n == 2 else 3):
            drain(block, snd.at[arr, k])

    def to_sibling(arr, x_):
        block = queries[arr](x_)
        remote(block, block, sib_s.at[arr, x_], sib_r.at[arr, x_], sibling).start()

    def wide(tile):
        return jnp.concatenate([tile, jnp.zeros((8, B - 128), F32)], axis=1) if B > 128 else tile[:, :B]

    in_piece_lanes = iota((8, 128), 1) < R

    def assemble(ref, at):
        total = jnp.zeros((8, B), F32)
        for s in range(Z):
            tile = jnp.where(in_piece_lanes, jnp.broadcast_to(ref[s, at:at + 1, :], (8, 128)), 0.0)
            total = total + (pltpu.roll(wide(tile), s * R, 1) if s else wide(tile))
        return total

    row_at = iota((8, 128), 0)
    drain(qst_in, p1_r.at[4])
    totals = jnp.zeros((8, 128), F32)
    for s in range(Z):
        totals = jnp.where(row_at == s, jnp.broadcast_to(qst_in[s, 0:1, 127:128], (8, 128)), totals)
    tot_all[x * CY + cy] = totals

    def spread(ref, slot, semr, sems):
        for dx, dc, dy in plane:
            to = dev((x + dx) % X, z, (c + dc) % CORES, (y + dy) % Y)
            remote(ref.at[slot], ref.at[slot], sems, semr, to).start()

    spread(tot_all, x * CY + cy, t_r.at[0], t_s.at[0])
    xc = x * CORES + c
    for at in range(2):
        qst_all[xc, at:at + 1, :] = assemble(qst_in, at)[0:1]
    q_team = [(dx, dc) for dx in range(X) for dc in range(CORES)][1:]
    for dx, dc in q_team:
        x_, c_ = (x + dx) % X, (c + dc) % CORES
        mine = qst_all.at[xc]
        remote(mine, mine, qs_s.at[0], qs_r.at[0], dev(x_, z, c_, y)).start()

    drain(kst_in, p1_r.at[5])
    kst_all[y] = assemble(kst_in, 0)[0:1]
    for dy in range(1, Y):
        mine = kst_all.at[y]
        remote(mine, mine, ks_s.at[0], ks_r.at[0], y_dev(dy)).start()
    for arr in range(2):
        drain(queries[arr](x), p1_r.at[arr])
        ring_start(queries, arr, q_id, X, x_dev, x_s, x_r)
        to_sibling(arr, x)

    dk_acc[...] = jnp.zeros_like(dk_acc)
    dv_acc[...] = jnp.zeros_like(dv_acc)
    cs_acc[...] = jnp.zeros_like(cs_acc)
    dqt[...] = jnp.zeros_like(dqt)
    row_acc[...] = jnp.zeros_like(row_acc)
    after_own[...] = jnp.zeros((8, 128), F32)
    k_at = iota((HB, 128), 0)
    k_z = section_of(k_at, R, half)
    for slot, dy in enumerate(order):
        k_y = (y + dy) % Y
        kpos[slot * HB:(slot + 1) * HB, :] = k_z * (CY * R) + c * (Y * R) + k_y * R + (k_at - R * k_z)
    q_at = iota((8, 2 * B), 1)
    q_half = (q_at >= B).astype(jnp.int32)
    q_rest = q_at - B * q_half
    q_c = section_of(q_rest, HB, CORES)
    q_rest = q_rest - HB * q_c
    q_z = section_of(q_rest, R, half)
    qpos = (q_half * half + q_z) * (CY * R) + q_c * (Y * R) + y * R + (q_rest - R * q_z)

    few = X * CY - 1
    drain(tot_all.at[pl.ds(0, few)], t_r.at[0])
    before = jnp.zeros((8, 128), F32)
    for x_ in range(X):
        level = jnp.zeros((8, 128), F32)
        for k in range(CY):
            level = level + tot_all[x_ * CY + k]
        run = before + row_scan(level, False)
        for k in range(CY):
            p_all[x_ * CY + k] = run
            run = run + tot_all[x_ * CY + k]
        before = before + jnp.sum(level, axis=0, keepdims=True)

    piece_row, piece_lane = iota((8, B), 0), iota((8, B), 1)
    in_piece = piece_row == section_of(piece_lane, R, Z)

    def along_lanes(tile):
        return jnp.sum(jnp.where(in_piece, lanes(tile, B), 0.0), axis=0, keepdims=True)

    low = iota((8, B), 1) < HB

    def halves(first, second):
        return (
            jnp.where(low, first, pltpu.roll(second, HB, 1)),
            jnp.where(low, pltpu.roll(first, HB, 1), second),
        )

    drain(qst_all.at[pl.ds(0, len(q_team))], qs_r.at[0])
    for x_ in range(X):
        rows = []
        for c_ in range(CORES):
            bias = along_lanes(p_all[x_ * CY + c_ * Y + y])
            stat = qst_all[x_ * CORES + c_]
            rows.append(jnp.where(iota((8, B), 0) == 0, (stat[0:1] + bias) * LOG2E, jnp.broadcast_to(stat[1:2], (8, B))))
        q_row[x_] = jnp.concatenate(halves(*rows), axis=1)

    if Y > 1:
        drain(kst_all.at[pl.ds(0, Y - 1)], ks_r.at[0])
    for slot, dy in enumerate(order):
        y_ = (y + dy) % Y
        tile = jnp.where(row_at < half, p_all[x * CY + c * Y + y_], p_all[xr * CY + c * Y + y_])
        column = jnp.broadcast_to((kst_all[y_] + along_lanes(tile)) * LOG2E, (8, B)).T[:, 0:1]
        spread_column = jnp.broadcast_to(column, (B, 128))
        kcol[0, slot * HB:(slot + 1) * HB, :] = spread_column[0:HB]
        kcol[1, slot * HB:(slot + 1) * HB, :] = spread_column[HB:B]

    def pair(x_, kh, rows, turned, first_lane, masked):
        count = 2 * B - first_lane
        part = slice(first_lane, 2 * B)
        if first_lane:
            q_blk, g_blk = q_all[x_, 1], g_all[x_, 1]
        else:
            q_blk, g_blk = q_all[x_].reshape(2 * B, D), g_all[x_].reshape(2 * B, D)
        row, delta = q_row[x_, 0:1, part], q_row[x_, 1:2, part]
        k_blk, v_blk = k_all[kh, rows, :], v_all[kh, rows, :]
        s = dot(k_blk, q_blk, NT)
        prob = jnp.exp2(s * (scale * LOG2E) + row - lanes(kcol[kh, rows, :], count))
        if masked:
            at = kpos[rows, :] + kh * (half * CY * R)
            prob = jnp.where(lanes(at, count) <= qpos[0:1, part], prob, 0.0)
        grad = prob * (dot(v_blk, g_blk, NT) - delta)
        prob_half, grad_half = prob.astype(BF16), grad.astype(BF16)
        dv_acc[kh, rows, :] += dot(prob_half, g_blk, NN)
        dk_acc[kh, rows, :] += dot(grad_half, q_blk, NN)
        dqt[x_, :, part] += dot(turned[kh], grad_half, NN)
        row_acc[x_, 0:1, part] += jnp.sum(grad, axis=0, keepdims=True)
        if count >= 128:
            folded = grad[:, 0:128]
            for lane in range(128, count, 128):
                folded = folded + grad[:, lane:lane + 128]
            cs_acc[kh, rows, :] += folded
        else:
            cs_acc[kh, rows, 0:count] += grad

    def key_turn(turned, rows):
        for kh in range(2):
            turned[kh] = k_all[kh, rows, :].astype(F32).T.astype(BF16)

    kt_all = (kt_own, kt_next, kt_far) if Y > 2 else (kt_own, kt_far)

    def sib_wait(x_):
        for arr in range(2):
            drain(q_block((q_all, g_all)[arr], x_, 1 - c), sib_r.at[arr, x_])

    def piece_totals(row):
        return jnp.sum(jnp.where(in_piece, jnp.broadcast_to(row, (8, B)), 0.0), axis=1, keepdims=True)

    lane_at = iota((8, 128), 1)

    def note(kind, row):
        after_own[...] = jnp.where(lane_at == kind * Z + row_at, piece_totals(row), after_own[...])

    def curve_send(slot):
        rows, dy = pl.ds(slot * HB, HB), order[slot]
        column = jnp.concatenate([cs_acc[0, rows, :], cs_acc[1, rows, :]], axis=0)
        sums = jnp.sum(column.T, axis=0, keepdims=True)
        cs_snd[slot] = sums
        note(X * CORES + (y + dy) % Y, sums)
        send(cs_snd.at[slot], cs_rcv.at[0, y], cs_s.at[0], cs_r.at[0], y_dev(dy), dy == 0)
        send(cs_snd.at[slot], cs_rcv.at[1, y], cs_s.at[1], cs_r.at[1], dev(xr, z, c, (y + dy) % Y), False)

    key_sums = ((dk_acc, dk_snd, dk_rcv, scale), (dv_acc, dv_snd, dv_rcv, 1.0))

    def key_send(slot):
        side = order.index(-order[slot] % Y) - 1
        for arr, (acc, snd, rcv, factor) in enumerate(key_sums):
            for kh in range(2):
                snd[slot, kh] = (acc[kh, slot * HB:(slot + 1) * HB, :] * factor).astype(BF16)
            remote(
                snd.at[slot], rcv.at[side], dk_s.at[arr, slot], dk_r.at[arr, side], y_dev(order[slot])
            ).start()

    def query_steps(i):
        if i == 1:
            for arr in range(2):
                ring_onward(queries, arr, q_id, X, x_dev, x_s, x_r)
                to_sibling(arr, (x + X - 1) % X if arr == 0 else (x + 1) % X)
            if X > 2:
                for arr in range(2):
                    ring_other(queries, arr, q_id, X, x_r)
                    to_sibling(arr, (x + 1) % X if arr == 0 else (x + X - 1) % X)
        if i == X - 1:
            for arr in range(2):
                ring_onward(keys, arr, k_id, Y, y_dev, y_s, y_r)
        if i == 3:
            for arr in range(2):
                ring_last(queries, arr, q_id, X, x_r)
                to_sibling(arr, (x + 2) % X)
        if i:
            sib_wait((x + x_order[i]) % X)

    def rows_done(x_):
        dq_part = dqt[x_].T * scale
        for hf in range(2):
            lower, upper = dq_part[hf * B:hf * B + HB], dq_part[hf * B + HB:hf * B + B]
            dqt_own[x_, hf] = jnp.where(c == 0, lower, upper)
            sib_snd[x_, hf] = jnp.where(c == 0, upper, lower).astype(BF16)
        remote(sib_snd.at[x_], sib_rcv.at[x_], dsib_s.at[x_], dsib_r.at[x_], sibling).start()
        tiles = halves(row_acc[x_, :, 0:B], row_acc[x_, :, B:2 * B])
        for c_ in range(CORES):
            rs_snd[x_ * CORES + c_] = tiles[c_][0:1]
            note(x_ * CORES + c_, tiles[c_][0:1])
            src, dst = rs_snd.at[x_ * CORES + c_], rs_rcv.at[xc]
            here = jnp.logical_and(x_ == x, c_ == c)
            send(src, dst, rs_s.at[0], rs_r.at[0], dev(x_, z, c_, y), here)

    def rows_home(x_):
        drain(sib_rcv.at[x_], dsib_r.at[x_])
        dq_snd[x_] = (dqt_own[x_] + sib_rcv[x_].astype(F32)).astype(BF16)
        remote(dq_snd.at[x_], dq_rcv.at[x], dq_s.at[x_], dq_r.at[x], dev(x_, z, c, y)).start()

    x_order = [0, 1, X - 1, 2][:X] if X > 2 else [0, 1][:X]
    bands = {1: [(0, 1)], 2: [(0, 1), (1, 1)], 4: [(0, 1), (1, 2), (3, 1)]}[Y]

    def pick(values, at):
        return sum(jnp.where(at == k, v, 0) for k, v in enumerate(values))

    for arr in range(2):
        drain(keys[arr](0), p1_r.at[2 + arr])
        ring_start(keys, arr, k_id, Y, y_dev, y_s, y_r)
    sib_wait(x)

    def band(first_slot, slots, turned, last, before_step):
        rows = pl.ds(first_slot * HB, slots * HB)
        key_turn(turned, rows)

        def step(i, carry):
            for k in range(1, X):
                if before_step:
                    pl.when(i == k)(functools.partial(before_step, k))
            x_ = (x + pick(x_order, X - 1 - i if last else i)) % X

            def key_half(kh, inner):
                @pl.when(x_ > jnp.where(kh == 0, x, xr))
                def _():
                    pair(x_, kh, rows, turned, 0, False)

                return inner

            lax.fori_loop(0, 2, key_half, 0)

            @pl.when(x_ == x)
            def _():
                pair(x_, 0, rows, turned, 0, True)

            @pl.when(x_ == xr)
            def _():
                pair(x_, 1, rows, turned, B, True)

            if last:
                rows_done(x_)

                @pl.when(i > 0)
                def _():
                    rows_home((x + pick(x_order, X - i)) % X)

            return carry

        lax.fori_loop(0, X, step, 0)

    for b, (first_slot, slots) in enumerate(bands):
        if b == 1:
            for arr in range(2):
                ring_other(keys, arr, k_id, Y, y_r)
        if b == 2:
            for arr in range(2):
                ring_last(keys, arr, k_id, Y, y_r)
        band(first_slot, slots, kt_all[b], b == len(bands) - 1, None if b else query_steps)
        for slot in range(first_slot, first_slot + slots):
            curve_send(slot)
        if b == len(bands) - 1:
            after_all[x * CY + cy] = jnp.sum(after_own[...], axis=0, keepdims=True)
            spread(after_all, x * CY + cy, t_r.at[1], t_s.at[1])
        if b:
            for slot in range(first_slot, first_slot + slots):
                key_send(slot)

    def give_back(fin, out, idx, keyed):
        for d in z_order:
            zz = (z + d) % Z
            src = fin.at[zz // half, pl.ds(pl.multiple_of((zz % half) * R, R), R), :]
            dst = out.at[:, columns(z)]
            at_x = jnp.where(zz < half, x, xr) if keyed else x
            here = False if d else ((at_x == x) if keyed else True)
            send(src, dst, f_s.at[idx], f_r.at[idx], dev(at_x, zz, c, y), here)

    drain(sib_rcv.at[x], dsib_r.at[x])
    dq_sum = dqt_own[x] + sib_rcv[x].astype(F32)
    for dx in range(1, X):
        x_ = (x + dx) % X
        drain(dq_rcv.at[x_], dq_r.at[x_])
        dq_sum = dq_sum + dq_rcv[x_].astype(F32)
    dq_fin[...] = dq_sum.astype(BF16)
    give_back(dq_fin, dq_out, 0, False)

    for rcv, acc, fin, out, idx, factor in (
        (dk_rcv, dk_acc, dk_fin, dk_out, 1, scale), (dv_rcv, dv_acc, dv_fin, dv_out, 2, 1.0)
    ):
        sums = [acc[kh, 0:HB, :] * factor for kh in range(2)]
        for side in range(Y - 1):
            drain(rcv.at[side], dk_r.at[idx - 1, side])
            sums = [sums[kh] + rcv[side, kh].astype(F32) for kh in range(2)]
        for kh in range(2):
            fin[kh] = sums[kh].astype(BF16)
        give_back(fin, out, idx, True)

    drain(rs_rcv, rs_r.at[0])
    drain(cs_rcv.at[0], cs_r.at[0])
    drain(cs_rcv.at[1], cs_r.at[1])
    rows_sum = jnp.zeros((1, B), F32)
    for x_ in range(X):
        for c_ in range(CORES):
            rows_sum = rows_sum + rs_rcv[x_ * CORES + c_]
    columns_sum = jnp.zeros((1, B), F32)
    for y_ in range(Y):
        columns_sum = columns_sum + jnp.where(low[0:1], cs_rcv[0, y_], cs_rcv[1, y_])
    later = section_scan(jnp.broadcast_to(rows_sum - columns_sum, (8, B)), R, Z, True)
    drain(after_all.at[pl.ds(0, few)], t_r.at[1])
    kind_at = section_of(lane_at, Z, X * CORES + Y)
    piece_at = lane_at - Z * kind_at
    of_x = section_of(kind_at, CORES, X + Y)
    turn_at = (kind_at - CORES * of_x) * Y
    later_x = own_x = own_later = jnp.zeros((8, 128), F32)
    for y_ in range(Y):
        tile = sum(after_all[(x_ * CORES + c_) * Y + y_] for x_ in range(X) for c_ in range(CORES))
        tile = jnp.where(kind_at < X * CORES, tile, 0.0)
        own = jnp.where(of_x == x, tile, 0.0)
        later_x = later_x + jnp.where(of_x > x, tile, 0.0)
        own_x = own_x + own
        own_later = own_later + jnp.where(turn_at + y_ > cy, own, 0.0)
    column_at = kind_at - X * CORES
    is_column = jnp.logical_and(column_at >= 0, column_at < Y)
    for c_ in range(CORES):
        tiles = [
            jnp.where(is_column, sum(after_all[(x_ * CORES + c_) * Y + y_] for y_ in range(Y)), 0.0)
            for x_ in range(X)
        ]
        for x_ in range(X):
            tile = jnp.where(piece_at < half, tiles[x_], tiles[X - 1 - x_])
            own = jnp.where(x_ == x, tile, 0.0)
            later_x = later_x - jnp.where(x_ > x, tile, 0.0)
            own_x = own_x - own
            own_later = own_later - jnp.where(column_at + c_ * Y > cy, own, 0.0)
    terms = later_x + jnp.where(piece_at > row_at, own_x, 0.0) + jnp.where(piece_at == row_at, own_later, 0.0)
    after = jnp.broadcast_to(jnp.sum(terms, axis=1, keepdims=True), (8, 128))
    gate_sum = later + along_lanes(after)
    for s in range(Z):
        moved = pltpu.roll(gate_sum, (B - s * R) % B, 1) if s else gate_sum
        gs_snd[s] = (moved[:, 0:128] if B >= 128 else jnp.concatenate([moved, jnp.zeros((8, 128 - B), F32)], axis=1))[0:1]
    for d in z_order:
        zz = (z + d) % Z
        send(gs_snd.at[zz], gs_rcv.at[z], f_s.at[3], f_r.at[3], dev(x, zz, c, y), d == 0)
    drain(gs_rcv, f_r.at[3])
    by_head = jnp.zeros((8, 128), F32)
    for h in range(H):
        by_head = by_head + jnp.where(row_at == h, jnp.broadcast_to(gs_rcv[h], (8, 128)), 0.0)
    dgate_out[...] = (by_head[0:H, 0:R] * jax.nn.sigmoid(-gate_float)).astype(BF16)

    for arr in range(2):
        ring_sent(queries, arr, q_id, X, x_s)
        ring_sent(keys, arr, k_id, Y, y_s)
        for x_ in range(X):
            drain(queries[arr](x_), sib_s.at[arr, x_])
        for slot in range(1, Y):
            drain(dk_snd.at[slot], dk_s.at[arr, slot])
    drain(qst_all.at[pl.ds(0, len(q_team))], qs_s.at[0])
    drain(rs_snd.at[pl.ds(0, len(q_team))], rs_s.at[0])
    if Y > 1:
        drain(kst_all.at[pl.ds(0, Y - 1)], ks_s.at[0])
        drain(cs_snd.at[pl.ds(0, Y - 1)], cs_s.at[0])
    drain(cs_snd, cs_s.at[1])
    drain(tot_all.at[pl.ds(0, few)], t_s.at[0])
    drain(after_all.at[pl.ds(0, few)], t_s.at[1])
    for dx in range(X):
        x_ = (x + dx) % X
        drain(sib_snd.at[x_], dsib_s.at[x_])
        if dx:
            drain(dq_snd.at[x_], dq_s.at[x_])

    for idx in range(4):
        less, more = q_in.at[:, pl.ds(0, (Z - 1) * D)], q_in
        if idx < 2:
            drain(less, p1_s.at[idx])
        else:
            @pl.when(xk == x)
            def _(idx=idx, less=less):
                drain(less, p1_s.at[idx])

            @pl.when(xk != x)
            def _(idx=idx, more=more):
                drain(more, p1_s.at[idx])
    drain(qst_in.at[pl.ds(0, Z - 1)], p1_s.at[4])
    drain(gs_snd.at[pl.ds(0, Z - 1)], f_s.at[3])

    @pl.when(xk == x)
    def _():
        drain(kst_in.at[pl.ds(0, Z - 1)], p1_s.at[5])
        drain(q_in.at[:, pl.ds(0, (Z - 1) * D)], f_s.at[1])
        drain(q_in.at[:, pl.ds(0, (Z - 1) * D)], f_s.at[2])

    @pl.when(xk != x)
    def _():
        drain(kst_in, p1_s.at[5])
        drain(q_in, f_s.at[1])
        drain(q_in, f_s.at[2])

    drain(q_in.at[:, pl.ds(0, (Z - 1) * D)], f_s.at[0])
    drain(dq_out, f_r.at[0])
    drain(dk_out, f_r.at[1])
    drain(dv_out, f_r.at[2])


def per_device(X, Y, *args):
    R, columns = args[0].shape
    D, Z, C = WIDTH, columns // WIDTH, CORES
    HB, B, H = Z // 2 * R, Z * R, Z
    vm = pltpu.VMEM
    dma = pltpu.SemaphoreType.DMA
    any_spec = pl.BlockSpec(memory_space=pl.ANY)
    vm_spec = pl.BlockSpec(memory_space=pltpu.VMEM)
    queries, keys = (X, 2, C * HB, D), (2, Y * HB, D)
    block, tile = (2, HB, D), (8, 128)
    scratch = [
        vm((R, columns), BF16), vm((R, columns), BF16), vm(tile, F32),
        vm((H, 2, 128), F32), vm((H, 1, 128), F32), vm((Z, 2, 128), F32), vm((Z, 1, 128), F32),
        vm(queries, BF16), vm(queries, BF16), vm((X * C, 2, B), F32),
        vm(keys, BF16), vm(keys, BF16), vm((Y, 1, B), F32),
        vm((2, Y * HB, 128), F32), vm((Y * HB, 128), jnp.int32),
        vm((X * C * Y,) + tile, F32), vm((X * C * Y,) + tile, F32),
        vm((2, D, HB), BF16), vm((2, D, 2 * HB), BF16), vm((2, D, HB), BF16), vm((X, 8, 2 * B), F32),
        vm((X, D, 2 * B), F32), vm((X,) + block, F32), vm((X, 8, 2 * B), F32),
        vm(keys, F32), vm(keys, F32), vm((2, Y * HB, 128), F32),
        vm((X,) + block, BF16), vm((X,) + block, BF16), vm((X,) + block, BF16), vm((X,) + block, BF16),
        vm((X * C, 1, B), F32), vm((X * C, 1, B), F32),
        vm((Y,) + block, BF16), vm((Y,) + block, BF16), vm((Y,) + block, BF16), vm((Y,) + block, BF16),
        vm((Y, 1, B), F32), vm((2, Y, 1, B), F32),
        vm(tile, F32), vm((X * C * Y, 1, 128), F32), vm(block, BF16), vm(block, BF16), vm(block, BF16),
        vm((Z, 1, 128), F32), vm((H, 1, 128), F32),
        dma((2,)), dma((6,)), dma((6,)), dma((2, 3)), dma((2, 3)), dma((2, 3)), dma((2, 3)),
        dma((2, X)), dma((2, X)), dma((1,)), dma((1,)), dma((1,)), dma((1,)),
        dma((2,)), dma((2,)), dma((X,)), dma((X,)), dma((X,)), dma((X,)), dma((1,)), dma((1,)),
        dma((2, Y)), dma((2, Y)), dma((2,)), dma((2,)), dma((4,)), dma((4,)),
    ]
    big = jax.ShapeDtypeStruct((R, columns), BF16)
    dq, dk, dv, dgate = pl.pallas_call(
        functools.partial(body, X, Z, Y, R),
        out_shape=(big, big, big, jax.ShapeDtypeStruct((H, R), BF16)),
        in_specs=[any_spec] * 5 + [vm_spec] * 2,
        out_specs=(any_spec, any_spec, any_spec, vm_spec),
        scratch_shapes=scratch,
        compiler_params=pltpu.CompilerParams(
            collective_id=0, has_side_effects=True, vmem_limit_bytes=63 * 1024 * 1024
        ),
    )(*args[:5], args[5].T, args[6].T)
    return dq, dk, dv, dgate.T


def solution(mesh):
    rows = P(("ctx", "head"), None)

    def whole(*args):
        X = mesh.shape["ctx"] // (CORES * (args[0].shape[1] // WIDTH))
        return jax.shard_map(
            functools.partial(per_device, X, mesh.shape["head"]),
            mesh=mesh,
            in_specs=(rows,) * 7,
            out_specs=(rows,) * 4,
            check_vma=False,
        )(*args)

    return whole
```

```python
import functools
import math

import jax
import jax.numpy as jnp
from jax import lax
from jax.experimental import pallas as pl
from jax.experimental.pallas import tpu as pltpu
from jax.sharding import PartitionSpec as P

CORES = 2
WIDTH = 128
LOG2E = math.log2(math.e)
F32 = jnp.float32
BF16 = jnp.bfloat16
NT = (((1,), (1,)), ((), ()))
NN = (((1,), (0,)), ((), ()))


def dot(a, b, dims):
    return lax.dot_general(a, b, dims, preferred_element_type=F32)


def iota(shape, axis):
    return lax.broadcasted_iota(jnp.int32, shape, axis)


def section_of(index, size, count):
    return sum(((index >= k * size).astype(jnp.int32) for k in range(1, count)), jnp.zeros_like(index))


def section_scan(value, size, count, reverse):
    lane = iota(value.shape, 1)
    inner = lane - size * section_of(lane, size, count)
    width, shift = value.shape[1], 1
    while shift < size:
        if reverse:
            value = value + jnp.where(inner < size - shift, pltpu.roll(value, width - shift, 1), 0.0)
        else:
            value = value + jnp.where(inner >= shift, pltpu.roll(value, shift, 1), 0.0)
        shift *= 2
    return value


def row_scan(value, reverse):
    row, rows = iota(value.shape, 0), value.shape[0]

    def moved(arr, shift):
        if reverse:
            return jnp.where(row < rows - shift, pltpu.roll(arr, rows - shift, 0), 0.0)
        return jnp.where(row >= shift, pltpu.roll(arr, shift, 0), 0.0)

    value, shift = moved(value, 1), 1
    while shift < rows:
        value = value + moved(value, shift)
        shift *= 2
    return value


def lanes(value, width):
    return value[:, :width] if width <= 128 else jnp.concatenate([value] * (width // 128), axis=1)


def body(
    X, Z, Y, R,
    q_in, k_in, v_in, g_in, o_in, gate_in, lse_in,
    dq_out, dk_out, dv_out, dgate_out,
    g_loc, o_loc, gate_loc, lse_loc, gate_pad, st_q, st_k, qst_in, kst_in,
    q_all, g_all, qst_all, k_all, v_all, kst_all, kcol, kpos, tot_all, p_all,
    kt_own, kt_next, kt_far, q_row, dqt, dqt_own, row_acc, dk_acc, dv_acc, cs_acc,
    sib_snd, sib_rcv, dq_snd, dq_rcv, rs_snd, rs_rcv, dk_snd, dv_snd, dk_rcv, dv_rcv, cs_snd, cs_rcv,
    after_own, after_all, dq_fin, dk_fin, dv_fin, gs_snd, gs_rcv,
    loc_sem, p1_r, p1_s, x_r, x_s, y_r, y_s, sib_r, sib_s, qs_r, qs_s, ks_r, ks_s,
    t_r, t_s, dsib_r, dsib_s, dq_r, dq_s, rs_r, rs_s, dk_r, dk_s, cs_r, cs_s, f_r, f_s,
):
    D, H = WIDTH, Z
    half, CY = Z // 2, CORES * Y
    HB, B = half * R, Z * R
    scale = D ** -0.5
    ctx = lax.axis_index("ctx")
    y = lax.axis_index("head")
    c = ctx % CORES
    z = (ctx // CORES) % Z
    x = ctx // (CORES * Z)
    xr = X - 1 - x
    xk = jnp.where(z < half, x, xr)
    cy = c * Y + y
    mesh_id = pl.DeviceIdType.MESH

    def dev(x_, z_, c_, y_):
        return ((x_ * Z + z_) * CORES + c_, y_)

    def remote(src, dst, ssem, rsem, to):
        return pltpu.make_async_remote_copy(
            src_ref=src, dst_ref=dst, send_sem=ssem, recv_sem=rsem, device_id=to, device_id_type=mesh_id
        )

    def drain(ref, sem):
        pltpu.make_async_copy(ref, ref, sem).wait()

    def send(src, dst, ssem, rsem, to, here):
        if here is False:
            remote(src, dst, ssem, rsem, to).start()
        elif here is True:
            pltpu.make_async_copy(src, dst, rsem).start()
        else:
            @pl.when(here)
            def _():
                pltpu.make_async_copy(src, dst, rsem).start()

            @pl.when(jnp.logical_not(here))
            def _():
                remote(src, dst, ssem, rsem, to).start()

    loc = [
        pltpu.make_async_copy(g_in, g_loc, loc_sem.at[0]),
        pltpu.make_async_copy(o_in, o_loc, loc_sem.at[1]),
        pltpu.make_async_copy(gate_in, gate_loc, loc_sem.at[2]),
        pltpu.make_async_copy(lse_in, lse_loc, loc_sem.at[3]),
    ]
    for copy in loc:
        copy.start()

    barrier = pltpu.get_barrier_semaphore()
    plane = [(dx, dc, dy) for dx in range(X) for dc in range(CORES) for dy in range(Y)][1:]

    def greet(to):
        pl.semaphore_signal(barrier, inc=1, device_id=to, device_id_type=mesh_id)

    for d in range(1, Z):
        zz = (z + d) % Z
        greet(dev(x, zz, c, y))
        greet(dev(xr, zz, c, y))
    for dx, dc, dy in plane:
        greet(dev((x + dx) % X, z, (c + dc) % CORES, (y + dy) % Y))
    for copy in loc:
        copy.wait()
    st_q[...] = jnp.zeros_like(st_q)
    st_k[...] = jnp.zeros_like(st_k)
    gate_pad[...] = jnp.zeros_like(gate_pad)
    gate_float = gate_loc[...].astype(F32)
    gate_pad[0:H, 0:R] = jax.nn.log_sigmoid(gate_float)
    curve = section_scan(gate_pad[...], R, 1, False)
    lse_rows = lse_loc[...]
    for h in range(H):
        cut = slice(h * D, (h + 1) * D)
        product = g_loc[:, cut].astype(F32) * o_loc[:, cut].astype(F32)
        st_q[h, 0:1, 0:R] = curve[h:h + 1, 0:R] - lse_rows[h:h + 1, :]
        st_q[h, 0:1, 127:128] = curve[h:h + 1, R - 1:R]
        st_q[h, 1:2, 0:R] = jnp.sum(product.T, axis=0, keepdims=True)
        st_k[h, 0:1, 0:R] = curve[h:h + 1, 0:R]
    pl.semaphore_wait(barrier, 2 * (Z - 1) + len(plane))

    z_order = sorted(range(Z), key=lambda d: -min(d, Z - d))

    def columns(h_):
        return pl.ds(pl.multiple_of(h_ * D, D), D)

    z_half = z // half

    def z_rows(block):
        return pl.ds(pl.multiple_of(block * HB + (z % half) * R, R), R)

    def block_rows(block):
        return pl.ds(pl.multiple_of(block * HB, HB), HB)

    for d in z_order:
        zz = (z + d) % Z
        send(st_q.at[zz], qst_in.at[z], p1_s.at[4], p1_r.at[4], dev(x, zz, c, y), d == 0)
        send(
            st_k.at[zz], kst_in.at[z], p1_s.at[5], p1_r.at[5], dev(xk, zz, c, y),
            (xk == x) if d == 0 else False,
        )

    for idx, src, dst in ((0, q_in, q_all), (1, g_in, g_all), (2, k_in, k_all), (3, v_in, v_all)):
        for d in z_order:
            zz = (z + d) % Z
            if idx < 2:
                at, to, here = dst.at[x, z_half, z_rows(c), :], dev(x, zz, c, y), d == 0
            else:
                at, to = dst.at[z_half, z_rows(0), :], dev(xk, zz, c, y)
                here = (xk == x) if d == 0 else False
            send(src.at[:, columns(zz)], at, p1_s.at[idx], p1_r.at[idx], to, here)

    def q_block(ref, x_, c_):
        return ref.at[x_, :, block_rows(c_), :]

    def k_block(ref, slot):
        return ref.at[:, block_rows(slot), :]

    sibling = dev(x, z, 1 - c, y)
    queries = [functools.partial(q_block, ref, c_=c) for ref in (q_all, g_all)]
    keys = [functools.partial(k_block, ref) for ref in (k_all, v_all)]

    def x_dev(d):
        return dev((x + d) % X, z, c, y)

    def y_dev(d):
        return dev(x, z, c, (y + d) % Y)

    order = [0, 1, Y - 1, 2][:Y] if Y > 2 else [0, 1][:Y]

    def q_id(d, e):
        return (x + d) % X

    def k_id(d, e):
        return order.index((d - e) % Y)

    def ring_copy(blocks, arr, name, d, e, place, section, snd, rcv):
        src, dst = blocks[arr](name(d, 0)), blocks[arr](name(d, e))
        return remote(src, dst, snd.at[arr, section], rcv.at[arr, section], place(e))

    def ring_start(blocks, arr, name, n, place, snd, rcv):
        if n > 1:
            ring_copy(blocks, arr, name, 0, 1, place, 0, snd, rcv).start()
        if n > 2:
            ring_copy(blocks, arr, name, 0, -1, place, 1, snd, rcv).start()

    def ring_onward(blocks, arr, name, n, place, snd, rcv):
        came = -1 if arr == 0 else 1
        if n > 1:
            drain(blocks[arr](name(came, 0)), rcv.at[arr, arr if n > 2 else 0])
        if n > 2:
            ring_copy(blocks, arr, name, came, -came, place, 2, snd, rcv).start()

    def ring_other(blocks, arr, name, n, rcv):
        if n > 2:
            drain(blocks[arr](name(1 if arr == 0 else -1, 0)), rcv.at[arr, 1 - arr])

    def ring_last(blocks, arr, name, n, rcv):
        if n > 2:
            drain(blocks[arr](name(2, 0)), rcv.at[arr, 2])

    def ring_sent(blocks, arr, name, n, snd):
        block = blocks[arr](name(0, 0))
        for k in range(0 if n == 1 else 1 if n == 2 else 3):
            drain(block, snd.at[arr, k])

    def to_sibling(arr, x_):
        block = queries[arr](x_)
        remote(block, block, sib_s.at[arr, x_], sib_r.at[arr, x_], sibling).start()

    def wide(tile):
        return jnp.concatenate([tile, jnp.zeros((8, B - 128), F32)], axis=1) if B > 128 else tile[:, :B]

    in_piece_lanes = iota((8, 128), 1) < R

    def assemble(ref, at):
        total = jnp.zeros((8, B), F32)
        for s in range(Z):
            tile = jnp.where(in_piece_lanes, jnp.broadcast_to(ref[s, at:at + 1, :], (8, 128)), 0.0)
            total = total + (pltpu.roll(wide(tile), s * R, 1) if s else wide(tile))
        return total

    row_at = iota((8, 128), 0)
    drain(qst_in, p1_r.at[4])
    totals = jnp.zeros((8, 128), F32)
    for s in range(Z):
        totals = jnp.where(row_at == s, jnp.broadcast_to(qst_in[s, 0:1, 127:128], (8, 128)), totals)
    tot_all[x * CY + cy] = totals

    def spread(ref, slot, semr, sems):
        for dx, dc, dy in plane:
            to = dev((x + dx) % X, z, (c + dc) % CORES, (y + dy) % Y)
            remote(ref.at[slot], ref.at[slot], sems, semr, to).start()

    spread(tot_all, x * CY + cy, t_r.at[0], t_s.at[0])
    xc = x * CORES + c
    for at in range(2):
        qst_all[xc, at:at + 1, :] = assemble(qst_in, at)[0:1]
    q_team = [(dx, dc) for dx in range(X) for dc in range(CORES)][1:]
    for dx, dc in q_team:
        x_, c_ = (x + dx) % X, (c + dc) % CORES
        mine = qst_all.at[xc]
        remote(mine, mine, qs_s.at[0], qs_r.at[0], dev(x_, z, c_, y)).start()

    drain(kst_in, p1_r.at[5])
    kst_all[y] = assemble(kst_in, 0)[0:1]
    for dy in range(1, Y):
        mine = kst_all.at[y]
        remote(mine, mine, ks_s.at[0], ks_r.at[0], y_dev(dy)).start()
    for arr in range(2):
        drain(queries[arr](x), p1_r.at[arr])
        ring_start(queries, arr, q_id, X, x_dev, x_s, x_r)
        to_sibling(arr, x)

    dk_acc[...] = jnp.zeros_like(dk_acc)
    dv_acc[...] = jnp.zeros_like(dv_acc)
    cs_acc[...] = jnp.zeros_like(cs_acc)
    dqt[...] = jnp.zeros_like(dqt)
    row_acc[...] = jnp.zeros_like(row_acc)
    after_own[...] = jnp.zeros((8, 128), F32)
    k_at = iota((HB, 128), 0)
    k_z = section_of(k_at, R, half)
    for slot, dy in enumerate(order):
        k_y = (y + dy) % Y
        kpos[slot * HB:(slot + 1) * HB, :] = k_z * (CY * R) + c * (Y * R) + k_y * R + (k_at - R * k_z)
    q_at = iota((8, 2 * B), 1)
    q_half = (q_at >= B).astype(jnp.int32)
    q_rest = q_at - B * q_half
    q_c = section_of(q_rest, HB, CORES)
    q_rest = q_rest - HB * q_c
    q_z = section_of(q_rest, R, half)
    qpos = (q_half * half + q_z) * (CY * R) + q_c * (Y * R) + y * R + (q_rest - R * q_z)

    few = X * CY - 1
    drain(tot_all.at[pl.ds(0, few)], t_r.at[0])
    before = jnp.zeros((8, 128), F32)
    for x_ in range(X):
        level = jnp.zeros((8, 128), F32)
        for k in range(CY):
            level = level + tot_all[x_ * CY + k]
        run = before + row_scan(level, False)
        for k in range(CY):
            p_all[x_ * CY + k] = run
            run = run + tot_all[x_ * CY + k]
        before = before + jnp.sum(level, axis=0, keepdims=True)

    piece_row, piece_lane = iota((8, B), 0), iota((8, B), 1)
    in_piece = piece_row == section_of(piece_lane, R, Z)

    def along_lanes(tile):
        return jnp.sum(jnp.where(in_piece, lanes(tile, B), 0.0), axis=0, keepdims=True)

    low = iota((8, B), 1) < HB

    def halves(first, second):
        return (
            jnp.where(low, first, pltpu.roll(second, HB, 1)),
            jnp.where(low, pltpu.roll(first, HB, 1), second),
        )

    drain(qst_all.at[pl.ds(0, len(q_team))], qs_r.at[0])
    for x_ in range(X):
        rows = []
        for c_ in range(CORES):
            bias = along_lanes(p_all[x_ * CY + c_ * Y + y])
            stat = qst_all[x_ * CORES + c_]
            rows.append(jnp.where(iota((8, B), 0) == 0, (stat[0:1] + bias) * LOG2E, jnp.broadcast_to(stat[1:2], (8, B))))
        q_row[x_] = jnp.concatenate(halves(*rows), axis=1)

    if Y > 1:
        drain(kst_all.at[pl.ds(0, Y - 1)], ks_r.at[0])
    for slot, dy in enumerate(order):
        y_ = (y + dy) % Y
        tile = jnp.where(row_at < half, p_all[x * CY + c * Y + y_], p_all[xr * CY + c * Y + y_])
        column = jnp.broadcast_to((kst_all[y_] + along_lanes(tile)) * LOG2E, (8, B)).T[:, 0:1]
        spread_column = jnp.broadcast_to(column, (B, 128))
        kcol[0, slot * HB:(slot + 1) * HB, :] = spread_column[0:HB]
        kcol[1, slot * HB:(slot + 1) * HB, :] = spread_column[HB:B]

    def pair(x_, kh, rows, turned, first_lane, masked):
        count = 2 * B - first_lane
        part = slice(first_lane, 2 * B)
        if first_lane:
            q_blk, g_blk = q_all[x_, 1], g_all[x_, 1]
        else:
            q_blk, g_blk = q_all[x_].reshape(2 * B, D), g_all[x_].reshape(2 * B, D)
        row, delta = q_row[x_, 0:1, part], q_row[x_, 1:2, part]
        k_blk, v_blk = k_all[kh, rows, :], v_all[kh, rows, :]
        s = dot(k_blk, q_blk, NT)
        prob = jnp.exp2(s * (scale * LOG2E) + row - lanes(kcol[kh, rows, :], count))
        if masked:
            at = kpos[rows, :] + kh * (half * CY * R)
            prob = jnp.where(lanes(at, count) <= qpos[0:1, part], prob, 0.0)
        grad = prob * (dot(v_blk, g_blk, NT) - delta)
        prob_half, grad_half = prob.astype(BF16), grad.astype(BF16)
        dv_acc[kh, rows, :] += dot(prob_half, g_blk, NN)
        dk_acc[kh, rows, :] += dot(grad_half, q_blk, NN)
        dqt[x_, :, part] += dot(turned[kh], grad_half, NN)
        row_acc[x_, 0:1, part] += jnp.sum(grad, axis=0, keepdims=True)
        if count >= 128:
            folded = grad[:, 0:128]
            for lane in range(128, count, 128):
                folded = folded + grad[:, lane:lane + 128]
            cs_acc[kh, rows, :] += folded
        else:
            cs_acc[kh, rows, 0:count] += grad

    def key_turn(turned, rows):
        for kh in range(2):
            turned[kh] = k_all[kh, rows, :].astype(F32).T.astype(BF16)

    kt_all = (kt_own, kt_next, kt_far) if Y > 2 else (kt_own, kt_far)

    def sib_wait(x_):
        for arr in range(2):
            drain(q_block((q_all, g_all)[arr], x_, 1 - c), sib_r.at[arr, x_])

    def piece_totals(row):
        return jnp.sum(jnp.where(in_piece, jnp.broadcast_to(row, (8, B)), 0.0), axis=1, keepdims=True)

    lane_at = iota((8, 128), 1)

    def note(kind, row):
        after_own[...] = jnp.where(lane_at == kind * Z + row_at, piece_totals(row), after_own[...])

    def curve_send(slot):
        rows, dy = pl.ds(slot * HB, HB), order[slot]
        column = jnp.concatenate([cs_acc[0, rows, :], cs_acc[1, rows, :]], axis=0)
        sums = jnp.sum(column.T, axis=0, keepdims=True)
        cs_snd[slot] = sums
        note(X * CORES + (y + dy) % Y, sums)
        send(cs_snd.at[slot], cs_rcv.at[0, y], cs_s.at[0], cs_r.at[0], y_dev(dy), dy == 0)
        send(cs_snd.at[slot], cs_rcv.at[1, y], cs_s.at[1], cs_r.at[1], dev(xr, z, c, (y + dy) % Y), False)

    key_sums = ((dk_acc, dk_snd, dk_rcv, scale), (dv_acc, dv_snd, dv_rcv, 1.0))

    def key_send(slot):
        side = order.index(-order[slot] % Y) - 1
        for arr, (acc, snd, rcv, factor) in enumerate(key_sums):
            for kh in range(2):
                snd[slot, kh] = (acc[kh, slot * HB:(slot + 1) * HB, :] * factor).astype(BF16)
            remote(
                snd.at[slot], rcv.at[side], dk_s.at[arr, slot], dk_r.at[arr, side], y_dev(order[slot])
            ).start()

    def query_steps(i):
        if i == 1:
            for arr in range(2):
                ring_onward(queries, arr, q_id, X, x_dev, x_s, x_r)
                to_sibling(arr, (x + X - 1) % X if arr == 0 else (x + 1) % X)
            if X > 2:
                for arr in range(2):
                    ring_other(queries, arr, q_id, X, x_r)
                    to_sibling(arr, (x + 1) % X if arr == 0 else (x + X - 1) % X)
        if i == X - 1:
            for arr in range(2):
                ring_onward(keys, arr, k_id, Y, y_dev, y_s, y_r)
        if i == 3:
            for arr in range(2):
                ring_last(queries, arr, q_id, X, x_r)
                to_sibling(arr, (x + 2) % X)
        if i:
            sib_wait((x + x_order[i]) % X)

    def rows_done(x_):
        dq_part = dqt[x_].T * scale
        for hf in range(2):
            lower, upper = dq_part[hf * B:hf * B + HB], dq_part[hf * B + HB:hf * B + B]
            dqt_own[x_, hf] = jnp.where(c == 0, lower, upper)
            sib_snd[x_, hf] = jnp.where(c == 0, upper, lower).astype(BF16)
        remote(sib_snd.at[x_], sib_rcv.at[x_], dsib_s.at[x_], dsib_r.at[x_], sibling).start()

    def rows_curve(x_):
        tiles = halves(row_acc[x_, :, 0:B], row_acc[x_, :, B:2 * B])
        for c_ in range(CORES):
            rs_snd[x_ * CORES + c_] = tiles[c_][0:1]
            note(x_ * CORES + c_, tiles[c_][0:1])
            src, dst = rs_snd.at[x_ * CORES + c_], rs_rcv.at[xc]
            here = jnp.logical_and(x_ == x, c_ == c)
            send(src, dst, rs_s.at[0], rs_r.at[0], dev(x_, z, c_, y), here)

    def rows_home(x_):
        drain(sib_rcv.at[x_], dsib_r.at[x_])
        dq_snd[x_] = (dqt_own[x_] + sib_rcv[x_].astype(F32)).astype(BF16)
        remote(dq_snd.at[x_], dq_rcv.at[x], dq_s.at[x_], dq_r.at[x], dev(x_, z, c, y)).start()

    x_order = [0, 1, X - 1, 2][:X] if X > 2 else [0, 1][:X]
    bands = {1: [(0, 1)], 2: [(0, 1), (1, 1)], 4: [(0, 1), (1, 2), (3, 1)]}[Y]

    def pick(values, at):
        return sum(jnp.where(at == k, v, 0) for k, v in enumerate(values))

    for arr in range(2):
        drain(keys[arr](0), p1_r.at[2 + arr])
        ring_start(keys, arr, k_id, Y, y_dev, y_s, y_r)
    sib_wait(x)

    def band(first_slot, slots, turned, last, before_step):
        rows = pl.ds(first_slot * HB, slots * HB)
        key_turn(turned, rows)

        def step(i, carry):
            for k in range(1, X):
                if before_step:
                    pl.when(i == k)(functools.partial(before_step, k))
            x_ = (x + pick(x_order, X - 1 - i if last else i)) % X

            def key_half(kh, inner):
                @pl.when(x_ > jnp.where(kh == 0, x, xr))
                def _():
                    pair(x_, kh, rows, turned, 0, False)

                return inner

            lax.fori_loop(0, 2, key_half, 0)

            @pl.when(x_ == x)
            def _():
                pair(x_, 0, rows, turned, 0, True)

            @pl.when(x_ == xr)
            def _():
                pair(x_, 1, rows, turned, B, True)

            if last:
                rows_done(x_)

                @pl.when(i > 0)
                def _():
                    rows_home((x + pick(x_order, X - i)) % X)

            return carry

        lax.fori_loop(0, X, step, 0)

    for b, (first_slot, slots) in enumerate(bands):
        if b == 1:
            for arr in range(2):
                ring_other(keys, arr, k_id, Y, y_r)
        if b == 2:
            for arr in range(2):
                ring_last(keys, arr, k_id, Y, y_r)
        band(first_slot, slots, kt_all[b], b == len(bands) - 1, None if b else query_steps)
        if b:
            for slot in range(first_slot, first_slot + slots):
                key_send(slot)

    for x_ in range(X):
        rows_curve(x_)
    for slot in range(Y):
        curve_send(slot)
    after_all[x * CY + cy] = jnp.sum(after_own[...], axis=0, keepdims=True)
    spread(after_all, x * CY + cy, t_r.at[1], t_s.at[1])

    def give_back(fin, out, idx, keyed):
        for d in z_order:
            zz = (z + d) % Z
            src = fin.at[zz // half, pl.ds(pl.multiple_of((zz % half) * R, R), R), :]
            dst = out.at[:, columns(z)]
            at_x = jnp.where(zz < half, x, xr) if keyed else x
            here = False if d else ((at_x == x) if keyed else True)
            send(src, dst, f_s.at[idx], f_r.at[idx], dev(at_x, zz, c, y), here)

    drain(sib_rcv.at[x], dsib_r.at[x])
    dq_sum = dqt_own[x] + sib_rcv[x].astype(F32)
    for dx in range(1, X):
        x_ = (x + dx) % X
        drain(dq_rcv.at[x_], dq_r.at[x_])
        dq_sum = dq_sum + dq_rcv[x_].astype(F32)
    dq_fin[...] = dq_sum.astype(BF16)
    give_back(dq_fin, dq_out, 0, False)

    for rcv, acc, fin, out, idx, factor in (
        (dk_rcv, dk_acc, dk_fin, dk_out, 1, scale), (dv_rcv, dv_acc, dv_fin, dv_out, 2, 1.0)
    ):
        sums = [acc[kh, 0:HB, :] * factor for kh in range(2)]
        for side in range(Y - 1):
            drain(rcv.at[side], dk_r.at[idx - 1, side])
            sums = [sums[kh] + rcv[side, kh].astype(F32) for kh in range(2)]
        for kh in range(2):
            fin[kh] = sums[kh].astype(BF16)
        give_back(fin, out, idx, True)

    drain(rs_rcv, rs_r.at[0])
    drain(cs_rcv.at[0], cs_r.at[0])
    drain(cs_rcv.at[1], cs_r.at[1])
    rows_sum = jnp.zeros((1, B), F32)
    for x_ in range(X):
        for c_ in range(CORES):
            rows_sum = rows_sum + rs_rcv[x_ * CORES + c_]
    columns_sum = jnp.zeros((1, B), F32)
    for y_ in range(Y):
        columns_sum = columns_sum + jnp.where(low[0:1], cs_rcv[0, y_], cs_rcv[1, y_])
    later = section_scan(jnp.broadcast_to(rows_sum - columns_sum, (8, B)), R, Z, True)
    drain(after_all.at[pl.ds(0, few)], t_r.at[1])
    kind_at = section_of(lane_at, Z, X * CORES + Y)
    piece_at = lane_at - Z * kind_at
    of_x = section_of(kind_at, CORES, X + Y)
    turn_at = (kind_at - CORES * of_x) * Y
    later_x = own_x = own_later = jnp.zeros((8, 128), F32)
    for y_ in range(Y):
        tile = sum(after_all[(x_ * CORES + c_) * Y + y_] for x_ in range(X) for c_ in range(CORES))
        tile = jnp.where(kind_at < X * CORES, tile, 0.0)
        own = jnp.where(of_x == x, tile, 0.0)
        later_x = later_x + jnp.where(of_x > x, tile, 0.0)
        own_x = own_x + own
        own_later = own_later + jnp.where(turn_at + y_ > cy, own, 0.0)
    column_at = kind_at - X * CORES
    is_column = jnp.logical_and(column_at >= 0, column_at < Y)
    for c_ in range(CORES):
        tiles = [
            jnp.where(is_column, sum(after_all[(x_ * CORES + c_) * Y + y_] for y_ in range(Y)), 0.0)
            for x_ in range(X)
        ]
        for x_ in range(X):
            tile = jnp.where(piece_at < half, tiles[x_], tiles[X - 1 - x_])
            own = jnp.where(x_ == x, tile, 0.0)
            later_x = later_x - jnp.where(x_ > x, tile, 0.0)
            own_x = own_x - own
            own_later = own_later - jnp.where(column_at + c_ * Y > cy, own, 0.0)
    terms = later_x + jnp.where(piece_at > row_at, own_x, 0.0) + jnp.where(piece_at == row_at, own_later, 0.0)
    after = jnp.broadcast_to(jnp.sum(terms, axis=1, keepdims=True), (8, 128))
    gate_sum = later + along_lanes(after)
    for s in range(Z):
        moved = pltpu.roll(gate_sum, (B - s * R) % B, 1) if s else gate_sum
        gs_snd[s] = (moved[:, 0:128] if B >= 128 else jnp.concatenate([moved, jnp.zeros((8, 128 - B), F32)], axis=1))[0:1]
    for d in z_order:
        zz = (z + d) % Z
        send(gs_snd.at[zz], gs_rcv.at[z], f_s.at[3], f_r.at[3], dev(x, zz, c, y), d == 0)
    drain(gs_rcv, f_r.at[3])
    by_head = jnp.zeros((8, 128), F32)
    for h in range(H):
        by_head = by_head + jnp.where(row_at == h, jnp.broadcast_to(gs_rcv[h], (8, 128)), 0.0)
    dgate_out[...] = (by_head[0:H, 0:R] * jax.nn.sigmoid(-gate_float)).astype(BF16)

    for arr in range(2):
        ring_sent(queries, arr, q_id, X, x_s)
        ring_sent(keys, arr, k_id, Y, y_s)
        for x_ in range(X):
            drain(queries[arr](x_), sib_s.at[arr, x_])
        for slot in range(1, Y):
            drain(dk_snd.at[slot], dk_s.at[arr, slot])
    drain(qst_all.at[pl.ds(0, len(q_team))], qs_s.at[0])
    drain(rs_snd.at[pl.ds(0, len(q_team))], rs_s.at[0])
    if Y > 1:
        drain(kst_all.at[pl.ds(0, Y - 1)], ks_s.at[0])
        drain(cs_snd.at[pl.ds(0, Y - 1)], cs_s.at[0])
    drain(cs_snd, cs_s.at[1])
    drain(tot_all.at[pl.ds(0, few)], t_s.at[0])
    drain(after_all.at[pl.ds(0, few)], t_s.at[1])
    for dx in range(X):
        x_ = (x + dx) % X
        drain(sib_snd.at[x_], dsib_s.at[x_])
        if dx:
            drain(dq_snd.at[x_], dq_s.at[x_])

    for idx in range(4):
        less, more = q_in.at[:, pl.ds(0, (Z - 1) * D)], q_in
        if idx < 2:
            drain(less, p1_s.at[idx])
        else:
            @pl.when(xk == x)
            def _(idx=idx, less=less):
                drain(less, p1_s.at[idx])

            @pl.when(xk != x)
            def _(idx=idx, more=more):
                drain(more, p1_s.at[idx])
    drain(qst_in.at[pl.ds(0, Z - 1)], p1_s.at[4])
    drain(gs_snd.at[pl.ds(0, Z - 1)], f_s.at[3])

    @pl.when(xk == x)
    def _():
        drain(kst_in.at[pl.ds(0, Z - 1)], p1_s.at[5])
        drain(q_in.at[:, pl.ds(0, (Z - 1) * D)], f_s.at[1])
        drain(q_in.at[:, pl.ds(0, (Z - 1) * D)], f_s.at[2])

    @pl.when(xk != x)
    def _():
        drain(kst_in, p1_s.at[5])
        drain(q_in, f_s.at[1])
        drain(q_in, f_s.at[2])

    drain(q_in.at[:, pl.ds(0, (Z - 1) * D)], f_s.at[0])
    drain(dq_out, f_r.at[0])
    drain(dk_out, f_r.at[1])
    drain(dv_out, f_r.at[2])


def per_device(X, Y, *args):
    R, columns = args[0].shape
    D, Z, C = WIDTH, columns // WIDTH, CORES
    HB, B, H = Z // 2 * R, Z * R, Z
    vm = pltpu.VMEM
    dma = pltpu.SemaphoreType.DMA
    any_spec = pl.BlockSpec(memory_space=pl.ANY)
    vm_spec = pl.BlockSpec(memory_space=pltpu.VMEM)
    queries, keys = (X, 2, C * HB, D), (2, Y * HB, D)
    block, tile = (2, HB, D), (8, 128)
    scratch = [
        vm((R, columns), BF16), vm((R, columns), BF16), vm((H, R), BF16), vm((H, R), F32), vm(tile, F32),
        vm((H, 2, 128), F32), vm((H, 1, 128), F32), vm((Z, 2, 128), F32), vm((Z, 1, 128), F32),
        vm(queries, BF16), vm(queries, BF16), vm((X * C, 2, B), F32),
        vm(keys, BF16), vm(keys, BF16), vm((Y, 1, B), F32),
        vm((2, Y * HB, 128), F32), vm((Y * HB, 128), jnp.int32),
        vm((X * C * Y,) + tile, F32), vm((X * C * Y,) + tile, F32),
        vm((2, D, HB), BF16), vm((2, D, 2 * HB), BF16), vm((2, D, HB), BF16), vm((X, 8, 2 * B), F32),
        vm((X, D, 2 * B), F32), vm((X,) + block, F32), vm((X, 8, 2 * B), F32),
        vm(keys, F32), vm(keys, F32), vm((2, Y * HB, 128), F32),
        vm((X,) + block, BF16), vm((X,) + block, BF16), vm((X,) + block, BF16), vm((X,) + block, BF16),
        vm((X * C, 1, B), F32), vm((X * C, 1, B), F32),
        vm((Y,) + block, BF16), vm((Y,) + block, BF16), vm((Y,) + block, BF16), vm((Y,) + block, BF16),
        vm((Y, 1, B), F32), vm((2, Y, 1, B), F32),
        vm(tile, F32), vm((X * C * Y, 1, 128), F32), vm(block, BF16), vm(block, BF16), vm(block, BF16),
        vm((Z, 1, 128), F32), vm((H, 1, 128), F32),
        dma((4,)), dma((6,)), dma((6,)), dma((2, 3)), dma((2, 3)), dma((2, 3)), dma((2, 3)),
        dma((2, X)), dma((2, X)), dma((1,)), dma((1,)), dma((1,)), dma((1,)),
        dma((2,)), dma((2,)), dma((X,)), dma((X,)), dma((X,)), dma((X,)), dma((1,)), dma((1,)),
        dma((2, Y)), dma((2, Y)), dma((2,)), dma((2,)), dma((4,)), dma((4,)),
    ]
    big = jax.ShapeDtypeStruct((R, columns), BF16)
    dq, dk, dv, dgate = pl.pallas_call(
        functools.partial(body, X, Z, Y, R),
        out_shape=(big, big, big, jax.ShapeDtypeStruct((H, R), BF16)),
        in_specs=[any_spec] * 7,
        out_specs=(any_spec, any_spec, any_spec, vm_spec),
        scratch_shapes=scratch,
        compiler_params=pltpu.CompilerParams(
            collective_id=0, has_side_effects=True, vmem_limit_bytes=63 * 1024 * 1024
        ),
    )(*args[:5], args[5].T, args[6].T)
    return dq, dk, dv, dgate.T


def solution(mesh):
    rows = P(("ctx", "head"), None)

    def whole(*args):
        X = mesh.shape["ctx"] // (CORES * (args[0].shape[1] // WIDTH))
        return jax.shard_map(
            functools.partial(per_device, X, mesh.shape["head"]),
            mesh=mesh,
            in_specs=(rows,) * 7,
            out_specs=(rows,) * 4,
            check_vma=False,
        )(*args)

    return whole
```

```python
import functools
import math

import jax
import jax.numpy as jnp
from jax import lax
from jax.experimental import pallas as pl
from jax.experimental.pallas import tpu as pltpu
from jax.sharding import PartitionSpec as P

CORES = 2
WIDTH = 128
LOG2E = math.log2(math.e)
F32 = jnp.float32
BF16 = jnp.bfloat16
NT = (((1,), (1,)), ((), ()))
NN = (((1,), (0,)), ((), ()))


def dot(a, b, dims):
    return lax.dot_general(a, b, dims, preferred_element_type=F32)


def iota(shape, axis):
    return lax.broadcasted_iota(jnp.int32, shape, axis)


def section_of(index, size, count):
    return sum(((index >= k * size).astype(jnp.int32) for k in range(1, count)), jnp.zeros_like(index))


def section_scan(value, size, count, reverse):
    lane = iota(value.shape, 1)
    inner = lane - size * section_of(lane, size, count)
    width, shift = value.shape[1], 1
    while shift < size:
        if reverse:
            value = value + jnp.where(inner < size - shift, pltpu.roll(value, width - shift, 1), 0.0)
        else:
            value = value + jnp.where(inner >= shift, pltpu.roll(value, shift, 1), 0.0)
        shift *= 2
    return value


def row_scan(value, reverse):
    row, rows = iota(value.shape, 0), value.shape[0]

    def moved(arr, shift):
        if reverse:
            return jnp.where(row < rows - shift, pltpu.roll(arr, rows - shift, 0), 0.0)
        return jnp.where(row >= shift, pltpu.roll(arr, shift, 0), 0.0)

    value, shift = moved(value, 1), 1
    while shift < rows:
        value = value + moved(value, shift)
        shift *= 2
    return value


def lanes(value, width):
    return value[:, :width] if width <= 128 else jnp.concatenate([value] * (width // 128), axis=1)


def body(
    X, Z, Y, R,
    q_in, k_in, v_in, g_in, o_in, gate_in, lse_in,
    dq_out, dk_out, dv_out, dgate_out,
    g_loc, o_loc, gate_loc, lse_loc, gate_pad, st_q, st_k, qst_in, kst_in,
    q_all, g_all, qst_all, k_all, v_all, kst_all, kcol, kpos, tot_all, p_all,
    kt_own, kt_next, kt_far, q_row, dqt, dqt_own, row_acc, dk_acc, dv_acc, cs_acc,
    sib_snd, sib_rcv, dq_snd, dq_rcv, rs_snd, rs_rcv, dk_snd, dv_snd, dk_rcv, dv_rcv, cs_snd, cs_rcv,
    after_own, after_all, dq_fin, dk_fin, dv_fin, gs_snd, gs_rcv,
    loc_sem, p1_r, p1_s, x_r, x_s, y_r, y_s, sib_r, sib_s, qs_r, qs_s, ks_r, ks_s,
    t_r, t_s, dsib_r, dsib_s, dq_r, dq_s, rs_r, rs_s, dk_r, dk_s, cs_r, cs_s, f_r, f_s,
):
    D, H = WIDTH, Z
    half, CY = Z // 2, CORES * Y
    HB, B = half * R, Z * R
    scale = D ** -0.5
    ctx = lax.axis_index("ctx")
    y = lax.axis_index("head")
    c = ctx % CORES
    z = (ctx // CORES) % Z
    x = ctx // (CORES * Z)
    xr = X - 1 - x
    xk = jnp.where(z < half, x, xr)
    cy = c * Y + y
    mesh_id = pl.DeviceIdType.MESH

    def dev(x_, z_, c_, y_):
        return ((x_ * Z + z_) * CORES + c_, y_)

    def remote(src, dst, ssem, rsem, to):
        return pltpu.make_async_remote_copy(
            src_ref=src, dst_ref=dst, send_sem=ssem, recv_sem=rsem, device_id=to, device_id_type=mesh_id
        )

    def drain(ref, sem):
        pltpu.make_async_copy(ref, ref, sem).wait()

    def send(src, dst, ssem, rsem, to, here):
        if here is False:
            remote(src, dst, ssem, rsem, to).start()
        elif here is True:
            pltpu.make_async_copy(src, dst, rsem).start()
        else:
            @pl.when(here)
            def _():
                pltpu.make_async_copy(src, dst, rsem).start()

            @pl.when(jnp.logical_not(here))
            def _():
                remote(src, dst, ssem, rsem, to).start()

    loc = [
        pltpu.make_async_copy(g_in, g_loc, loc_sem.at[0]),
        pltpu.make_async_copy(o_in, o_loc, loc_sem.at[1]),
        pltpu.make_async_copy(gate_in, gate_loc, loc_sem.at[2]),
        pltpu.make_async_copy(lse_in, lse_loc, loc_sem.at[3]),
    ]
    for copy in loc:
        copy.start()

    barrier = pltpu.get_barrier_semaphore()
    plane = [(dx, dc, dy) for dx in range(X) for dc in range(CORES) for dy in range(Y)][1:]

    def greet(to):
        pl.semaphore_signal(barrier, inc=1, device_id=to, device_id_type=mesh_id)

    for d in range(1, Z):
        zz = (z + d) % Z
        greet(dev(x, zz, c, y))
        greet(dev(xr, zz, c, y))
    for dx, dc, dy in plane:
        greet(dev((x + dx) % X, z, (c + dc) % CORES, (y + dy) % Y))
    for copy in loc:
        copy.wait()
    st_q[...] = jnp.zeros_like(st_q)
    st_k[...] = jnp.zeros_like(st_k)
    gate_pad[...] = jnp.zeros_like(gate_pad)
    gate_float = gate_loc[...].astype(F32)
    gate_pad[0:H, 0:R] = jax.nn.log_sigmoid(gate_float)
    curve = section_scan(gate_pad[...], R, 1, False)
    lse_rows = lse_loc[...]
    for h in range(H):
        cut = slice(h * D, (h + 1) * D)
        product = g_loc[:, cut].astype(F32) * o_loc[:, cut].astype(F32)
        st_q[h, 0:1, 0:R] = curve[h:h + 1, 0:R] - lse_rows[h:h + 1, :]
        st_q[h, 0:1, 127:128] = curve[h:h + 1, R - 1:R]
        st_q[h, 1:2, 0:R] = jnp.sum(product.T, axis=0, keepdims=True)
        st_k[h, 0:1, 0:R] = curve[h:h + 1, 0:R]
    pl.semaphore_wait(barrier, 2 * (Z - 1) + len(plane))

    z_order = sorted(range(Z), key=lambda d: -min(d, Z - d))

    def columns(h_):
        return pl.ds(pl.multiple_of(h_ * D, D), D)

    z_half = z // half

    def z_rows(block):
        return pl.ds(pl.multiple_of(block * HB + (z % half) * R, R), R)

    def block_rows(block):
        return pl.ds(pl.multiple_of(block * HB, HB), HB)

    for d in z_order:
        zz = (z + d) % Z
        send(st_q.at[zz], qst_in.at[z], p1_s.at[4], p1_r.at[4], dev(x, zz, c, y), d == 0)
        send(
            st_k.at[zz], kst_in.at[z], p1_s.at[5], p1_r.at[5], dev(xk, zz, c, y),
            (xk == x) if d == 0 else False,
        )

    for idx, src, dst in ((0, q_in, q_all), (1, g_in, g_all), (2, k_in, k_all), (3, v_in, v_all)):
        for d in z_order:
            zz = (z + d) % Z
            if idx < 2:
                at, to, here = dst.at[x, z_half, z_rows(c), :], dev(x, zz, c, y), d == 0
            else:
                at, to = dst.at[z_half, z_rows(0), :], dev(xk, zz, c, y)
                here = (xk == x) if d == 0 else False
            send(src.at[:, columns(zz)], at, p1_s.at[idx], p1_r.at[idx], to, here)

    def q_block(ref, x_, c_):
        return ref.at[x_, :, block_rows(c_), :]

    def k_block(ref, slot):
        return ref.at[:, block_rows(slot), :]

    sibling = dev(x, z, 1 - c, y)
    queries = [functools.partial(q_block, ref, c_=c) for ref in (q_all, g_all)]
    keys = [functools.partial(k_block, ref) for ref in (k_all, v_all)]

    def x_dev(d):
        return dev((x + d) % X, z, c, y)

    def y_dev(d):
        return dev(x, z, c, (y + d) % Y)

    order = [0, 1, Y - 1, 2][:Y] if Y > 2 else [0, 1][:Y]

    def q_id(d, e):
        return (x + d) % X

    def k_id(d, e):
        return order.index((d - e) % Y)

    def ring_copy(blocks, arr, name, d, e, place, section, snd, rcv):
        src, dst = blocks[arr](name(d, 0)), blocks[arr](name(d, e))
        return remote(src, dst, snd.at[arr, section], rcv.at[arr, section], place(e))

    def ring_start(blocks, arr, name, n, place, snd, rcv):
        if n > 1:
            ring_copy(blocks, arr, name, 0, 1, place, 0, snd, rcv).start()
        if n > 2:
            ring_copy(blocks, arr, name, 0, -1, place, 1, snd, rcv).start()

    def ring_onward(blocks, arr, name, n, place, snd, rcv):
        came = -1 if arr == 0 else 1
        if n > 1:
            drain(blocks[arr](name(came, 0)), rcv.at[arr, arr if n > 2 else 0])
        if n > 2:
            ring_copy(blocks, arr, name, came, -came, place, 2, snd, rcv).start()

    def ring_other(blocks, arr, name, n, rcv):
        if n > 2:
            drain(blocks[arr](name(1 if arr == 0 else -1, 0)), rcv.at[arr, 1 - arr])

    def ring_last(blocks, arr, name, n, rcv):
        if n > 2:
            drain(blocks[arr](name(2, 0)), rcv.at[arr, 2])

    def ring_sent(blocks, arr, name, n, snd):
        block = blocks[arr](name(0, 0))
        for k in range(0 if n == 1 else 1 if n == 2 else 3):
            drain(block, snd.at[arr, k])

    def to_sibling(arr, x_):
        block = queries[arr](x_)
        remote(block, block, sib_s.at[arr, x_], sib_r.at[arr, x_], sibling).start()

    def wide(tile):
        return jnp.concatenate([tile, jnp.zeros((8, B - 128), F32)], axis=1) if B > 128 else tile[:, :B]

    in_piece_lanes = iota((8, 128), 1) < R

    def assemble(ref, at):
        total = jnp.zeros((8, B), F32)
        for s in range(Z):
            tile = jnp.where(in_piece_lanes, jnp.broadcast_to(ref[s, at:at + 1, :], (8, 128)), 0.0)
            total = total + (pltpu.roll(wide(tile), s * R, 1) if s else wide(tile))
        return total

    row_at = iota((8, 128), 0)
    drain(qst_in, p1_r.at[4])
    totals = jnp.zeros((8, 128), F32)
    for s in range(Z):
        totals = jnp.where(row_at == s, jnp.broadcast_to(qst_in[s, 0:1, 127:128], (8, 128)), totals)
    tot_all[x * CY + cy] = totals

    def spread(ref, slot, semr, sems):
        for dx, dc, dy in plane:
            to = dev((x + dx) % X, z, (c + dc) % CORES, (y + dy) % Y)
            remote(ref.at[slot], ref.at[slot], sems, semr, to).start()

    spread(tot_all, x * CY + cy, t_r.at[0], t_s.at[0])
    xc = x * CORES + c
    for at in range(2):
        qst_all[xc, at:at + 1, :] = assemble(qst_in, at)[0:1]
    q_team = [(dx, dc) for dx in range(X) for dc in range(CORES)][1:]
    for dx, dc in q_team:
        x_, c_ = (x + dx) % X, (c + dc) % CORES
        mine = qst_all.at[xc]
        remote(mine, mine, qs_s.at[0], qs_r.at[0], dev(x_, z, c_, y)).start()

    drain(kst_in, p1_r.at[5])
    kst_all[y] = assemble(kst_in, 0)[0:1]
    for dy in range(1, Y):
        mine = kst_all.at[y]
        remote(mine, mine, ks_s.at[0], ks_r.at[0], y_dev(dy)).start()
    for arr in range(2):
        drain(queries[arr](x), p1_r.at[arr])
        ring_start(queries, arr, q_id, X, x_dev, x_s, x_r)
        to_sibling(arr, x)

    dk_acc[...] = jnp.zeros_like(dk_acc)
    dv_acc[...] = jnp.zeros_like(dv_acc)
    cs_acc[...] = jnp.zeros_like(cs_acc)
    dqt[...] = jnp.zeros_like(dqt)
    row_acc[...] = jnp.zeros_like(row_acc)
    after_own[...] = jnp.zeros((8, 128), F32)
    k_at = iota((HB, 128), 0)
    k_z = section_of(k_at, R, half)
    for slot, dy in enumerate(order):
        k_y = (y + dy) % Y
        kpos[slot * HB:(slot + 1) * HB, :] = k_z * (CY * R) + c * (Y * R) + k_y * R + (k_at - R * k_z)
    q_at = iota((8, 2 * B), 1)
    q_half = (q_at >= B).astype(jnp.int32)
    q_rest = q_at - B * q_half
    q_c = section_of(q_rest, HB, CORES)
    q_rest = q_rest - HB * q_c
    q_z = section_of(q_rest, R, half)
    qpos = (q_half * half + q_z) * (CY * R) + q_c * (Y * R) + y * R + (q_rest - R * q_z)

    few = X * CY - 1
    drain(tot_all.at[pl.ds(0, few)], t_r.at[0])
    before = jnp.zeros((8, 128), F32)
    for x_ in range(X):
        level = jnp.zeros((8, 128), F32)
        for k in range(CY):
            level = level + tot_all[x_ * CY + k]
        run = before + row_scan(level, False)
        for k in range(CY):
            p_all[x_ * CY + k] = run
            run = run + tot_all[x_ * CY + k]
        before = before + jnp.sum(level, axis=0, keepdims=True)

    piece_row, piece_lane = iota((8, B), 0), iota((8, B), 1)
    in_piece = piece_row == section_of(piece_lane, R, Z)

    def along_lanes(tile):
        return jnp.sum(jnp.where(in_piece, lanes(tile, B), 0.0), axis=0, keepdims=True)

    low = iota((8, B), 1) < HB

    def halves(first, second):
        return (
            jnp.where(low, first, pltpu.roll(second, HB, 1)),
            jnp.where(low, pltpu.roll(first, HB, 1), second),
        )

    drain(qst_all.at[pl.ds(0, len(q_team))], qs_r.at[0])
    for x_ in range(X):
        rows = []
        for c_ in range(CORES):
            bias = along_lanes(p_all[x_ * CY + c_ * Y + y])
            stat = qst_all[x_ * CORES + c_]
            rows.append(jnp.where(iota((8, B), 0) == 0, (stat[0:1] + bias) * LOG2E, jnp.broadcast_to(stat[1:2], (8, B))))
        q_row[x_] = jnp.concatenate(halves(*rows), axis=1)

    if Y > 1:
        drain(kst_all.at[pl.ds(0, Y - 1)], ks_r.at[0])
    for slot, dy in enumerate(order):
        y_ = (y + dy) % Y
        tile = jnp.where(row_at < half, p_all[x * CY + c * Y + y_], p_all[xr * CY + c * Y + y_])
        column = jnp.broadcast_to((kst_all[y_] + along_lanes(tile)) * LOG2E, (8, B)).T[:, 0:1]
        spread_column = jnp.broadcast_to(column, (B, 128))
        kcol[0, slot * HB:(slot + 1) * HB, :] = spread_column[0:HB]
        kcol[1, slot * HB:(slot + 1) * HB, :] = spread_column[HB:B]

    def pair(x_, kh, rows, turned, first_lane, masked):
        count = 2 * B - first_lane
        part = slice(first_lane, 2 * B)
        if first_lane:
            q_blk, g_blk = q_all[x_, 1], g_all[x_, 1]
        else:
            q_blk, g_blk = q_all[x_].reshape(2 * B, D), g_all[x_].reshape(2 * B, D)
        row, delta = q_row[x_, 0:1, part], q_row[x_, 1:2, part]
        k_blk, v_blk = k_all[kh, rows, :], v_all[kh, rows, :]
        s = dot(k_blk, q_blk, NT)
        prob = jnp.exp2(s * (scale * LOG2E) + row - lanes(kcol[kh, rows, :], count))
        if masked:
            at = kpos[rows, :] + kh * (half * CY * R)
            prob = jnp.where(lanes(at, count) <= qpos[0:1, part], prob, 0.0)
        grad = prob * (dot(v_blk, g_blk, NT) - delta)
        prob_half, grad_half = prob.astype(BF16), grad.astype(BF16)
        dv_acc[kh, rows, :] += dot(prob_half, g_blk, NN)
        dk_acc[kh, rows, :] += dot(grad_half, q_blk, NN)
        dqt[x_, :, part] += dot(turned[kh], grad_half, NN)
        row_acc[x_, 0:1, part] += jnp.sum(grad, axis=0, keepdims=True)
        if count >= 128:
            folded = grad[:, 0:128]
            for lane in range(128, count, 128):
                folded = folded + grad[:, lane:lane + 128]
            cs_acc[kh, rows, :] += folded
        else:
            cs_acc[kh, rows, 0:count] += grad

    def key_turn(turned, rows):
        for kh in range(2):
            turned[kh] = k_all[kh, rows, :].astype(F32).T.astype(BF16)

    kt_all = (kt_own, kt_next, kt_far) if Y > 2 else (kt_own, kt_far)

    def sib_wait(x_):
        for arr in range(2):
            drain(q_block((q_all, g_all)[arr], x_, 1 - c), sib_r.at[arr, x_])

    def piece_totals(row):
        return jnp.sum(jnp.where(in_piece, jnp.broadcast_to(row, (8, B)), 0.0), axis=1, keepdims=True)

    lane_at = iota((8, 128), 1)

    def note(kind, row):
        after_own[...] = jnp.where(lane_at == kind * Z + row_at, piece_totals(row), after_own[...])

    def curve_send(slot):
        rows, dy = pl.ds(slot * HB, HB), order[slot]
        column = jnp.concatenate([cs_acc[0, rows, :], cs_acc[1, rows, :]], axis=0)
        sums = jnp.sum(column.T, axis=0, keepdims=True)
        cs_snd[slot] = sums
        note(X * CORES + (y + dy) % Y, sums)
        send(cs_snd.at[slot], cs_rcv.at[0, y], cs_s.at[0], cs_r.at[0], y_dev(dy), dy == 0)
        send(cs_snd.at[slot], cs_rcv.at[1, y], cs_s.at[1], cs_r.at[1], dev(xr, z, c, (y + dy) % Y), False)

    key_sums = ((dk_acc, dk_snd, dk_rcv, scale), (dv_acc, dv_snd, dv_rcv, 1.0))

    def key_send(slot):
        side = order.index(-order[slot] % Y) - 1
        for arr, (acc, snd, rcv, factor) in enumerate(key_sums):
            for kh in range(2):
                snd[slot, kh] = (acc[kh, slot * HB:(slot + 1) * HB, :] * factor).astype(BF16)
            remote(
                snd.at[slot], rcv.at[side], dk_s.at[arr, slot], dk_r.at[arr, side], y_dev(order[slot])
            ).start()

    def query_steps(i):
        if i == 1:
            for arr in range(2):
                ring_onward(queries, arr, q_id, X, x_dev, x_s, x_r)
                to_sibling(arr, (x + X - 1) % X if arr == 0 else (x + 1) % X)
            if X > 2:
                for arr in range(2):
                    ring_other(queries, arr, q_id, X, x_r)
                    to_sibling(arr, (x + 1) % X if arr == 0 else (x + X - 1) % X)
        if i == 3:
            for arr in range(2):
                ring_last(queries, arr, q_id, X, x_r)
                to_sibling(arr, (x + 2) % X)
        if i == X - 1:
            for arr in range(2):
                ring_onward(keys, arr, k_id, Y, y_dev, y_s, y_r)
        if i:
            sib_wait((x + x_order[i]) % X)

    def rows_done(x_):
        dq_part = dqt[x_].T * scale
        for hf in range(2):
            lower, upper = dq_part[hf * B:hf * B + HB], dq_part[hf * B + HB:hf * B + B]
            dqt_own[x_, hf] = jnp.where(c == 0, lower, upper)
            sib_snd[x_, hf] = jnp.where(c == 0, upper, lower).astype(BF16)
        remote(sib_snd.at[x_], sib_rcv.at[x_], dsib_s.at[x_], dsib_r.at[x_], sibling).start()

    def rows_curve(x_):
        tiles = halves(row_acc[x_, :, 0:B], row_acc[x_, :, B:2 * B])
        for c_ in range(CORES):
            rs_snd[x_ * CORES + c_] = tiles[c_][0:1]
            note(x_ * CORES + c_, tiles[c_][0:1])
            src, dst = rs_snd.at[x_ * CORES + c_], rs_rcv.at[xc]
            here = jnp.logical_and(x_ == x, c_ == c)
            send(src, dst, rs_s.at[0], rs_r.at[0], dev(x_, z, c_, y), here)

    def rows_home(x_):
        drain(sib_rcv.at[x_], dsib_r.at[x_])
        dq_snd[x_] = (dqt_own[x_] + sib_rcv[x_].astype(F32)).astype(BF16)
        remote(dq_snd.at[x_], dq_rcv.at[x], dq_s.at[x_], dq_r.at[x], dev(x_, z, c, y)).start()

    x_order = [0, 1, X - 1, 2][:X] if X > 2 else [0, 1][:X]
    bands = {1: [(0, 1)], 2: [(0, 1), (1, 1)], 4: [(0, 1), (1, 2), (3, 1)]}[Y]

    def pick(values, at):
        return sum(jnp.where(at == k, v, 0) for k, v in enumerate(values))

    for arr in range(2):
        drain(keys[arr](0), p1_r.at[2 + arr])
        ring_start(keys, arr, k_id, Y, y_dev, y_s, y_r)
    sib_wait(x)

    def band(first_slot, slots, turned, last, before_step):
        rows = pl.ds(first_slot * HB, slots * HB)
        key_turn(turned, rows)

        def step(i, carry):
            for k in range(1, X):
                if before_step:
                    pl.when(i == k)(functools.partial(before_step, k))
            x_ = (x + pick(x_order, X - 1 - i if last else i)) % X

            def key_half(kh, inner):
                @pl.when(x_ > jnp.where(kh == 0, x, xr))
                def _():
                    pair(x_, kh, rows, turned, 0, False)

                return inner

            lax.fori_loop(0, 2, key_half, 0)

            @pl.when(x_ == x)
            def _():
                pair(x_, 0, rows, turned, 0, True)

            @pl.when(x_ == xr)
            def _():
                pair(x_, 1, rows, turned, B, True)

            if last:
                rows_done(x_)

                @pl.when(i > 0)
                def _():
                    rows_home((x + pick(x_order, X - i)) % X)

            return carry

        lax.fori_loop(0, X, step, 0)

    for b, (first_slot, slots) in enumerate(bands):
        if b == 1:
            for arr in range(2):
                ring_other(keys, arr, k_id, Y, y_r)
        if b == 2:
            for arr in range(2):
                ring_last(keys, arr, k_id, Y, y_r)
        band(first_slot, slots, kt_all[b], b == len(bands) - 1, None if b else query_steps)
        if b:
            for slot in range(first_slot, first_slot + slots):
                key_send(slot)

    for x_ in range(X):
        rows_curve(x_)
    for slot in range(Y):
        curve_send(slot)
    after_all[x * CY + cy] = jnp.sum(after_own[...], axis=0, keepdims=True)
    spread(after_all, x * CY + cy, t_r.at[1], t_s.at[1])

    def give_back(fin, out, idx, keyed):
        for d in z_order:
            zz = (z + d) % Z
            src = fin.at[zz // half, pl.ds(pl.multiple_of((zz % half) * R, R), R), :]
            dst = out.at[:, columns(z)]
            at_x = jnp.where(zz < half, x, xr) if keyed else x
            here = False if d else ((at_x == x) if keyed else True)
            send(src, dst, f_s.at[idx], f_r.at[idx], dev(at_x, zz, c, y), here)

    drain(sib_rcv.at[x], dsib_r.at[x])
    dq_sum = dqt_own[x] + sib_rcv[x].astype(F32)
    for dx in range(1, X):
        x_ = (x + dx) % X
        drain(dq_rcv.at[x_], dq_r.at[x_])
        dq_sum = dq_sum + dq_rcv[x_].astype(F32)
    dq_fin[...] = dq_sum.astype(BF16)
    give_back(dq_fin, dq_out, 0, False)

    for rcv, acc, fin, out, idx, factor in (
        (dk_rcv, dk_acc, dk_fin, dk_out, 1, scale), (dv_rcv, dv_acc, dv_fin, dv_out, 2, 1.0)
    ):
        sums = [acc[kh, 0:HB, :] * factor for kh in range(2)]
        for side in range(Y - 1):
            drain(rcv.at[side], dk_r.at[idx - 1, side])
            sums = [sums[kh] + rcv[side, kh].astype(F32) for kh in range(2)]
        for kh in range(2):
            fin[kh] = sums[kh].astype(BF16)
        give_back(fin, out, idx, True)

    drain(rs_rcv, rs_r.at[0])
    drain(cs_rcv.at[0], cs_r.at[0])
    drain(cs_rcv.at[1], cs_r.at[1])
    rows_sum = jnp.zeros((1, B), F32)
    for x_ in range(X):
        for c_ in range(CORES):
            rows_sum = rows_sum + rs_rcv[x_ * CORES + c_]
    columns_sum = jnp.zeros((1, B), F32)
    for y_ in range(Y):
        columns_sum = columns_sum + jnp.where(low[0:1], cs_rcv[0, y_], cs_rcv[1, y_])
    later = section_scan(jnp.broadcast_to(rows_sum - columns_sum, (8, B)), R, Z, True)
    drain(after_all.at[pl.ds(0, few)], t_r.at[1])
    kind_at = section_of(lane_at, Z, X * CORES + Y)
    piece_at = lane_at - Z * kind_at
    of_x = section_of(kind_at, CORES, X + Y)
    turn_at = (kind_at - CORES * of_x) * Y
    later_x = own_x = own_later = jnp.zeros((8, 128), F32)
    for y_ in range(Y):
        tile = sum(after_all[(x_ * CORES + c_) * Y + y_] for x_ in range(X) for c_ in range(CORES))
        tile = jnp.where(kind_at < X * CORES, tile, 0.0)
        own = jnp.where(of_x == x, tile, 0.0)
        later_x = later_x + jnp.where(of_x > x, tile, 0.0)
        own_x = own_x + own
        own_later = own_later + jnp.where(turn_at + y_ > cy, own, 0.0)
    column_at = kind_at - X * CORES
    is_column = jnp.logical_and(column_at >= 0, column_at < Y)
    for c_ in range(CORES):
        tiles = [
            jnp.where(is_column, sum(after_all[(x_ * CORES + c_) * Y + y_] for y_ in range(Y)), 0.0)
            for x_ in range(X)
        ]
        for x_ in range(X):
            tile = jnp.where(piece_at < half, tiles[x_], tiles[X - 1 - x_])
            own = jnp.where(x_ == x, tile, 0.0)
            later_x = later_x - jnp.where(x_ > x, tile, 0.0)
            own_x = own_x - own
            own_later = own_later - jnp.where(column_at + c_ * Y > cy, own, 0.0)
    terms = later_x + jnp.where(piece_at > row_at, own_x, 0.0) + jnp.where(piece_at == row_at, own_later, 0.0)
    after = jnp.broadcast_to(jnp.sum(terms, axis=1, keepdims=True), (8, 128))
    gate_sum = later + along_lanes(after)
    for s in range(Z):
        moved = pltpu.roll(gate_sum, (B - s * R) % B, 1) if s else gate_sum
        gs_snd[s] = (moved[:, 0:128] if B >= 128 else jnp.concatenate([moved, jnp.zeros((8, 128 - B), F32)], axis=1))[0:1]
    for d in z_order:
        zz = (z + d) % Z
        send(gs_snd.at[zz], gs_rcv.at[z], f_s.at[3], f_r.at[3], dev(x, zz, c, y), d == 0)
    drain(gs_rcv, f_r.at[3])
    by_head = jnp.zeros((8, 128), F32)
    for h in range(H):
        by_head = by_head + jnp.where(row_at == h, jnp.broadcast_to(gs_rcv[h], (8, 128)), 0.0)
    dgate_out[...] = (by_head[0:H, 0:R] * jax.nn.sigmoid(-gate_float)).astype(BF16)

    for arr in range(2):
        ring_sent(queries, arr, q_id, X, x_s)
        ring_sent(keys, arr, k_id, Y, y_s)
        for x_ in range(X):
            drain(queries[arr](x_), sib_s.at[arr, x_])
        for slot in range(1, Y):
            drain(dk_snd.at[slot], dk_s.at[arr, slot])
    drain(qst_all.at[pl.ds(0, len(q_team))], qs_s.at[0])
    drain(rs_snd.at[pl.ds(0, len(q_team))], rs_s.at[0])
    if Y > 1:
        drain(kst_all.at[pl.ds(0, Y - 1)], ks_s.at[0])
        drain(cs_snd.at[pl.ds(0, Y - 1)], cs_s.at[0])
    drain(cs_snd, cs_s.at[1])
    drain(tot_all.at[pl.ds(0, few)], t_s.at[0])
    drain(after_all.at[pl.ds(0, few)], t_s.at[1])
    for dx in range(X):
        x_ = (x + dx) % X
        drain(sib_snd.at[x_], dsib_s.at[x_])
        if dx:
            drain(dq_snd.at[x_], dq_s.at[x_])

    for idx in range(4):
        less, more = q_in.at[:, pl.ds(0, (Z - 1) * D)], q_in
        if idx < 2:
            drain(less, p1_s.at[idx])
        else:
            @pl.when(xk == x)
            def _(idx=idx, less=less):
                drain(less, p1_s.at[idx])

            @pl.when(xk != x)
            def _(idx=idx, more=more):
                drain(more, p1_s.at[idx])
    drain(qst_in.at[pl.ds(0, Z - 1)], p1_s.at[4])
    drain(gs_snd.at[pl.ds(0, Z - 1)], f_s.at[3])

    @pl.when(xk == x)
    def _():
        drain(kst_in.at[pl.ds(0, Z - 1)], p1_s.at[5])
        drain(q_in.at[:, pl.ds(0, (Z - 1) * D)], f_s.at[1])
        drain(q_in.at[:, pl.ds(0, (Z - 1) * D)], f_s.at[2])

    @pl.when(xk != x)
    def _():
        drain(kst_in, p1_s.at[5])
        drain(q_in, f_s.at[1])
        drain(q_in, f_s.at[2])

    drain(q_in.at[:, pl.ds(0, (Z - 1) * D)], f_s.at[0])
    drain(dq_out, f_r.at[0])
    drain(dk_out, f_r.at[1])
    drain(dv_out, f_r.at[2])


def per_device(X, Y, *args):
    R, columns = args[0].shape
    D, Z, C = WIDTH, columns // WIDTH, CORES
    HB, B, H = Z // 2 * R, Z * R, Z
    vm = pltpu.VMEM
    dma = pltpu.SemaphoreType.DMA
    any_spec = pl.BlockSpec(memory_space=pl.ANY)
    vm_spec = pl.BlockSpec(memory_space=pltpu.VMEM)
    queries, keys = (X, 2, C * HB, D), (2, Y * HB, D)
    block, tile = (2, HB, D), (8, 128)
    scratch = [
        vm((R, columns), BF16), vm((R, columns), BF16), vm((H, R), BF16), vm((H, R), F32), vm(tile, F32),
        vm((H, 2, 128), F32), vm((H, 1, 128), F32), vm((Z, 2, 128), F32), vm((Z, 1, 128), F32),
        vm(queries, BF16), vm(queries, BF16), vm((X * C, 2, B), F32),
        vm(keys, BF16), vm(keys, BF16), vm((Y, 1, B), F32),
        vm((2, Y * HB, 128), F32), vm((Y * HB, 128), jnp.int32),
        vm((X * C * Y,) + tile, F32), vm((X * C * Y,) + tile, F32),
        vm((2, D, HB), BF16), vm((2, D, 2 * HB), BF16), vm((2, D, HB), BF16), vm((X, 8, 2 * B), F32),
        vm((X, D, 2 * B), F32), vm((X,) + block, F32), vm((X, 8, 2 * B), F32),
        vm(keys, F32), vm(keys, F32), vm((2, Y * HB, 128), F32),
        vm((X,) + block, BF16), vm((X,) + block, BF16), vm((X,) + block, BF16), vm((X,) + block, BF16),
        vm((X * C, 1, B), F32), vm((X * C, 1, B), F32),
        vm((Y,) + block, BF16), vm((Y,) + block, BF16), vm((Y,) + block, BF16), vm((Y,) + block, BF16),
        vm((Y, 1, B), F32), vm((2, Y, 1, B), F32),
        vm(tile, F32), vm((X * C * Y, 1, 128), F32), vm(block, BF16), vm(block, BF16), vm(block, BF16),
        vm((Z, 1, 128), F32), vm((H, 1, 128), F32),
        dma((4,)), dma((6,)), dma((6,)), dma((2, 3)), dma((2, 3)), dma((2, 3)), dma((2, 3)),
        dma((2, X)), dma((2, X)), dma((1,)), dma((1,)), dma((1,)), dma((1,)),
        dma((2,)), dma((2,)), dma((X,)), dma((X,)), dma((X,)), dma((X,)), dma((1,)), dma((1,)),
        dma((2, Y)), dma((2, Y)), dma((2,)), dma((2,)), dma((4,)), dma((4,)),
    ]
    big = jax.ShapeDtypeStruct((R, columns), BF16)
    dq, dk, dv, dgate = pl.pallas_call(
        functools.partial(body, X, Z, Y, R),
        out_shape=(big, big, big, jax.ShapeDtypeStruct((H, R), BF16)),
        in_specs=[any_spec] * 7,
        out_specs=(any_spec, any_spec, any_spec, vm_spec),
        scratch_shapes=scratch,
        compiler_params=pltpu.CompilerParams(
            collective_id=0, has_side_effects=True, vmem_limit_bytes=48 * 1024 * 1024
        ),
    )(*(pltpu.with_memory_space_constraint(value, pltpu.HBM) for value in (*args[:5], args[5].T, args[6].T)))
    return dq, dk, dv, dgate.T


def solution(mesh):
    rows = P(("ctx", "head"), None)

    def whole(*args):
        X = mesh.shape["ctx"] // (CORES * (args[0].shape[1] // WIDTH))
        return jax.shard_map(
            functools.partial(per_device, X, mesh.shape["head"]),
            mesh=mesh,
            in_specs=(rows,) * 7,
            out_specs=(rows,) * 4,
            check_vma=False,
        )(*args)

    return whole
```

```python
import functools
import math

import jax
import jax.numpy as jnp
from jax import lax
from jax.experimental import pallas as pl
from jax.experimental.pallas import tpu as pltpu
from jax.sharding import PartitionSpec as P

CORES = 2
WIDTH = 128
LOG2E = math.log2(math.e)
F32 = jnp.float32
BF16 = jnp.bfloat16
NT = (((1,), (1,)), ((), ()))
NN = (((1,), (0,)), ((), ()))


def dot(a, b, dims):
    return lax.dot_general(a, b, dims, preferred_element_type=F32)


def iota(shape, axis):
    return lax.broadcasted_iota(jnp.int32, shape, axis)


def section_of(index, size, count):
    return sum(((index >= k * size).astype(jnp.int32) for k in range(1, count)), jnp.zeros_like(index))


def section_scan(value, size, count, reverse):
    lane = iota(value.shape, 1)
    inner = lane - size * section_of(lane, size, count)
    width, shift = value.shape[1], 1
    while shift < size:
        if reverse:
            value = value + jnp.where(inner < size - shift, pltpu.roll(value, width - shift, 1), 0.0)
        else:
            value = value + jnp.where(inner >= shift, pltpu.roll(value, shift, 1), 0.0)
        shift *= 2
    return value


def row_scan(value, reverse):
    row, rows = iota(value.shape, 0), value.shape[0]

    def moved(arr, shift):
        if reverse:
            return jnp.where(row < rows - shift, pltpu.roll(arr, rows - shift, 0), 0.0)
        return jnp.where(row >= shift, pltpu.roll(arr, shift, 0), 0.0)

    value, shift = moved(value, 1), 1
    while shift < rows:
        value = value + moved(value, shift)
        shift *= 2
    return value


def lanes(value, width):
    return value[:, :width] if width <= 128 else jnp.concatenate([value] * (width // 128), axis=1)


def body(
    X, Z, Y, R,
    q_in, k_in, v_in, g_in, o_in, gate_in, lse_in,
    grads_out, dgate_out,
    g_loc, o_loc, gate_loc, lse_loc, gate_pad, st_q, st_k, qst_in, kst_in,
    q_all, g_all, qst_all, k_all, v_all, kst_all, kcol, kpos, tot_all, p_all,
    kt_own, kt_next, kt_far, q_row, dqt, dqt_own, row_acc, dk_acc, dv_acc, cs_acc,
    sib_snd, sib_rcv, dq_snd, dq_rcv, rs_snd, rs_rcv, dk_snd, dv_snd, dk_rcv, dv_rcv, cs_snd, cs_rcv,
    after_own, after_all, dq_fin, dk_fin, dv_fin, gs_snd, gs_rcv,
    loc_sem, p1_r, p1_s, x_r, x_s, y_r, y_s, sib_r, sib_s, qs_r, qs_s, ks_r, ks_s,
    t_r, t_s, dsib_r, dsib_s, dq_r, dq_s, rs_r, rs_s, dk_r, dk_s, cs_r, cs_s, f_r, f_s,
):
    dq_out, dk_out, dv_out = (grads_out.at[k] for k in range(3))
    D, H = WIDTH, Z
    half, CY = Z // 2, CORES * Y
    HB, B = half * R, Z * R
    scale = D ** -0.5
    ctx = lax.axis_index("ctx")
    y = lax.axis_index("head")
    c = ctx % CORES
    z = (ctx // CORES) % Z
    x = ctx // (CORES * Z)
    xr = X - 1 - x
    xk = jnp.where(z < half, x, xr)
    cy = c * Y + y
    mesh_id = pl.DeviceIdType.MESH

    def dev(x_, z_, c_, y_):
        return ((x_ * Z + z_) * CORES + c_, y_)

    def remote(src, dst, ssem, rsem, to):
        return pltpu.make_async_remote_copy(
            src_ref=src, dst_ref=dst, send_sem=ssem, recv_sem=rsem, device_id=to, device_id_type=mesh_id
        )

    def drain(ref, sem):
        pltpu.make_async_copy(ref, ref, sem).wait()

    def send(src, dst, ssem, rsem, to, here):
        if here is False:
            remote(src, dst, ssem, rsem, to).start()
        elif here is True:
            pltpu.make_async_copy(src, dst, rsem).start()
        else:
            @pl.when(here)
            def _():
                pltpu.make_async_copy(src, dst, rsem).start()

            @pl.when(jnp.logical_not(here))
            def _():
                remote(src, dst, ssem, rsem, to).start()

    loc = [
        pltpu.make_async_copy(g_in, g_loc, loc_sem.at[0]),
        pltpu.make_async_copy(o_in, o_loc, loc_sem.at[1]),
        pltpu.make_async_copy(gate_in, gate_loc, loc_sem.at[2]),
        pltpu.make_async_copy(lse_in, lse_loc, loc_sem.at[3]),
    ]
    for copy in loc:
        copy.start()

    barrier = pltpu.get_barrier_semaphore()
    plane = [(dx, dc, dy) for dx in range(X) for dc in range(CORES) for dy in range(Y)][1:]

    def greet(to):
        pl.semaphore_signal(barrier, inc=1, device_id=to, device_id_type=mesh_id)

    for d in range(1, Z):
        zz = (z + d) % Z
        greet(dev(x, zz, c, y))
        greet(dev(xr, zz, c, y))
    for dx, dc, dy in plane:
        greet(dev((x + dx) % X, z, (c + dc) % CORES, (y + dy) % Y))
    for copy in loc:
        copy.wait()
    st_q[...] = jnp.zeros_like(st_q)
    st_k[...] = jnp.zeros_like(st_k)
    gate_pad[...] = jnp.zeros_like(gate_pad)
    gate_float = gate_loc[...].astype(F32)
    gate_pad[0:H, 0:R] = jax.nn.log_sigmoid(gate_float)
    curve = section_scan(gate_pad[...], R, 1, False)
    lse_rows = lse_loc[...]
    for h in range(H):
        cut = slice(h * D, (h + 1) * D)
        product = g_loc[:, cut].astype(F32) * o_loc[:, cut].astype(F32)
        st_q[h, 0:1, 0:R] = curve[h:h + 1, 0:R] - lse_rows[h:h + 1, :]
        st_q[h, 0:1, 127:128] = curve[h:h + 1, R - 1:R]
        st_q[h, 1:2, 0:R] = jnp.sum(product.T, axis=0, keepdims=True)
        st_k[h, 0:1, 0:R] = curve[h:h + 1, 0:R]
    pl.semaphore_wait(barrier, 2 * (Z - 1) + len(plane))

    z_order = sorted(range(Z), key=lambda d: -min(d, Z - d))

    def columns(h_):
        return pl.ds(pl.multiple_of(h_ * D, D), D)

    z_half = z // half

    def z_rows(block):
        return pl.ds(pl.multiple_of(block * HB + (z % half) * R, R), R)

    def block_rows(block):
        return pl.ds(pl.multiple_of(block * HB, HB), HB)

    for d in z_order:
        zz = (z + d) % Z
        send(st_q.at[zz], qst_in.at[z], p1_s.at[4], p1_r.at[4], dev(x, zz, c, y), d == 0)
        send(
            st_k.at[zz], kst_in.at[z], p1_s.at[5], p1_r.at[5], dev(xk, zz, c, y),
            (xk == x) if d == 0 else False,
        )

    for idx, src, dst in ((0, q_in, q_all), (1, g_in, g_all), (2, k_in, k_all), (3, v_in, v_all)):
        for d in z_order:
            zz = (z + d) % Z
            if idx < 2:
                at, to, here = dst.at[x, z_half, z_rows(c), :], dev(x, zz, c, y), d == 0
            else:
                at, to = dst.at[z_half, z_rows(0), :], dev(xk, zz, c, y)
                here = (xk == x) if d == 0 else False
            send(src.at[:, columns(zz)], at, p1_s.at[idx], p1_r.at[idx], to, here)

    def q_block(ref, x_, c_):
        return ref.at[x_, :, block_rows(c_), :]

    def k_block(ref, slot):
        return ref.at[:, block_rows(slot), :]

    sibling = dev(x, z, 1 - c, y)
    queries = [functools.partial(q_block, ref, c_=c) for ref in (q_all, g_all)]
    keys = [functools.partial(k_block, ref) for ref in (k_all, v_all)]

    def x_dev(d):
        return dev((x + d) % X, z, c, y)

    def y_dev(d):
        return dev(x, z, c, (y + d) % Y)

    order = [0, 1, Y - 1, 2][:Y] if Y > 2 else [0, 1][:Y]

    def q_id(d, e):
        return (x + d) % X

    def k_id(d, e):
        return order.index((d - e) % Y)

    def ring_copy(blocks, arr, name, d, e, place, section, snd, rcv):
        src, dst = blocks[arr](name(d, 0)), blocks[arr](name(d, e))
        return remote(src, dst, snd.at[arr, section], rcv.at[arr, section], place(e))

    def ring_start(blocks, arr, name, n, place, snd, rcv):
        if n > 1:
            ring_copy(blocks, arr, name, 0, 1, place, 0, snd, rcv).start()
        if n > 2:
            ring_copy(blocks, arr, name, 0, -1, place, 1, snd, rcv).start()

    def ring_onward(blocks, arr, name, n, place, snd, rcv):
        came = -1 if arr == 0 else 1
        if n > 1:
            drain(blocks[arr](name(came, 0)), rcv.at[arr, arr if n > 2 else 0])
        if n > 2:
            ring_copy(blocks, arr, name, came, -came, place, 2, snd, rcv).start()

    def ring_other(blocks, arr, name, n, rcv):
        if n > 2:
            drain(blocks[arr](name(1 if arr == 0 else -1, 0)), rcv.at[arr, 1 - arr])

    def ring_last(blocks, arr, name, n, rcv):
        if n > 2:
            drain(blocks[arr](name(2, 0)), rcv.at[arr, 2])

    def ring_sent(blocks, arr, name, n, snd):
        block = blocks[arr](name(0, 0))
        for k in range(0 if n == 1 else 1 if n == 2 else 3):
            drain(block, snd.at[arr, k])

    def to_sibling(arr, x_):
        block = queries[arr](x_)
        remote(block, block, sib_s.at[arr, x_], sib_r.at[arr, x_], sibling).start()

    def wide(tile):
        return jnp.concatenate([tile, jnp.zeros((8, B - 128), F32)], axis=1) if B > 128 else tile[:, :B]

    in_piece_lanes = iota((8, 128), 1) < R

    def assemble(ref, at):
        total = jnp.zeros((8, B), F32)
        for s in range(Z):
            tile = jnp.where(in_piece_lanes, jnp.broadcast_to(ref[s, at:at + 1, :], (8, 128)), 0.0)
            total = total + (pltpu.roll(wide(tile), s * R, 1) if s else wide(tile))
        return total

    row_at = iota((8, 128), 0)
    drain(qst_in, p1_r.at[4])
    totals = jnp.zeros((8, 128), F32)
    for s in range(Z):
        totals = jnp.where(row_at == s, jnp.broadcast_to(qst_in[s, 0:1, 127:128], (8, 128)), totals)
    tot_all[x * CY + cy] = totals

    def spread(ref, slot, semr, sems):
        for dx, dc, dy in plane:
            to = dev((x + dx) % X, z, (c + dc) % CORES, (y + dy) % Y)
            remote(ref.at[slot], ref.at[slot], sems, semr, to).start()

    spread(tot_all, x * CY + cy, t_r.at[0], t_s.at[0])
    xc = x * CORES + c
    for at in range(2):
        qst_all[xc, at:at + 1, :] = assemble(qst_in, at)[0:1]
    q_team = [(dx, dc) for dx in range(X) for dc in range(CORES)][1:]
    for dx, dc in q_team:
        x_, c_ = (x + dx) % X, (c + dc) % CORES
        mine = qst_all.at[xc]
        remote(mine, mine, qs_s.at[0], qs_r.at[0], dev(x_, z, c_, y)).start()

    drain(kst_in, p1_r.at[5])
    kst_all[y] = assemble(kst_in, 0)[0:1]
    for dy in range(1, Y):
        mine = kst_all.at[y]
        remote(mine, mine, ks_s.at[0], ks_r.at[0], y_dev(dy)).start()
    for arr in range(2):
        drain(queries[arr](x), p1_r.at[arr])
        ring_start(queries, arr, q_id, X, x_dev, x_s, x_r)
        to_sibling(arr, x)

    dk_acc[...] = jnp.zeros_like(dk_acc)
    dv_acc[...] = jnp.zeros_like(dv_acc)
    cs_acc[...] = jnp.zeros_like(cs_acc)
    dqt[...] = jnp.zeros_like(dqt)
    row_acc[...] = jnp.zeros_like(row_acc)
    after_own[...] = jnp.zeros((8, 128), F32)
    k_at = iota((HB, 128), 0)
    k_z = section_of(k_at, R, half)
    for slot, dy in enumerate(order):
        k_y = (y + dy) % Y
        kpos[slot * HB:(slot + 1) * HB, :] = k_z * (CY * R) + c * (Y * R) + k_y * R + (k_at - R * k_z)
    q_at = iota((8, 2 * B), 1)
    q_half = (q_at >= B).astype(jnp.int32)
    q_rest = q_at - B * q_half
    q_c = section_of(q_rest, HB, CORES)
    q_rest = q_rest - HB * q_c
    q_z = section_of(q_rest, R, half)
    qpos = (q_half * half + q_z) * (CY * R) + q_c * (Y * R) + y * R + (q_rest - R * q_z)

    few = X * CY - 1
    drain(tot_all.at[pl.ds(0, few)], t_r.at[0])
    before = jnp.zeros((8, 128), F32)
    for x_ in range(X):
        level = jnp.zeros((8, 128), F32)
        for k in range(CY):
            level = level + tot_all[x_ * CY + k]
        run = before + row_scan(level, False)
        for k in range(CY):
            p_all[x_ * CY + k] = run
            run = run + tot_all[x_ * CY + k]
        before = before + jnp.sum(level, axis=0, keepdims=True)

    piece_row, piece_lane = iota((8, B), 0), iota((8, B), 1)
    in_piece = piece_row == section_of(piece_lane, R, Z)

    def along_lanes(tile):
        return jnp.sum(jnp.where(in_piece, lanes(tile, B), 0.0), axis=0, keepdims=True)

    low = iota((8, B), 1) < HB

    def halves(first, second):
        return (
            jnp.where(low, first, pltpu.roll(second, HB, 1)),
            jnp.where(low, pltpu.roll(first, HB, 1), second),
        )

    drain(qst_all.at[pl.ds(0, len(q_team))], qs_r.at[0])
    for x_ in range(X):
        rows = []
        for c_ in range(CORES):
            bias = along_lanes(p_all[x_ * CY + c_ * Y + y])
            stat = qst_all[x_ * CORES + c_]
            rows.append(jnp.where(iota((8, B), 0) == 0, (stat[0:1] + bias) * LOG2E, jnp.broadcast_to(stat[1:2], (8, B))))
        q_row[x_] = jnp.concatenate(halves(*rows), axis=1)

    if Y > 1:
        drain(kst_all.at[pl.ds(0, Y - 1)], ks_r.at[0])
    for slot, dy in enumerate(order):
        y_ = (y + dy) % Y
        tile = jnp.where(row_at < half, p_all[x * CY + c * Y + y_], p_all[xr * CY + c * Y + y_])
        column = jnp.broadcast_to((kst_all[y_] + along_lanes(tile)) * LOG2E, (8, B)).T[:, 0:1]
        spread_column = jnp.broadcast_to(column, (B, 128))
        kcol[0, slot * HB:(slot + 1) * HB, :] = spread_column[0:HB]
        kcol[1, slot * HB:(slot + 1) * HB, :] = spread_column[HB:B]

    def pair(x_, kh, rows, turned, first_lane, masked):
        count = 2 * B - first_lane
        part = slice(first_lane, 2 * B)
        if first_lane:
            q_blk, g_blk = q_all[x_, 1], g_all[x_, 1]
        else:
            q_blk, g_blk = q_all[x_].reshape(2 * B, D), g_all[x_].reshape(2 * B, D)
        row, delta = q_row[x_, 0:1, part], q_row[x_, 1:2, part]
        k_blk, v_blk = k_all[kh, rows, :], v_all[kh, rows, :]
        s = dot(k_blk, q_blk, NT)
        prob = jnp.exp2(s * (scale * LOG2E) + row - lanes(kcol[kh, rows, :], count))
        if masked:
            at = kpos[rows, :] + kh * (half * CY * R)
            prob = jnp.where(lanes(at, count) <= qpos[0:1, part], prob, 0.0)
        grad = prob * (dot(v_blk, g_blk, NT) - delta)
        prob_half, grad_half = prob.astype(BF16), grad.astype(BF16)
        dv_acc[kh, rows, :] += dot(prob_half, g_blk, NN)
        dk_acc[kh, rows, :] += dot(grad_half, q_blk, NN)
        dqt[x_, :, part] += dot(turned[kh], grad_half, NN)
        row_acc[x_, 0:1, part] += jnp.sum(grad, axis=0, keepdims=True)
        if count >= 128:
            folded = grad[:, 0:128]
            for lane in range(128, count, 128):
                folded = folded + grad[:, lane:lane + 128]
            cs_acc[kh, rows, :] += folded
        else:
            cs_acc[kh, rows, 0:count] += grad

    def key_turn(turned, rows):
        for kh in range(2):
            turned[kh] = k_all[kh, rows, :].astype(F32).T.astype(BF16)

    kt_all = (kt_own, kt_next, kt_far) if Y > 2 else (kt_own, kt_far)

    def sib_wait(x_):
        for arr in range(2):
            drain(q_block((q_all, g_all)[arr], x_, 1 - c), sib_r.at[arr, x_])

    def piece_totals(row):
        return jnp.sum(jnp.where(in_piece, jnp.broadcast_to(row, (8, B)), 0.0), axis=1, keepdims=True)

    lane_at = iota((8, 128), 1)

    def note(kind, row):
        after_own[...] = jnp.where(lane_at == kind * Z + row_at, piece_totals(row), after_own[...])

    def curve_send(slot):
        rows, dy = pl.ds(slot * HB, HB), order[slot]
        column = jnp.concatenate([cs_acc[0, rows, :], cs_acc[1, rows, :]], axis=0)
        sums = jnp.sum(column.T, axis=0, keepdims=True)
        cs_snd[slot] = sums
        note(X * CORES + (y + dy) % Y, sums)
        send(cs_snd.at[slot], cs_rcv.at[0, y], cs_s.at[0], cs_r.at[0], y_dev(dy), dy == 0)
        send(cs_snd.at[slot], cs_rcv.at[1, y], cs_s.at[1], cs_r.at[1], dev(xr, z, c, (y + dy) % Y), False)

    key_sums = ((dk_acc, dk_snd, dk_rcv, scale), (dv_acc, dv_snd, dv_rcv, 1.0))

    def key_send(slot):
        side = order.index(-order[slot] % Y) - 1
        for arr, (acc, snd, rcv, factor) in enumerate(key_sums):
            for kh in range(2):
                snd[slot, kh] = (acc[kh, slot * HB:(slot + 1) * HB, :] * factor).astype(BF16)
            remote(
                snd.at[slot], rcv.at[side], dk_s.at[arr, slot], dk_r.at[arr, side], y_dev(order[slot])
            ).start()

    def query_steps(i):
        if i == 1:
            for arr in range(2):
                ring_onward(queries, arr, q_id, X, x_dev, x_s, x_r)
                to_sibling(arr, (x + X - 1) % X if arr == 0 else (x + 1) % X)
            if X > 2:
                for arr in range(2):
                    ring_other(queries, arr, q_id, X, x_r)
                    to_sibling(arr, (x + 1) % X if arr == 0 else (x + X - 1) % X)
        if i == 3:
            for arr in range(2):
                ring_last(queries, arr, q_id, X, x_r)
                to_sibling(arr, (x + 2) % X)
        if i == X - 1:
            for arr in range(2):
                ring_onward(keys, arr, k_id, Y, y_dev, y_s, y_r)
        if i:
            sib_wait((x + x_order[i]) % X)

    def rows_done(x_):
        dq_part = dqt[x_].T * scale
        for hf in range(2):
            lower, upper = dq_part[hf * B:hf * B + HB], dq_part[hf * B + HB:hf * B + B]
            dqt_own[x_, hf] = jnp.where(c == 0, lower, upper)
            sib_snd[x_, hf] = jnp.where(c == 0, upper, lower).astype(BF16)
        remote(sib_snd.at[x_], sib_rcv.at[x_], dsib_s.at[x_], dsib_r.at[x_], sibling).start()

    def rows_curve(x_):
        tiles = halves(row_acc[x_, :, 0:B], row_acc[x_, :, B:2 * B])
        for c_ in range(CORES):
            rs_snd[x_ * CORES + c_] = tiles[c_][0:1]
            note(x_ * CORES + c_, tiles[c_][0:1])
            src, dst = rs_snd.at[x_ * CORES + c_], rs_rcv.at[xc]
            here = jnp.logical_and(x_ == x, c_ == c)
            send(src, dst, rs_s.at[0], rs_r.at[0], dev(x_, z, c_, y), here)

    def rows_home(x_):
        drain(sib_rcv.at[x_], dsib_r.at[x_])
        dq_snd[x_] = (dqt_own[x_] + sib_rcv[x_].astype(F32)).astype(BF16)
        remote(dq_snd.at[x_], dq_rcv.at[x], dq_s.at[x_], dq_r.at[x], dev(x_, z, c, y)).start()

    x_order = [0, 1, X - 1, 2][:X] if X > 2 else [0, 1][:X]
    bands = {1: [(0, 1)], 2: [(0, 1), (1, 1)], 4: [(0, 1), (1, 2), (3, 1)]}[Y]

    def pick(values, at):
        return sum(jnp.where(at == k, v, 0) for k, v in enumerate(values))

    for arr in range(2):
        drain(keys[arr](0), p1_r.at[2 + arr])
        ring_start(keys, arr, k_id, Y, y_dev, y_s, y_r)
    sib_wait(x)

    def band(first_slot, slots, turned, last, before_step):
        rows = pl.ds(first_slot * HB, slots * HB)
        key_turn(turned, rows)

        def step(i, carry):
            for k in range(1, X):
                if before_step:
                    pl.when(i == k)(functools.partial(before_step, k))
            x_ = (x + pick(x_order, X - 1 - i if last else i)) % X

            def key_half(kh, inner):
                @pl.when(x_ > jnp.where(kh == 0, x, xr))
                def _():
                    pair(x_, kh, rows, turned, 0, False)

                return inner

            lax.fori_loop(0, 2, key_half, 0)

            @pl.when(x_ == x)
            def _():
                pair(x_, 0, rows, turned, 0, True)

            @pl.when(x_ == xr)
            def _():
                pair(x_, 1, rows, turned, B, True)

            if last:
                rows_done(x_)

                @pl.when(i > 0)
                def _():
                    rows_home((x + pick(x_order, X - i)) % X)

            return carry

        lax.fori_loop(0, X, step, 0)

    for b, (first_slot, slots) in enumerate(bands):
        if b == 1:
            for arr in range(2):
                ring_other(keys, arr, k_id, Y, y_r)
        if b == 2:
            for arr in range(2):
                ring_last(keys, arr, k_id, Y, y_r)
        band(first_slot, slots, kt_all[b], b == len(bands) - 1, None if b else query_steps)
        if b:
            for slot in range(first_slot, first_slot + slots):
                key_send(slot)

    for x_ in range(X):
        rows_curve(x_)
    for slot in range(Y):
        curve_send(slot)
    after_all[x * CY + cy] = jnp.sum(after_own[...], axis=0, keepdims=True)
    spread(after_all, x * CY + cy, t_r.at[1], t_s.at[1])

    def give_back(fin, out, idx, keyed):
        for d in z_order:
            zz = (z + d) % Z
            src = fin.at[zz // half, pl.ds(pl.multiple_of((zz % half) * R, R), R), :]
            dst = out.at[:, columns(z)]
            at_x = jnp.where(zz < half, x, xr) if keyed else x
            here = False if d else ((at_x == x) if keyed else True)
            send(src, dst, f_s.at[idx], f_r.at[idx], dev(at_x, zz, c, y), here)

    drain(sib_rcv.at[x], dsib_r.at[x])
    dq_sum = dqt_own[x] + sib_rcv[x].astype(F32)
    for dx in range(1, X):
        x_ = (x + dx) % X
        drain(dq_rcv.at[x_], dq_r.at[x_])
        dq_sum = dq_sum + dq_rcv[x_].astype(F32)
    dq_fin[...] = dq_sum.astype(BF16)
    give_back(dq_fin, dq_out, 0, False)

    for rcv, acc, fin, out, idx, factor in (
        (dk_rcv, dk_acc, dk_fin, dk_out, 1, scale), (dv_rcv, dv_acc, dv_fin, dv_out, 2, 1.0)
    ):
        sums = [acc[kh, 0:HB, :] * factor for kh in range(2)]
        for side in range(Y - 1):
            drain(rcv.at[side], dk_r.at[idx - 1, side])
            sums = [sums[kh] + rcv[side, kh].astype(F32) for kh in range(2)]
        for kh in range(2):
            fin[kh] = sums[kh].astype(BF16)
        give_back(fin, out, idx, True)

    drain(rs_rcv, rs_r.at[0])
    drain(cs_rcv.at[0], cs_r.at[0])
    drain(cs_rcv.at[1], cs_r.at[1])
    rows_sum = jnp.zeros((1, B), F32)
    for x_ in range(X):
        for c_ in range(CORES):
            rows_sum = rows_sum + rs_rcv[x_ * CORES + c_]
    columns_sum = jnp.zeros((1, B), F32)
    for y_ in range(Y):
        columns_sum = columns_sum + jnp.where(low[0:1], cs_rcv[0, y_], cs_rcv[1, y_])
    later = section_scan(jnp.broadcast_to(rows_sum - columns_sum, (8, B)), R, Z, True)
    drain(after_all.at[pl.ds(0, few)], t_r.at[1])
    kind_at = section_of(lane_at, Z, X * CORES + Y)
    piece_at = lane_at - Z * kind_at
    of_x = section_of(kind_at, CORES, X + Y)
    turn_at = (kind_at - CORES * of_x) * Y
    later_x = own_x = own_later = jnp.zeros((8, 128), F32)
    for y_ in range(Y):
        tile = sum(after_all[(x_ * CORES + c_) * Y + y_] for x_ in range(X) for c_ in range(CORES))
        tile = jnp.where(kind_at < X * CORES, tile, 0.0)
        own = jnp.where(of_x == x, tile, 0.0)
        later_x = later_x + jnp.where(of_x > x, tile, 0.0)
        own_x = own_x + own
        own_later = own_later + jnp.where(turn_at + y_ > cy, own, 0.0)
    column_at = kind_at - X * CORES
    is_column = jnp.logical_and(column_at >= 0, column_at < Y)
    for c_ in range(CORES):
        tiles = [
            jnp.where(is_column, sum(after_all[(x_ * CORES + c_) * Y + y_] for y_ in range(Y)), 0.0)
            for x_ in range(X)
        ]
        for x_ in range(X):
            tile = jnp.where(piece_at < half, tiles[x_], tiles[X - 1 - x_])
            own = jnp.where(x_ == x, tile, 0.0)
            later_x = later_x - jnp.where(x_ > x, tile, 0.0)
            own_x = own_x - own
            own_later = own_later - jnp.where(column_at + c_ * Y > cy, own, 0.0)
    terms = later_x + jnp.where(piece_at > row_at, own_x, 0.0) + jnp.where(piece_at == row_at, own_later, 0.0)
    after = jnp.broadcast_to(jnp.sum(terms, axis=1, keepdims=True), (8, 128))
    gate_sum = later + along_lanes(after)
    for s in range(Z):
        moved = pltpu.roll(gate_sum, (B - s * R) % B, 1) if s else gate_sum
        gs_snd[s] = (moved[:, 0:128] if B >= 128 else jnp.concatenate([moved, jnp.zeros((8, 128 - B), F32)], axis=1))[0:1]
    for d in z_order:
        zz = (z + d) % Z
        send(gs_snd.at[zz], gs_rcv.at[z], f_s.at[3], f_r.at[3], dev(x, zz, c, y), d == 0)
    drain(gs_rcv, f_r.at[3])
    by_head = jnp.zeros((8, 128), F32)
    for h in range(H):
        by_head = by_head + jnp.where(row_at == h, jnp.broadcast_to(gs_rcv[h], (8, 128)), 0.0)
    dgate_out[...] = (by_head[0:H, 0:R] * jax.nn.sigmoid(-gate_float)).astype(BF16)

    for arr in range(2):
        ring_sent(queries, arr, q_id, X, x_s)
        ring_sent(keys, arr, k_id, Y, y_s)
        for x_ in range(X):
            drain(queries[arr](x_), sib_s.at[arr, x_])
        for slot in range(1, Y):
            drain(dk_snd.at[slot], dk_s.at[arr, slot])
    drain(qst_all.at[pl.ds(0, len(q_team))], qs_s.at[0])
    drain(rs_snd.at[pl.ds(0, len(q_team))], rs_s.at[0])
    if Y > 1:
        drain(kst_all.at[pl.ds(0, Y - 1)], ks_s.at[0])
        drain(cs_snd.at[pl.ds(0, Y - 1)], cs_s.at[0])
    drain(cs_snd, cs_s.at[1])
    drain(tot_all.at[pl.ds(0, few)], t_s.at[0])
    drain(after_all.at[pl.ds(0, few)], t_s.at[1])
    for dx in range(X):
        x_ = (x + dx) % X
        drain(sib_snd.at[x_], dsib_s.at[x_])
        if dx:
            drain(dq_snd.at[x_], dq_s.at[x_])

    for idx in range(4):
        less, more = q_in.at[:, pl.ds(0, (Z - 1) * D)], q_in
        if idx < 2:
            drain(less, p1_s.at[idx])
        else:
            @pl.when(xk == x)
            def _(idx=idx, less=less):
                drain(less, p1_s.at[idx])

            @pl.when(xk != x)
            def _(idx=idx, more=more):
                drain(more, p1_s.at[idx])
    drain(qst_in.at[pl.ds(0, Z - 1)], p1_s.at[4])
    drain(gs_snd.at[pl.ds(0, Z - 1)], f_s.at[3])

    @pl.when(xk == x)
    def _():
        drain(kst_in.at[pl.ds(0, Z - 1)], p1_s.at[5])
        drain(q_in.at[:, pl.ds(0, (Z - 1) * D)], f_s.at[1])
        drain(q_in.at[:, pl.ds(0, (Z - 1) * D)], f_s.at[2])

    @pl.when(xk != x)
    def _():
        drain(kst_in, p1_s.at[5])
        drain(q_in, f_s.at[1])
        drain(q_in, f_s.at[2])

    drain(q_in.at[:, pl.ds(0, (Z - 1) * D)], f_s.at[0])
    drain(dq_out, f_r.at[0])
    drain(dk_out, f_r.at[1])
    drain(dv_out, f_r.at[2])


def per_device(X, Y, *args):
    R, columns = args[0].shape
    D, Z, C = WIDTH, columns // WIDTH, CORES
    HB, B, H = Z // 2 * R, Z * R, Z
    vm = pltpu.VMEM
    dma = pltpu.SemaphoreType.DMA
    any_spec = pl.BlockSpec(memory_space=pl.ANY)
    vm_spec = pl.BlockSpec(memory_space=pltpu.VMEM)
    queries, keys = (X, 2, C * HB, D), (2, Y * HB, D)
    block, tile = (2, HB, D), (8, 128)
    scratch = [
        vm((R, columns), BF16), vm((R, columns), BF16), vm((H, R), BF16), vm((H, R), F32), vm(tile, F32),
        vm((H, 2, 128), F32), vm((H, 1, 128), F32), vm((Z, 2, 128), F32), vm((Z, 1, 128), F32),
        vm(queries, BF16), vm(queries, BF16), vm((X * C, 2, B), F32),
        vm(keys, BF16), vm(keys, BF16), vm((Y, 1, B), F32),
        vm((2, Y * HB, 128), F32), vm((Y * HB, 128), jnp.int32),
        vm((X * C * Y,) + tile, F32), vm((X * C * Y,) + tile, F32),
        vm((2, D, HB), BF16), vm((2, D, 2 * HB), BF16), vm((2, D, HB), BF16), vm((X, 8, 2 * B), F32),
        vm((X, D, 2 * B), F32), vm((X,) + block, F32), vm((X, 8, 2 * B), F32),
        vm(keys, F32), vm(keys, F32), vm((2, Y * HB, 128), F32),
        vm((X,) + block, BF16), vm((X,) + block, BF16), vm((X,) + block, BF16), vm((X,) + block, BF16),
        vm((X * C, 1, B), F32), vm((X * C, 1, B), F32),
        vm((Y,) + block, BF16), vm((Y,) + block, BF16), vm((Y,) + block, BF16), vm((Y,) + block, BF16),
        vm((Y, 1, B), F32), vm((2, Y, 1, B), F32),
        vm(tile, F32), vm((X * C * Y, 1, 128), F32), vm(block, BF16), vm(block, BF16), vm(block, BF16),
        vm((Z, 1, 128), F32), vm((H, 1, 128), F32),
        dma((4,)), dma((6,)), dma((6,)), dma((2, 3)), dma((2, 3)), dma((2, 3)), dma((2, 3)),
        dma((2, X)), dma((2, X)), dma((1,)), dma((1,)), dma((1,)), dma((1,)),
        dma((2,)), dma((2,)), dma((X,)), dma((X,)), dma((X,)), dma((X,)), dma((1,)), dma((1,)),
        dma((2, Y)), dma((2, Y)), dma((2,)), dma((2,)), dma((4,)), dma((4,)),
    ]
    grads, dgate = pl.pallas_call(
        functools.partial(body, X, Z, Y, R),
        out_shape=(jax.ShapeDtypeStruct((3, R, columns), BF16), jax.ShapeDtypeStruct((H, R), BF16)),
        in_specs=[any_spec] * 7,
        out_specs=(any_spec, vm_spec),
        scratch_shapes=scratch,
        compiler_params=pltpu.CompilerParams(
            collective_id=0, has_side_effects=True, vmem_limit_bytes=48 * 1024 * 1024
        ),
    )(*(pltpu.with_memory_space_constraint(value, pltpu.HBM) for value in (*args[:5], args[5].T, args[6].T)))
    return grads[0], grads[1], grads[2], dgate.T


def solution(mesh):
    rows = P(("ctx", "head"), None)

    def whole(*args):
        X = mesh.shape["ctx"] // (CORES * (args[0].shape[1] // WIDTH))
        return jax.shard_map(
            functools.partial(per_device, X, mesh.shape["head"]),
            mesh=mesh,
            in_specs=(rows,) * 7,
            out_specs=(rows,) * 4,
            check_vma=False,
        )(*args)

    return whole
```

```python
import functools
import math

import jax
import jax.numpy as jnp
from jax import lax
from jax.experimental import pallas as pl
from jax.experimental.pallas import tpu as pltpu
from jax.sharding import PartitionSpec as P

CORES = 2
WIDTH = 128
LOG2E = math.log2(math.e)
F32 = jnp.float32
BF16 = jnp.bfloat16
NT = (((1,), (1,)), ((), ()))
NN = (((1,), (0,)), ((), ()))


def dot(a, b, dims):
    return lax.dot_general(a, b, dims, preferred_element_type=F32)


def iota(shape, axis):
    return lax.broadcasted_iota(jnp.int32, shape, axis)


def section_of(index, size, count):
    return sum(((index >= k * size).astype(jnp.int32) for k in range(1, count)), jnp.zeros_like(index))


def section_scan(value, size, count, reverse):
    lane = iota(value.shape, 1)
    inner = lane - size * section_of(lane, size, count)
    width, shift = value.shape[1], 1
    while shift < size:
        if reverse:
            value = value + jnp.where(inner < size - shift, pltpu.roll(value, width - shift, 1), 0.0)
        else:
            value = value + jnp.where(inner >= shift, pltpu.roll(value, shift, 1), 0.0)
        shift *= 2
    return value


def row_scan(value, reverse):
    row, rows = iota(value.shape, 0), value.shape[0]

    def moved(arr, shift):
        if reverse:
            return jnp.where(row < rows - shift, pltpu.roll(arr, rows - shift, 0), 0.0)
        return jnp.where(row >= shift, pltpu.roll(arr, shift, 0), 0.0)

    value, shift = moved(value, 1), 1
    while shift < rows:
        value = value + moved(value, shift)
        shift *= 2
    return value


def lanes(value, width):
    return value[:, :width] if width <= 128 else jnp.concatenate([value] * (width // 128), axis=1)


def body(
    X, Z, Y, R,
    q_in, k_in, v_in, g_in, o_in, gate_in, lse_in,
    grads_out, dgate_out,
    g_loc, o_loc, gate_loc, lse_loc, gate_pad, st_q, st_k, qst_in, kst_in,
    q_all, g_all, qst_all, k_all, v_all, kst_all, kcol, kpos, tot_all, p_all,
    kt_own, kt_next, kt_far, q_row, dqt, dqt_own, row_acc, dk_acc, dv_acc, cs_acc,
    sib_snd, sib_rcv, dq_snd, dq_rcv, rs_snd, rs_rcv, dk_snd, dv_snd, dk_rcv, dv_rcv, cs_snd, cs_rcv,
    after_own, after_all, dq_fin, dk_fin, dv_fin, gs_snd, gs_rcv,
    loc_sem, p1_r, p1_s, x_r, x_s, y_r, y_s, sib_r, sib_s, qs_r, qs_s, ks_r, ks_s,
    t_r, t_s, dsib_r, dsib_s, dq_r, dq_s, rs_r, rs_s, dk_r, dk_s, cs_r, cs_s, f_r, f_s,
):
    dq_out, dk_out, dv_out = (grads_out.at[k] for k in range(3))
    D, H = WIDTH, Z
    half, CY = Z // 2, CORES * Y
    HB, B = half * R, Z * R
    scale = D ** -0.5
    ctx = lax.axis_index("ctx")
    y = lax.axis_index("head")
    c = ctx % CORES
    z = (ctx // CORES) % Z
    x = ctx // (CORES * Z)
    xr = X - 1 - x
    xk = jnp.where(z < half, x, xr)
    cy = c * Y + y
    mesh_id = pl.DeviceIdType.MESH

    def dev(x_, z_, c_, y_):
        return ((x_ * Z + z_) * CORES + c_, y_)

    def remote(src, dst, ssem, rsem, to):
        return pltpu.make_async_remote_copy(
            src_ref=src, dst_ref=dst, send_sem=ssem, recv_sem=rsem, device_id=to, device_id_type=mesh_id
        )

    def drain(ref, sem):
        pltpu.make_async_copy(ref, ref, sem).wait()

    def send(src, dst, ssem, rsem, to, here):
        if here is False:
            remote(src, dst, ssem, rsem, to).start()
        elif here is True:
            pltpu.make_async_copy(src, dst, rsem).start()
        else:
            @pl.when(here)
            def _():
                pltpu.make_async_copy(src, dst, rsem).start()

            @pl.when(jnp.logical_not(here))
            def _():
                remote(src, dst, ssem, rsem, to).start()

    loc = [
        pltpu.make_async_copy(g_in, g_loc, loc_sem.at[0]),
        pltpu.make_async_copy(o_in, o_loc, loc_sem.at[1]),
        pltpu.make_async_copy(gate_in, gate_loc, loc_sem.at[2]),
        pltpu.make_async_copy(lse_in, lse_loc, loc_sem.at[3]),
    ]
    for copy in loc:
        copy.start()

    barrier = pltpu.get_barrier_semaphore()
    plane = [(dx, dc, dy) for dx in range(X) for dc in range(CORES) for dy in range(Y)][1:]

    def greet(to):
        pl.semaphore_signal(barrier, inc=1, device_id=to, device_id_type=mesh_id)

    for d in range(1, Z):
        zz = (z + d) % Z
        greet(dev(x, zz, c, y))
        greet(dev(xr, zz, c, y))
    for dx, dc, dy in plane:
        greet(dev((x + dx) % X, z, (c + dc) % CORES, (y + dy) % Y))
    for copy in loc:
        copy.wait()
    st_q[...] = jnp.zeros_like(st_q)
    st_k[...] = jnp.zeros_like(st_k)
    gate_pad[...] = jnp.zeros_like(gate_pad)
    gate_float = gate_loc[...].astype(F32)
    gate_pad[0:H, 0:R] = jax.nn.log_sigmoid(gate_float)
    curve = section_scan(gate_pad[...], R, 1, False)
    lse_rows = lse_loc[...]
    for h in range(H):
        cut = slice(h * D, (h + 1) * D)
        product = g_loc[:, cut].astype(F32) * o_loc[:, cut].astype(F32)
        st_q[h, 0:1, 0:R] = curve[h:h + 1, 0:R] - lse_rows[h:h + 1, :]
        st_q[h, 0:1, 127:128] = curve[h:h + 1, R - 1:R]
        st_q[h, 1:2, 0:R] = jnp.sum(product.T, axis=0, keepdims=True)
        st_k[h, 0:1, 0:R] = curve[h:h + 1, 0:R]
    pl.semaphore_wait(barrier, 2 * (Z - 1) + len(plane))

    z_order = sorted(range(Z), key=lambda d: -min(d, Z - d))

    def columns(h_):
        return pl.ds(pl.multiple_of(h_ * D, D), D)

    z_half = z // half

    def z_rows(block):
        return pl.ds(pl.multiple_of(block * HB + (z % half) * R, R), R)

    def block_rows(block):
        return pl.ds(pl.multiple_of(block * HB, HB), HB)

    for d in z_order:
        zz = (z + d) % Z
        send(st_q.at[zz], qst_in.at[z], p1_s.at[4], p1_r.at[4], dev(x, zz, c, y), d == 0)
        send(
            st_k.at[zz], kst_in.at[z], p1_s.at[5], p1_r.at[5], dev(xk, zz, c, y),
            (xk == x) if d == 0 else False,
        )

    for idx, src, dst in ((0, q_in, q_all), (1, g_in, g_all), (2, k_in, k_all), (3, v_in, v_all)):
        for d in z_order:
            zz = (z + d) % Z
            if idx < 2:
                at, to, here = dst.at[x, z_half, z_rows(c), :], dev(x, zz, c, y), d == 0
            else:
                at, to = dst.at[z_half, z_rows(0), :], dev(xk, zz, c, y)
                here = (xk == x) if d == 0 else False
            send(src.at[:, columns(zz)], at, p1_s.at[idx], p1_r.at[idx], to, here)

    def q_block(ref, x_, c_):
        return ref.at[x_, :, block_rows(c_), :]

    def k_block(ref, slot):
        return ref.at[:, block_rows(slot), :]

    sibling = dev(x, z, 1 - c, y)
    queries = [functools.partial(q_block, ref, c_=c) for ref in (q_all, g_all)]
    keys = [functools.partial(k_block, ref) for ref in (k_all, v_all)]

    def x_dev(d):
        return dev((x + d) % X, z, c, y)

    def y_dev(d):
        return dev(x, z, c, (y + d) % Y)

    order = [0, 1, Y - 1, 2][:Y] if Y > 2 else [0, 1][:Y]

    def q_id(d, e):
        return (x + d) % X

    def k_id(d, e):
        return order.index((d - e) % Y)

    def ring_copy(blocks, arr, name, d, e, place, section, snd, rcv):
        src, dst = blocks[arr](name(d, 0)), blocks[arr](name(d, e))
        return remote(src, dst, snd.at[arr, section], rcv.at[arr, section], place(e))

    def ring_start(blocks, arr, name, n, place, snd, rcv):
        if n > 1:
            ring_copy(blocks, arr, name, 0, 1, place, 0, snd, rcv).start()
        if n > 2:
            ring_copy(blocks, arr, name, 0, -1, place, 1, snd, rcv).start()

    def ring_onward(blocks, arr, name, n, place, snd, rcv):
        came = -1 if arr == 0 else 1
        if n > 1:
            drain(blocks[arr](name(came, 0)), rcv.at[arr, arr if n > 2 else 0])
        if n > 2:
            ring_copy(blocks, arr, name, came, -came, place, 2, snd, rcv).start()

    def ring_other(blocks, arr, name, n, rcv):
        if n > 2:
            drain(blocks[arr](name(1 if arr == 0 else -1, 0)), rcv.at[arr, 1 - arr])

    def ring_last(blocks, arr, name, n, rcv):
        if n > 2:
            drain(blocks[arr](name(2, 0)), rcv.at[arr, 2])

    def ring_sent(blocks, arr, name, n, snd):
        block = blocks[arr](name(0, 0))
        for k in range(0 if n == 1 else 1 if n == 2 else 3):
            drain(block, snd.at[arr, k])

    def to_sibling(arr, x_):
        block = queries[arr](x_)
        remote(block, block, sib_s.at[arr, x_], sib_r.at[arr, x_], sibling).start()

    def wide(tile):
        return jnp.concatenate([tile, jnp.zeros((8, B - 128), F32)], axis=1) if B > 128 else tile[:, :B]

    in_piece_lanes = iota((8, 128), 1) < R

    def assemble(ref, at):
        total = jnp.zeros((8, B), F32)
        for s in range(Z):
            tile = jnp.where(in_piece_lanes, jnp.broadcast_to(ref[s, at:at + 1, :], (8, 128)), 0.0)
            total = total + (pltpu.roll(wide(tile), s * R, 1) if s else wide(tile))
        return total

    row_at = iota((8, 128), 0)
    drain(qst_in, p1_r.at[4])
    totals = jnp.zeros((8, 128), F32)
    for s in range(Z):
        totals = jnp.where(row_at == s, jnp.broadcast_to(qst_in[s, 0:1, 127:128], (8, 128)), totals)
    tot_all[x * CY + cy] = totals

    def spread(ref, slot, semr, sems):
        for dx, dc, dy in plane:
            to = dev((x + dx) % X, z, (c + dc) % CORES, (y + dy) % Y)
            remote(ref.at[slot], ref.at[slot], sems, semr, to).start()

    spread(tot_all, x * CY + cy, t_r.at[0], t_s.at[0])
    xc = x * CORES + c
    for at in range(2):
        qst_all[xc, at:at + 1, :] = assemble(qst_in, at)[0:1]
    q_team = [(dx, dc) for dx in range(X) for dc in range(CORES)][1:]
    for dx, dc in q_team:
        x_, c_ = (x + dx) % X, (c + dc) % CORES
        mine = qst_all.at[xc]
        remote(mine, mine, qs_s.at[0], qs_r.at[0], dev(x_, z, c_, y)).start()

    drain(kst_in, p1_r.at[5])
    kst_all[y] = assemble(kst_in, 0)[0:1]
    for dy in range(1, Y):
        mine = kst_all.at[y]
        remote(mine, mine, ks_s.at[0], ks_r.at[0], y_dev(dy)).start()
    for arr in range(2):
        drain(queries[arr](x), p1_r.at[arr])
        ring_start(queries, arr, q_id, X, x_dev, x_s, x_r)
        to_sibling(arr, x)

    dk_acc[...] = jnp.zeros_like(dk_acc)
    dv_acc[...] = jnp.zeros_like(dv_acc)
    cs_acc[...] = jnp.zeros_like(cs_acc)
    dqt[...] = jnp.zeros_like(dqt)
    row_acc[...] = jnp.zeros_like(row_acc)
    after_own[...] = jnp.zeros((8, 128), F32)
    k_at = iota((HB, 128), 0)
    k_z = section_of(k_at, R, half)
    for slot, dy in enumerate(order):
        k_y = (y + dy) % Y
        kpos[slot * HB:(slot + 1) * HB, :] = k_z * (CY * R) + c * (Y * R) + k_y * R + (k_at - R * k_z)
    q_at = iota((8, 2 * B), 1)
    q_half = (q_at >= B).astype(jnp.int32)
    q_rest = q_at - B * q_half
    q_c = section_of(q_rest, HB, CORES)
    q_rest = q_rest - HB * q_c
    q_z = section_of(q_rest, R, half)
    qpos = (q_half * half + q_z) * (CY * R) + q_c * (Y * R) + y * R + (q_rest - R * q_z)

    def key_start(arr):
        drain(keys[arr](0), p1_r.at[2 + arr])
        ring_start(keys, arr, k_id, Y, y_dev, y_s, y_r)

    def query_onward(arr):
        if X > 1:
            ring_onward(queries, arr, q_id, X, x_dev, x_s, x_r)
            to_sibling(arr, (x + X - 1) % X if arr == 0 else (x + 1) % X)

    key_start(0)
    query_onward(0)

    few = X * CY - 1
    drain(tot_all.at[pl.ds(0, few)], t_r.at[0])
    before = jnp.zeros((8, 128), F32)
    for x_ in range(X):
        level = jnp.zeros((8, 128), F32)
        for k in range(CY):
            level = level + tot_all[x_ * CY + k]
        run = before + row_scan(level, False)
        for k in range(CY):
            p_all[x_ * CY + k] = run
            run = run + tot_all[x_ * CY + k]
        before = before + jnp.sum(level, axis=0, keepdims=True)

    piece_row, piece_lane = iota((8, B), 0), iota((8, B), 1)
    in_piece = piece_row == section_of(piece_lane, R, Z)

    def along_lanes(tile):
        return jnp.sum(jnp.where(in_piece, lanes(tile, B), 0.0), axis=0, keepdims=True)

    low = iota((8, B), 1) < HB

    def halves(first, second):
        return (
            jnp.where(low, first, pltpu.roll(second, HB, 1)),
            jnp.where(low, pltpu.roll(first, HB, 1), second),
        )

    drain(qst_all.at[pl.ds(0, len(q_team))], qs_r.at[0])
    for x_ in range(X):
        rows = []
        for c_ in range(CORES):
            bias = along_lanes(p_all[x_ * CY + c_ * Y + y])
            stat = qst_all[x_ * CORES + c_]
            rows.append(jnp.where(iota((8, B), 0) == 0, (stat[0:1] + bias) * LOG2E, jnp.broadcast_to(stat[1:2], (8, B))))
        q_row[x_] = jnp.concatenate(halves(*rows), axis=1)

    if Y > 1:
        drain(kst_all.at[pl.ds(0, Y - 1)], ks_r.at[0])
    for slot, dy in enumerate(order):
        y_ = (y + dy) % Y
        tile = jnp.where(row_at < half, p_all[x * CY + c * Y + y_], p_all[xr * CY + c * Y + y_])
        column = jnp.broadcast_to((kst_all[y_] + along_lanes(tile)) * LOG2E, (8, B)).T[:, 0:1]
        spread_column = jnp.broadcast_to(column, (B, 128))
        kcol[0, slot * HB:(slot + 1) * HB, :] = spread_column[0:HB]
        kcol[1, slot * HB:(slot + 1) * HB, :] = spread_column[HB:B]

    def pair(x_, kh, rows, turned, first_lane, masked):
        count = 2 * B - first_lane
        part = slice(first_lane, 2 * B)
        if first_lane:
            q_blk, g_blk = q_all[x_, 1], g_all[x_, 1]
        else:
            q_blk, g_blk = q_all[x_].reshape(2 * B, D), g_all[x_].reshape(2 * B, D)
        row, delta = q_row[x_, 0:1, part], q_row[x_, 1:2, part]
        k_blk, v_blk = k_all[kh, rows, :], v_all[kh, rows, :]
        s = dot(k_blk, q_blk, NT)
        prob = jnp.exp2(s * (scale * LOG2E) + row - lanes(kcol[kh, rows, :], count))
        if masked:
            at = kpos[rows, :] + kh * (half * CY * R)
            prob = jnp.where(lanes(at, count) <= qpos[0:1, part], prob, 0.0)
        grad = prob * (dot(v_blk, g_blk, NT) - delta)
        prob_half, grad_half = prob.astype(BF16), grad.astype(BF16)
        dv_acc[kh, rows, :] += dot(prob_half, g_blk, NN)
        dk_acc[kh, rows, :] += dot(grad_half, q_blk, NN)
        dqt[x_, :, part] += dot(turned[kh], grad_half, NN)
        row_acc[x_, 0:1, part] += jnp.sum(grad, axis=0, keepdims=True)
        if count >= 128:
            folded = grad[:, 0:128]
            for lane in range(128, count, 128):
                folded = folded + grad[:, lane:lane + 128]
            cs_acc[kh, rows, :] += folded
        else:
            cs_acc[kh, rows, 0:count] += grad

    def key_turn(turned, rows):
        for kh in range(2):
            turned[kh] = k_all[kh, rows, :].astype(F32).T.astype(BF16)

    kt_all = (kt_own, kt_next, kt_far) if Y > 2 else (kt_own, kt_far)

    def sib_wait(x_):
        for arr in range(2):
            drain(q_block((q_all, g_all)[arr], x_, 1 - c), sib_r.at[arr, x_])

    def piece_totals(row):
        return jnp.sum(jnp.where(in_piece, jnp.broadcast_to(row, (8, B)), 0.0), axis=1, keepdims=True)

    lane_at = iota((8, 128), 1)

    def note(kind, row):
        after_own[...] = jnp.where(lane_at == kind * Z + row_at, piece_totals(row), after_own[...])

    def curve_send(slot):
        rows, dy = pl.ds(slot * HB, HB), order[slot]
        column = jnp.concatenate([cs_acc[0, rows, :], cs_acc[1, rows, :]], axis=0)
        sums = jnp.sum(column.T, axis=0, keepdims=True)
        cs_snd[slot] = sums
        note(X * CORES + (y + dy) % Y, sums)
        send(cs_snd.at[slot], cs_rcv.at[0, y], cs_s.at[0], cs_r.at[0], y_dev(dy), dy == 0)
        send(cs_snd.at[slot], cs_rcv.at[1, y], cs_s.at[1], cs_r.at[1], dev(xr, z, c, (y + dy) % Y), False)

    key_sums = ((dk_acc, dk_snd, dk_rcv, scale), (dv_acc, dv_snd, dv_rcv, 1.0))

    def key_send(slot):
        side = order.index(-order[slot] % Y) - 1
        for arr, (acc, snd, rcv, factor) in enumerate(key_sums):
            for kh in range(2):
                snd[slot, kh] = (acc[kh, slot * HB:(slot + 1) * HB, :] * factor).astype(BF16)
            remote(
                snd.at[slot], rcv.at[side], dk_s.at[arr, slot], dk_r.at[arr, side], y_dev(order[slot])
            ).start()

    def query_steps(i):
        if i == 1:
            if X > 2:
                for arr in range(2):
                    ring_other(queries, arr, q_id, X, x_r)
                    to_sibling(arr, (x + 1) % X if arr == 0 else (x + X - 1) % X)
        if i == 3:
            for arr in range(2):
                ring_last(queries, arr, q_id, X, x_r)
                to_sibling(arr, (x + 2) % X)
        if i == X - 1:
            for arr in range(2):
                ring_onward(keys, arr, k_id, Y, y_dev, y_s, y_r)
        if i:
            sib_wait((x + x_order[i]) % X)

    def rows_done(x_):
        dq_part = dqt[x_].T * scale
        for hf in range(2):
            lower, upper = dq_part[hf * B:hf * B + HB], dq_part[hf * B + HB:hf * B + B]
            dqt_own[x_, hf] = jnp.where(c == 0, lower, upper)
            sib_snd[x_, hf] = jnp.where(c == 0, upper, lower).astype(BF16)
        remote(sib_snd.at[x_], sib_rcv.at[x_], dsib_s.at[x_], dsib_r.at[x_], sibling).start()

    def rows_curve(x_):
        tiles = halves(row_acc[x_, :, 0:B], row_acc[x_, :, B:2 * B])
        for c_ in range(CORES):
            rs_snd[x_ * CORES + c_] = tiles[c_][0:1]
            note(x_ * CORES + c_, tiles[c_][0:1])
            src, dst = rs_snd.at[x_ * CORES + c_], rs_rcv.at[xc]
            here = jnp.logical_and(x_ == x, c_ == c)
            send(src, dst, rs_s.at[0], rs_r.at[0], dev(x_, z, c_, y), here)

    def rows_home(x_):
        drain(sib_rcv.at[x_], dsib_r.at[x_])
        dq_snd[x_] = (dqt_own[x_] + sib_rcv[x_].astype(F32)).astype(BF16)
        remote(dq_snd.at[x_], dq_rcv.at[x], dq_s.at[x_], dq_r.at[x], dev(x_, z, c, y)).start()

    x_order = [0, 1, X - 1, 2][:X] if X > 2 else [0, 1][:X]
    bands = {1: [(0, 1)], 2: [(0, 1), (1, 1)], 4: [(0, 1), (1, 2), (3, 1)]}[Y]

    def pick(values, at):
        return sum(jnp.where(at == k, v, 0) for k, v in enumerate(values))

    key_start(1)
    query_onward(1)
    sib_wait(x)

    def band(first_slot, slots, turned, last, before_step):
        rows = pl.ds(first_slot * HB, slots * HB)
        key_turn(turned, rows)

        def step(i, carry):
            for k in range(1, X):
                if before_step:
                    pl.when(i == k)(functools.partial(before_step, k))
            x_ = (x + pick(x_order, X - 1 - i if last else i)) % X

            def key_half(kh, inner):
                @pl.when(x_ > jnp.where(kh == 0, x, xr))
                def _():
                    pair(x_, kh, rows, turned, 0, False)

                return inner

            lax.fori_loop(0, 2, key_half, 0)

            @pl.when(x_ == x)
            def _():
                pair(x_, 0, rows, turned, 0, True)

            @pl.when(x_ == xr)
            def _():
                pair(x_, 1, rows, turned, B, True)

            if last:
                rows_done(x_)

                @pl.when(i > 0)
                def _():
                    rows_home((x + pick(x_order, X - i)) % X)

            return carry

        lax.fori_loop(0, X, step, 0)

    for b, (first_slot, slots) in enumerate(bands):
        if b == 1:
            for arr in range(2):
                ring_other(keys, arr, k_id, Y, y_r)
        if b == 2:
            for arr in range(2):
                ring_last(keys, arr, k_id, Y, y_r)
        band(first_slot, slots, kt_all[b], b == len(bands) - 1, None if b else query_steps)
        if b:
            for slot in range(first_slot, first_slot + slots):
                key_send(slot)

    for x_ in range(X):
        rows_curve(x_)
    for slot in range(Y):
        curve_send(slot)
    after_all[x * CY + cy] = jnp.sum(after_own[...], axis=0, keepdims=True)
    spread(after_all, x * CY + cy, t_r.at[1], t_s.at[1])

    def give_back(fin, out, idx, keyed):
        for d in z_order:
            zz = (z + d) % Z
            src = fin.at[zz // half, pl.ds(pl.multiple_of((zz % half) * R, R), R), :]
            dst = out.at[:, columns(z)]
            at_x = jnp.where(zz < half, x, xr) if keyed else x
            here = False if d else ((at_x == x) if keyed else True)
            send(src, dst, f_s.at[idx], f_r.at[idx], dev(at_x, zz, c, y), here)

    drain(sib_rcv.at[x], dsib_r.at[x])
    dq_sum = dqt_own[x] + sib_rcv[x].astype(F32)
    for dx in range(1, X):
        x_ = (x + dx) % X
        drain(dq_rcv.at[x_], dq_r.at[x_])
        dq_sum = dq_sum + dq_rcv[x_].astype(F32)
    dq_fin[...] = dq_sum.astype(BF16)
    give_back(dq_fin, dq_out, 0, False)

    for rcv, acc, fin, out, idx, factor in (
        (dk_rcv, dk_acc, dk_fin, dk_out, 1, scale), (dv_rcv, dv_acc, dv_fin, dv_out, 2, 1.0)
    ):
        sums = [acc[kh, 0:HB, :] * factor for kh in range(2)]
        for side in range(Y - 1):
            drain(rcv.at[side], dk_r.at[idx - 1, side])
            sums = [sums[kh] + rcv[side, kh].astype(F32) for kh in range(2)]
        for kh in range(2):
            fin[kh] = sums[kh].astype(BF16)
        give_back(fin, out, idx, True)

    drain(rs_rcv, rs_r.at[0])
    drain(cs_rcv.at[0], cs_r.at[0])
    drain(cs_rcv.at[1], cs_r.at[1])
    rows_sum = jnp.zeros((1, B), F32)
    for x_ in range(X):
        for c_ in range(CORES):
            rows_sum = rows_sum + rs_rcv[x_ * CORES + c_]
    columns_sum = jnp.zeros((1, B), F32)
    for y_ in range(Y):
        columns_sum = columns_sum + jnp.where(low[0:1], cs_rcv[0, y_], cs_rcv[1, y_])
    later = section_scan(jnp.broadcast_to(rows_sum - columns_sum, (8, B)), R, Z, True)
    drain(after_all.at[pl.ds(0, few)], t_r.at[1])
    kind_at = section_of(lane_at, Z, X * CORES + Y)
    piece_at = lane_at - Z * kind_at
    of_x = section_of(kind_at, CORES, X + Y)
    turn_at = (kind_at - CORES * of_x) * Y
    later_x = own_x = own_later = jnp.zeros((8, 128), F32)
    for y_ in range(Y):
        tile = sum(after_all[(x_ * CORES + c_) * Y + y_] for x_ in range(X) for c_ in range(CORES))
        tile = jnp.where(kind_at < X * CORES, tile, 0.0)
        own = jnp.where(of_x == x, tile, 0.0)
        later_x = later_x + jnp.where(of_x > x, tile, 0.0)
        own_x = own_x + own
        own_later = own_later + jnp.where(turn_at + y_ > cy, own, 0.0)
    column_at = kind_at - X * CORES
    is_column = jnp.logical_and(column_at >= 0, column_at < Y)
    for c_ in range(CORES):
        tiles = [
            jnp.where(is_column, sum(after_all[(x_ * CORES + c_) * Y + y_] for y_ in range(Y)), 0.0)
            for x_ in range(X)
        ]
        for x_ in range(X):
            tile = jnp.where(piece_at < half, tiles[x_], tiles[X - 1 - x_])
            own = jnp.where(x_ == x, tile, 0.0)
            later_x = later_x - jnp.where(x_ > x, tile, 0.0)
            own_x = own_x - own
            own_later = own_later - jnp.where(column_at + c_ * Y > cy, own, 0.0)
    terms = later_x + jnp.where(piece_at > row_at, own_x, 0.0) + jnp.where(piece_at == row_at, own_later, 0.0)
    after = jnp.broadcast_to(jnp.sum(terms, axis=1, keepdims=True), (8, 128))
    gate_sum = later + along_lanes(after)
    for s in range(Z):
        moved = pltpu.roll(gate_sum, (B - s * R) % B, 1) if s else gate_sum
        gs_snd[s] = (moved[:, 0:128] if B >= 128 else jnp.concatenate([moved, jnp.zeros((8, 128 - B), F32)], axis=1))[0:1]
    for d in z_order:
        zz = (z + d) % Z
        send(gs_snd.at[zz], gs_rcv.at[z], f_s.at[3], f_r.at[3], dev(x, zz, c, y), d == 0)
    drain(gs_rcv, f_r.at[3])
    by_head = jnp.zeros((8, 128), F32)
    for h in range(H):
        by_head = by_head + jnp.where(row_at == h, jnp.broadcast_to(gs_rcv[h], (8, 128)), 0.0)
    dgate_out[...] = (by_head[0:H, 0:R] * jax.nn.sigmoid(-gate_float)).astype(BF16)

    for arr in range(2):
        ring_sent(queries, arr, q_id, X, x_s)
        ring_sent(keys, arr, k_id, Y, y_s)
        for x_ in range(X):
            drain(queries[arr](x_), sib_s.at[arr, x_])
        for slot in range(1, Y):
            drain(dk_snd.at[slot], dk_s.at[arr, slot])
    drain(qst_all.at[pl.ds(0, len(q_team))], qs_s.at[0])
    drain(rs_snd.at[pl.ds(0, len(q_team))], rs_s.at[0])
    if Y > 1:
        drain(kst_all.at[pl.ds(0, Y - 1)], ks_s.at[0])
        drain(cs_snd.at[pl.ds(0, Y - 1)], cs_s.at[0])
    drain(cs_snd, cs_s.at[1])
    drain(tot_all.at[pl.ds(0, few)], t_s.at[0])
    drain(after_all.at[pl.ds(0, few)], t_s.at[1])
    for dx in range(X):
        x_ = (x + dx) % X
        drain(sib_snd.at[x_], dsib_s.at[x_])
        if dx:
            drain(dq_snd.at[x_], dq_s.at[x_])

    for idx in range(4):
        less, more = q_in.at[:, pl.ds(0, (Z - 1) * D)], q_in
        if idx < 2:
            drain(less, p1_s.at[idx])
        else:
            @pl.when(xk == x)
            def _(idx=idx, less=less):
                drain(less, p1_s.at[idx])

            @pl.when(xk != x)
            def _(idx=idx, more=more):
                drain(more, p1_s.at[idx])
    drain(qst_in.at[pl.ds(0, Z - 1)], p1_s.at[4])
    drain(gs_snd.at[pl.ds(0, Z - 1)], f_s.at[3])

    @pl.when(xk == x)
    def _():
        drain(kst_in.at[pl.ds(0, Z - 1)], p1_s.at[5])
        drain(q_in.at[:, pl.ds(0, (Z - 1) * D)], f_s.at[1])
        drain(q_in.at[:, pl.ds(0, (Z - 1) * D)], f_s.at[2])

    @pl.when(xk != x)
    def _():
        drain(kst_in, p1_s.at[5])
        drain(q_in, f_s.at[1])
        drain(q_in, f_s.at[2])

    drain(q_in.at[:, pl.ds(0, (Z - 1) * D)], f_s.at[0])
    drain(dq_out, f_r.at[0])
    drain(dk_out, f_r.at[1])
    drain(dv_out, f_r.at[2])


def per_device(X, Y, *args):
    R, columns = args[0].shape
    D, Z, C = WIDTH, columns // WIDTH, CORES
    HB, B, H = Z // 2 * R, Z * R, Z
    vm = pltpu.VMEM
    dma = pltpu.SemaphoreType.DMA
    any_spec = pl.BlockSpec(memory_space=pl.ANY)
    vm_spec = pl.BlockSpec(memory_space=pltpu.VMEM)
    queries, keys = (X, 2, C * HB, D), (2, Y * HB, D)
    block, tile = (2, HB, D), (8, 128)
    scratch = [
        vm((R, columns), BF16), vm((R, columns), BF16), vm((H, R), BF16), vm((H, R), F32), vm(tile, F32),
        vm((H, 2, 128), F32), vm((H, 1, 128), F32), vm((Z, 2, 128), F32), vm((Z, 1, 128), F32),
        vm(queries, BF16), vm(queries, BF16), vm((X * C, 2, B), F32),
        vm(keys, BF16), vm(keys, BF16), vm((Y, 1, B), F32),
        vm((2, Y * HB, 128), F32), vm((Y * HB, 128), jnp.int32),
        vm((X * C * Y,) + tile, F32), vm((X * C * Y,) + tile, F32),
        vm((2, D, HB), BF16), vm((2, D, 2 * HB), BF16), vm((2, D, HB), BF16), vm((X, 8, 2 * B), F32),
        vm((X, D, 2 * B), F32), vm((X,) + block, F32), vm((X, 8, 2 * B), F32),
        vm(keys, F32), vm(keys, F32), vm((2, Y * HB, 128), F32),
        vm((X,) + block, BF16), vm((X,) + block, BF16), vm((X,) + block, BF16), vm((X,) + block, BF16),
        vm((X * C, 1, B), F32), vm((X * C, 1, B), F32),
        vm((Y,) + block, BF16), vm((Y,) + block, BF16), vm((Y,) + block, BF16), vm((Y,) + block, BF16),
        vm((Y, 1, B), F32), vm((2, Y, 1, B), F32),
        vm(tile, F32), vm((X * C * Y, 1, 128), F32), vm(block, BF16), vm(block, BF16), vm(block, BF16),
        vm((Z, 1, 128), F32), vm((H, 1, 128), F32),
        dma((4,)), dma((6,)), dma((6,)), dma((2, 3)), dma((2, 3)), dma((2, 3)), dma((2, 3)),
        dma((2, X)), dma((2, X)), dma((1,)), dma((1,)), dma((1,)), dma((1,)),
        dma((2,)), dma((2,)), dma((X,)), dma((X,)), dma((X,)), dma((X,)), dma((1,)), dma((1,)),
        dma((2, Y)), dma((2, Y)), dma((2,)), dma((2,)), dma((4,)), dma((4,)),
    ]
    grads, dgate = pl.pallas_call(
        functools.partial(body, X, Z, Y, R),
        out_shape=(jax.ShapeDtypeStruct((3, R, columns), BF16), jax.ShapeDtypeStruct((H, R), BF16)),
        in_specs=[any_spec] * 7,
        out_specs=(any_spec, vm_spec),
        scratch_shapes=scratch,
        compiler_params=pltpu.CompilerParams(
            collective_id=0, has_side_effects=True, vmem_limit_bytes=48 * 1024 * 1024
        ),
    )(*(pltpu.with_memory_space_constraint(value, pltpu.HBM) for value in (*args[:5], args[5].T, args[6].T)))
    return grads[0], grads[1], grads[2], dgate.T


def solution(mesh):
    rows = P(("ctx", "head"), None)

    def whole(*args):
        X = mesh.shape["ctx"] // (CORES * (args[0].shape[1] // WIDTH))
        return jax.shard_map(
            functools.partial(per_device, X, mesh.shape["head"]),
            mesh=mesh,
            in_specs=(rows,) * 7,
            out_specs=(rows,) * 4,
            check_vma=False,
        )(*args)

    return whole
```
